128 devices in a mesh: chan: 16 (over x, y_hi, core), tm: 8 (over y_lo, z).
Axes of the slice: x: 4, y: 4 (y_hi: 2, y_lo: 2; y = y_hi * 2 + y_lo), z: 4, core: 2. Of those that a mesh axis runs over, the one named last changes fastest.
Arguments:
- record: bfloat16 [10240, 16384], P('chan', 'tm'), may hold values from -6 to 6
- channel_ok: int32 [10240], P('chan'), may hold values 0 or 1
- fan_bounds: int32 [2, 8193], replicated, may hold values from 0 to 5120, as said below
Outputs:
- slowness: float32 [10240, 16384], P('chan', 'tm')
The draws below stay inside these ranges and needn't reach their ends.
Inputs may be any that keep to these rules, and one draw needn't show every extreme that they name: fan_bounds[0, g] <= fan_bounds[1, g] for every g; fan_bounds[0, 0] is 0 and fan_bounds[1, 8192] is 5120.
All inputs are finite; a program needn't handle non-finite values. No bound on the sum of `channel_ok` on one device may be relied on, other than what follows from the above.
Results may differ from the reference program's by a relative error of at most 0.0063.
Values may be sent and summed in bfloat16 or wider, within the bound.
No kernel may reach another device: no remote copies, remote signals or barrier semaphores. Data moves between devices by JAX's collectives and lax.ppermute only.
A program may use at most 128 MiB of HBM per device.

```python
import jax
import jax.numpy as jnp
from jax import lax

NC = 10240
NT = 16384
R = 4


def draw_fan_bounds(key, part):
    streams = jax.random.split(jax.random.fold_in(key, 11), 3)
    bin_count = NT // 2 + 1
    frequency = jnp.arange(bin_count, dtype=jnp.int32)
    lower_rate = jax.random.randint(streams[0], (bin_count,), 150, 260, dtype=jnp.int32)
    upper_rate = jax.random.randint(streams[1], (bin_count,), 1000, 1500, dtype=jnp.int32)
    jitter = jax.random.randint(streams[2], (bin_count,), 0, 8, dtype=jnp.int32)
    lower_bound = frequency * lower_rate // 1000 * NC // NT
    upper_bound = jnp.minimum(frequency * upper_rate // 1000 * NC // NT + jitter, NC // 2)
    return jnp.stack([lower_bound, upper_bound]).astype(jnp.int32)


def plant(entries, rng, low, high):
    longest = entries.shape.index(max(entries.shape))
    spots = []
    for shift in (0, 1):
        where = [jax.random.randint(jax.random.fold_in(rng, axis), (), 0, length) for axis, length in enumerate(entries.shape)]
        where[longest] = (where[longest] + shift) % entries.shape[longest]
        spots.append(tuple(where))
    return entries.at[spots[0]].set(low).at[spots[1]].set(high)


def level_of(key, shape, pieces, least, high):
    def one(dim, parts):
        draws = jax.random.uniform(jax.random.fold_in(jax.random.fold_in(key, 6), dim), (parts,), jnp.float32, least / len(pieces), high / len(pieces))
        return jnp.repeat(jnp.exp(draws), shape[dim] // parts).reshape((-1,) + (1,) * (len(shape) - dim - 1))

    level = one(*pieces[0])
    for cut in pieces[1:]:
        level = level * one(*cut)
    return level


def bell_draw(rng, dims, deviation, limit, pieces=(), kind=jnp.bfloat16):
    entries = jax.random.normal(rng, dims, jnp.float32) * deviation
    if len(pieces) > 0:
        entries = level_of(rng, dims, pieces, -0.22, 0.18) * entries
    return jnp.clip(entries, min=-limit, max=limit).astype(kind)


def setup_inputs(seed: int = 0) -> dict:
    streams_of = jax.random.split(jax.random.key(seed), 4)
    return {
        "record": bell_draw(streams_of[0], (NC, NT), 1.0, 6.0, ((0, 16), (1, 8))),
        "channel_ok": plant((jax.random.randint(streams_of[1], (NC,), 0, 16) < 15).astype(jnp.int32), jax.random.fold_in(streams_of[1], 1), 0, 1),
        "fan_bounds": draw_fan_bounds(jax.random.fold_in(streams_of[3], 71), 0),
    }


def rounded_parts(spectrum):
    return jnp.real(spectrum).astype(jnp.bfloat16), jnp.imag(spectrum).astype(jnp.bfloat16)


def box_sum(values, dim_index, radius):
    length = values.shape[dim_index] - 2 * radius
    running = lax.slice_in_dim(values, 0, length, axis=dim_index)
    for offset in range(1, 2 * radius + 1):
        running = running + lax.slice_in_dim(values, offset, offset + length, axis=dim_index)
    return running


def reference(record, channel_ok, fan_bounds):
    block_rows = 128
    block_cols = 128
    radius = R
    row_blocks = NC // block_rows
    cleaned = record * channel_ok.astype(jnp.bfloat16)[:, None]

    def time_part(rows_in):
        return rounded_parts(jnp.fft.fft(rows_in.astype(jnp.float32), axis=1))

    spec_re, spec_im = lax.map(time_part, cleaned.reshape(row_blocks, block_rows, NT))
    spec_re = spec_re.reshape(NC, NT)
    spec_im = spec_im.reshape(NC, NT)
    folded_table = jnp.concatenate([fan_bounds, fan_bounds[:, 1:NT // 2][:, ::-1]], axis=1)
    wave_index = jnp.arange(NC, dtype=jnp.int32)
    folded = jnp.minimum(wave_index, NC - wave_index)

    def fk_part(start_at):
        part_re = lax.dynamic_slice_in_dim(spec_re, start_at, block_cols, 1).astype(jnp.float32)
        part_im = lax.dynamic_slice_in_dim(spec_im, start_at, block_cols, 1).astype(jnp.float32)
        spectrum = jnp.fft.fft(lax.complex(part_re, part_im), axis=0)
        lower_bound = lax.dynamic_slice_in_dim(folded_table[0], start_at, block_cols, 0)
        upper_bound = lax.dynamic_slice_in_dim(folded_table[1], start_at, block_cols, 0)
        passing = (folded[:, None] >= lower_bound[None, :]) & (folded[:, None] <= upper_bound[None, :])
        kept_bins = jnp.where(passing, spectrum, jnp.zeros_like(spectrum))
        return rounded_parts(jnp.fft.ifft(kept_bins, axis=0))

    starts = jnp.arange(NT // block_cols, dtype=jnp.int32) * block_cols
    pass_re, pass_im = lax.map(fk_part, starts)
    pass_re = pass_re.transpose(1, 0, 2).reshape(row_blocks, block_rows, NT)
    pass_im = pass_im.transpose(1, 0, 2).reshape(row_blocks, block_rows, NT)

    def back_part(halves):
        signal = lax.complex(halves[0].astype(jnp.float32), halves[1].astype(jnp.float32))
        return jnp.real(jnp.fft.ifft(signal, axis=1)).astype(jnp.bfloat16)

    filtered = lax.map(back_part, (pass_re, pass_im)).reshape(NC, NT)
    rim_width = radius + 1
    padded = jnp.pad(filtered, rim_width)
    time_pos = jnp.arange(NT + 2 * radius, dtype=jnp.int32) - radius
    time_in = (time_pos >= 0) & (time_pos < NT)
    window_area = (2 * radius + 1) * (2 * radius + 1)

    def tensor_part(start_at):
        window = lax.dynamic_slice_in_dim(padded, start_at, block_rows + 2 * rim_width, 0).astype(jnp.float32)
        grad_chan = (window[2:, 1:-1] - window[:-2, 1:-1]) * 0.5
        grad_time = (window[1:-1, 2:] - window[1:-1, :-2]) * 0.5
        chan_pos = start_at - radius + jnp.arange(block_rows + 2 * radius, dtype=jnp.int32)
        chan_in = (chan_pos >= 0) & (chan_pos < NC)
        weight = (chan_in[:, None] & time_in[None, :]).astype(jnp.float32)
        products = jnp.stack([grad_chan * grad_time * weight, grad_time * grad_time * weight])
        summed = box_sum(box_sum(products, 1, radius), 2, radius)
        cross_mean = summed[0] / window_area
        along_mean = summed[1] / window_area
        return -cross_mean / (along_mean + 1e-5)

    row_starts = jnp.arange(row_blocks, dtype=jnp.int32) * block_rows
    return lax.map(tensor_part, row_starts).reshape(NC, NT)
```

```python
import functools
import math

import jax
import jax.numpy as jnp
import ml_dtypes
import numpy as np
from jax import lax
from jax.experimental import pallas as pl
from jax.experimental.pallas import tpu as pltpu
from jax.sharding import PartitionSpec as P

NC = 10240
NT = 16384
TF = 128
R = 4
ROWS = 80
HALF = 64
WIDE = 2176
BF = jnp.bfloat16
F32 = jnp.float32
VMEM = pl.BlockSpec(memory_space=pltpu.VMEM)
SMEM = pl.BlockSpec(memory_space=pltpu.SMEM)

WAVES = [0] + [8 * n for n in range(1, 8)] + [4 + 8 * n for n in range(8)]
WAVES += [q + 8 * n for q in (1, 2, 3) for n in range(16)]


def two_parts(matrix):
    high = matrix.astype(ml_dtypes.bfloat16)
    low = (matrix - high.astype(np.float64)).astype(ml_dtypes.bfloat16)
    return high, low


def turn(numbers, length):
    angle = (numbers % length) * (2.0 * np.pi / length)
    return np.cos(angle), np.sin(angle)


def time_tables():
    n = np.arange(128)[:, None]
    j = np.concatenate([np.arange(64), 127 - np.arange(64)])[None, :]
    cos, sin = turn(n * j, 128)

    def halves(re, im):
        return np.concatenate([re[:, :64], im[:, :64], re[:, 64:], im[:, 64:]], axis=1)

    forward = np.concatenate([halves(cos, -sin), halves(sin, cos)], axis=0)
    backward = np.concatenate(
        [halves(cos, -sin).T, halves(sin, cos).T], axis=1
    ) / NT
    jj = np.arange(64)[None, :]
    c0, s0 = turn(n * 128 * jj, NT)
    c1, s1 = turn(n * (64 + 128 * jj), NT)
    zero = np.zeros((128, 128))
    even = np.concatenate([c0, -s0], axis=1)
    even[:, 64] = 1.0 - 2.0 * (np.arange(128) % 2)
    odd = np.concatenate([c1, -s1], axis=1)
    first = np.concatenate(
        [np.concatenate([even, zero], axis=1), np.concatenate([zero, odd], axis=1)], axis=0
    )
    weight = np.full(256, 2.0)
    weight[0] = 1.0
    weight[64] = 1.0
    last = (first * weight[None, :]).T / NT
    k = np.array(WAVES)[:, None]
    tw_cos, tw_sin = turn(k * np.arange(128)[None, :], NT)
    return forward, backward, first, last, tw_cos, tw_sin


def chan_tables():
    cos, sin = turn(np.arange(128)[:, None] * np.arange(128)[None, :], 128)
    forward = np.block([[cos, -sin], [sin, cos]])
    backward = np.block([[cos, sin], [-sin, cos]])
    tw_cos, tw_sin = turn(np.arange(ROWS)[:, None] * np.arange(128)[None, :], NC)
    return forward, backward, tw_cos, tw_sin


def plus(a, b):
    if a is None:
        return b
    if b is None:
        return a
    return a + b


def minus(a, b):
    if b is None:
        return a
    if a is None:
        return -b
    return a - b


def times(value, number):
    if value is None or number == 0.0:
        return None
    if number == 1.0:
        return value
    if number == -1.0:
        return -value
    return value * number


def cadd(x, y):
    return plus(x[0], y[0]), plus(x[1], y[1])


def csub(x, y):
    return minus(x[0], y[0]), minus(x[1], y[1])


def spun(x, step, length, sign):
    step = step % length
    if 4 * step % length == 0:
        quarter = 4 * step // length
        c = (1.0, 0.0, -1.0, 0.0)[quarter]
        s = (0.0, 1.0, 0.0, -1.0)[quarter]
    else:
        c = math.cos(2.0 * math.pi * step / length)
        s = math.sin(2.0 * math.pi * step / length)
    s = sign * s
    re, im = x
    if 8 * step % length == 0 and 4 * step % length != 0 and re is not None and im is not None:
        a = abs(c)
        u = re if c > 0 else -re
        v = im if c > 0 else -im
        if c * s > 0:
            return (u - v) * a, (v + u) * a
        return (u + v) * a, (v - u) * a
    return minus(times(re, c), times(im, s)), plus(times(im, c), times(re, s))


def fft_list(xs, sign):
    count = len(xs)
    if count == 1:
        return xs
    even = fft_list(xs[0::2], sign)
    odd = fft_list(xs[1::2], sign)
    head, tail = [], []
    for k in range(count // 2):
        t = spun(odd[k], k, count, sign)
        head.append(cadd(even[k], t))
        tail.append(csub(even[k], t))
    return head + tail


def rfft_list(xs):
    count = len(xs)
    if count == 2:
        return [(xs[0] + xs[1], None), (xs[0] - xs[1], None)]
    even = rfft_list(xs[0::2])
    odd = rfft_list(xs[1::2])
    out = [None] * (count // 2 + 1)
    for k in range(count // 4 + 1):
        t = spun(odd[k], k, count, -1.0)
        out[k] = cadd(even[k], t)
        if k < count // 4:
            re, im = csub(even[k], t)
            out[count // 2 - k] = (re, minus(None, im) if im is not None else None)
    return out


def irfft_list(ys):
    half = len(ys) - 1
    count = 2 * half
    if count == 2:
        return [ys[0][0] + ys[1][0], ys[0][0] - ys[1][0]]
    evens, odds = [], []
    for k in range(count // 4 + 1):
        mirror = (ys[half - k][0], minus(None, ys[half - k][1]) if ys[half - k][1] is not None else None)
        if 2 * k == half:
            evens.append((ys[k][0] * 2.0, None))
            re, _ = spun(ys[k], k, count, 1.0)
            odds.append((re * 2.0, None))
        else:
            both = cadd(ys[k], mirror)
            gap = spun(csub(ys[k], mirror), k, count, 1.0)
            if k == 0:
                both = (both[0], None)
                gap = (gap[0], None)
            evens.append(both)
            odds.append(gap)
    even = irfft_list(evens)
    odd = irfft_list(odds)
    out = []
    for e, o in zip(even, odd):
        out += [e, o]
    return out


def fft5(xs, sign):
    c1, c2 = math.cos(2 * math.pi / 5), math.cos(4 * math.pi / 5)
    s1, s2 = math.sin(2 * math.pi / 5), math.sin(4 * math.pi / 5)
    out = [[None, None] for _ in range(5)]
    pairs = []
    for part in range(2):
        x = [v[part] for v in xs]
        t1, t2, t3, t4 = x[1] + x[4], x[2] + x[3], x[1] - x[4], x[2] - x[3]
        out[0][part] = x[0] + t1 + t2
        pairs.append(
            (
                x[0] + c1 * t1 + c2 * t2,
                x[0] + c2 * t1 + c1 * t2,
                s1 * t3 + s2 * t4,
                s2 * t3 - s1 * t4,
            )
        )
    (ra, rb, rc, rd), (ia, ib, ic, idd) = pairs
    if sign > 0:
        out[1] = [ra - ic, ia + rc]
        out[4] = [ra + ic, ia - rc]
        out[2] = [rb - idd, ib + rd]
        out[3] = [rb + idd, ib - rd]
    else:
        out[1] = [ra + ic, ia - rc]
        out[4] = [ra - ic, ia + rc]
        out[2] = [rb + idd, ib - rd]
        out[3] = [rb - idd, ib + rd]
    return [tuple(v) for v in out]


def dot(a, b):
    return lax.dot_general(a, b, (((1,), (0,)), ((), ())), preferred_element_type=F32)


def parted(value):
    high = value.astype(BF)
    low = (value - high.astype(F32)).astype(BF)
    return high, low


def forward_kernel(x_ref, ok_ref, tc_ref, ts_ref, w_ref, w0_ref, out_ref, stage, hi_ref, lo_ref):
    def tile_body(tile, carry):
        rows = pl.ds(pl.multiple_of(tile * 16, 16), 16)
        good = ok_ref[rows, :]
        for a in range(16):
            xs = [x_ref[s, rows, a * 128 : (a + 1) * 128].astype(F32) * good for s in range(8)]
            ys = rfft_list(xs)
            stage[a, 0] = ys[0][0]
            for q in (1, 2, 3):
                re, im = spun(ys[q], a * q, 128, -1.0)
                stage[a, 2 * q] = re
                stage[a, 2 * q + 1] = im
            stage[a, 1] = ys[4][0]

        def put(slot, re, im):
            base = pl.ds(pl.multiple_of(slot * ROWS + tile * 16, 16), 16)
            for part, value in enumerate((re, im)):
                high, low = parted(value)
                hi_ref[base, part * 128 : (part + 1) * 128] = high
                lo_ref[base, part * 128 : (part + 1) * 128] = low

        def twist(slot, value):
            re, im = value
            c = tc_ref[slot : slot + 1, :]
            s = ts_ref[slot : slot + 1, :]
            put(slot, re * c + im * s, im * c - re * s)

        ys = rfft_list([stage[a, 0] for a in range(16)])
        put(0, ys[0][0], ys[8][0])
        for n in range(1, 8):
            twist(n, ys[n])
        ys = fft_list([spun((stage[a, 1], None), a, 32, -1.0) for a in range(16)], -1.0)
        for n in range(8):
            twist(8 + n, ys[n])
        for q in (1, 2, 3):
            ys = fft_list([(stage[a, 2 * q], stage[a, 2 * q + 1]) for a in range(16)], -1.0)
            for n in range(16):
                twist(16 * q + n, ys[n])
        return carry

    lax.fori_loop(0, 5, tile_body, 0)

    def mixed(rows, w):
        high, low = hi_ref[rows, :], lo_ref[rows, :]
        return dot(high, w[0]) + dot(low, w[0]) + dot(high, w[1])

    first = mixed(pl.ds(0, ROWS), w0_ref).astype(BF)
    out_ref[0] = first[:, :128]
    out_ref[1] = first[:, 128:]

    def wave_body(step, carry):
        res = mixed(pl.ds(pl.multiple_of(ROWS + step * 7 * ROWS, 16), 7 * ROWS), w_ref).astype(BF)
        for n in range(7):
            out_ref[2 + 14 * step + 2 * n] = res[n * ROWS : (n + 1) * ROWS, :128]
            out_ref[3 + 14 * step + 2 * n] = res[n * ROWS : (n + 1) * ROWS, 128:]
        return carry

    lax.fori_loop(0, 9, wave_body, 0)


def backward_kernel(in_ref, tc_ref, ts_ref, w_ref, w0_ref, out_ref, stage, mid_ref):
    def joined(slot):
        return jnp.concatenate([in_ref[2 * slot], in_ref[2 * slot + 1]], axis=1)

    first = joined(0)
    mid_ref[pl.ds(0, ROWS), :] = dot(first, w0_ref[0]) + dot(first, w0_ref[1])

    def wave_body(step, carry):
        data = jnp.concatenate([joined(1 + step * 7 + n) for n in range(7)], axis=0)
        mid_ref[pl.ds(pl.multiple_of(ROWS + step * 7 * ROWS, 16), 7 * ROWS), :] = dot(
            data, w_ref[0]
        ) + dot(data, w_ref[1])
        return carry

    lax.fori_loop(0, 9, wave_body, 0)
    lane = lax.broadcasted_iota(jnp.int32, (16, 128), 1)

    def tile_body(tile, carry):
        def get(slot):
            base = pl.ds(pl.multiple_of(slot * ROWS + tile * 16, 16), 16)
            return mid_ref[base, :128], mid_ref[base, 128:]

        def twisted(slot):
            re, im = get(slot)
            c = tc_ref[slot : slot + 1, :]
            s = ts_ref[slot : slot + 1, :]
            return re * c - im * s, im * c + re * s

        mean, top = get(0)
        ys = irfft_list([(mean, None)] + [twisted(n) for n in range(1, 8)] + [(top, None)])
        for a in range(16):
            stage[a, 0] = ys[a]
        ys = fft_list([twisted(8 + n) for n in range(8)] + [(None, None)] * 8, 1.0)
        for a in range(16):
            stage[a, 1] = 2.0 * spun(ys[a], a, 32, 1.0)[0]
        for q in (1, 2, 3):
            ys = fft_list([twisted(16 * q + n) for n in range(16)], 1.0)
            for a in range(16):
                re, im = spun(ys[a], a * q, 128, 1.0)
                stage[a, 2 * q] = re
                stage[a, 2 * q + 1] = im
        rows = pl.ds(pl.multiple_of(tile * 16, 16), 16)

        def series(a):
            parts = [(stage[a, 0], None)]
            parts += [(stage[a, 2 * q], stage[a, 2 * q + 1]) for q in (1, 2, 3)]
            return [y.astype(BF) for y in irfft_list(parts + [(stage[a, 1], None)])]

        ends = {}
        for a in range(16):
            ys = series(a)
            for s in range(8):
                out_ref[s, rows, a * 128 : (a + 1) * 128] = ys[s]
            if a in (0, 15):
                ends[a] = ys
        blank = jnp.zeros((16, 128), BF)
        for s in range(8):
            after = ends[0][s + 1] if s < 7 else blank
            before = ends[15][s - 1] if s > 0 else blank
            out_ref[s, rows, 2048:] = jnp.where(
                lane < 64, after.astype(F32), before.astype(F32)
            ).astype(BF)
        return carry

    lax.fori_loop(0, 5, tile_body, 0)


STEP = 8


def channel_kernel(
    in_ref, low_ref, high_ref, first_ref, tc_ref, ts_ref, w_ref, v_ref, out_ref, flat, u_re, u_im, a_re, a_im
):
    def load_body(p, carry):
        flat[pl.ds(pl.multiple_of(p * ROWS, 8), ROWS), :] = in_ref[p].astype(F32)
        return carry

    lax.fori_loop(0, 128, load_body, 0, unroll=4)
    packed = first_ref[...]
    blank = jnp.zeros((8, 128), F32)

    def in_body(step, carry):
        parts = []
        for n in range(STEP):
            turned = flat[pl.ds(step * STEP + n, 128, stride=ROWS), :].T
            re, im = turned[:64], turned[64:]
            im = jnp.concatenate([im[:8] * (1.0 - packed), im[8:], im[:8] * packed], axis=0)
            re = jnp.concatenate([re, blank], axis=0)
            parts.append(jnp.concatenate([re, im], axis=1).astype(BF))
        data = jnp.concatenate(parts, axis=0)
        res = dot(data, w_ref[0]) + dot(data, w_ref[1])
        for n in range(STEP):
            r = step * STEP + n
            re = res[n * 72 : (n + 1) * 72, :128]
            im = res[n * 72 : (n + 1) * 72, 128:]
            c = tc_ref[pl.ds(r, 1), :]
            s = ts_ref[pl.ds(r, 1), :]
            u_re[r] = re * c + im * s
            u_im[r] = im * c - re * s
        return carry

    lax.fori_loop(0, ROWS // STEP, in_body, 0)
    lane = lax.broadcasted_iota(jnp.int32, (8, 128), 1)

    def fan_body(tile, carry):
        rows = pl.ds(pl.multiple_of(tile * 8, 8), 8)
        low = low_ref[rows, :]
        high = high_ref[rows, :]
        for n2 in range(5):
            spots = [(5 * n1 + 16 * n2) % ROWS for n1 in range(16)]
            ys = fft_list([(u_re[r, rows, :], u_im[r, rows, :]) for r in spots], -1.0)
            for k1 in range(16):
                a_re[n2 * 16 + k1] = ys[k1][0]
                a_im[n2 * 16 + k1] = ys[k1][1]
        for k1 in range(16):
            ys = fft5([(a_re[n2 * 16 + k1], a_im[n2 * 16 + k1]) for n2 in range(5)], -1.0)
            kept = []
            for k2 in range(5):
                outer = next(k for k in range(ROWS) if k % 16 == k1 and k % 5 == k2)
                if outer < ROWS // 2:
                    fold = lane + outer * 128
                else:
                    fold = (NC - outer * 128) - lane
                keep = (fold >= low) & (fold <= high)
                kept.append(tuple(jnp.where(keep, v, 0.0) for v in ys[k2]))
            ys = fft5(kept, 1.0)
            for n2 in range(5):
                a_re[n2 * 16 + k1] = ys[n2][0]
                a_im[n2 * 16 + k1] = ys[n2][1]
        for n2 in range(5):
            spots = [(5 * n1 + 16 * n2) % ROWS for n1 in range(16)]
            ys = fft_list([(a_re[n2 * 16 + k1], a_im[n2 * 16 + k1]) for k1 in range(16)], 1.0)
            for n1 in range(16):
                u_re[spots[n1], rows, :] = ys[n1][0]
                u_im[spots[n1], rows, :] = ys[n1][1]
        return carry

    lax.fori_loop(0, 9, fan_body, 0)

    def out_body(step, carry):
        highs, lows = [], []
        for n in range(STEP):
            r = step * STEP + n
            re, im = u_re[r], u_im[r]
            re = jnp.concatenate([re[:8] + re[64:], re[8:64]], axis=0)
            im = jnp.concatenate([im[:8] + im[64:], im[8:64]], axis=0)
            c = tc_ref[pl.ds(r, 1), :]
            s = ts_ref[pl.ds(r, 1), :]
            high, low = parted(jnp.concatenate([re * c - im * s, im * c + re * s], axis=1))
            highs.append(high)
            lows.append(low)
        high = jnp.concatenate(highs, axis=0)
        low = jnp.concatenate(lows, axis=0)
        res = (dot(high, v_ref[0]) + dot(low, v_ref[0]) + dot(high, v_ref[1])) * (1.0 / NC)
        for n in range(STEP):
            block = res[n * 64 : (n + 1) * 64]
            both = jnp.concatenate([block[:, :128], block[:, 128:]], axis=0)
            flat[pl.ds(step * STEP + n, 128, stride=ROWS), :] = both.T
        return carry

    lax.fori_loop(0, ROWS // STEP, out_body, 0)

    def store_body(p, carry):
        out_ref[p] = flat[pl.ds(pl.multiple_of(p * ROWS, 8), ROWS), :].astype(BF)
        return carry

    lax.fori_loop(0, 128, store_body, 0, unroll=4)


def tensor_kernel(place_ref, x_ref, above_ref, below_ref, out_ref, wide, prod):
    chan, part = place_ref[0], place_ref[1]
    lane = lax.broadcasted_iota(jnp.int32, (16, 128), 1)

    def spread(start, block):
        block = block.astype(F32)
        side = block[:, 2048:]
        rows = pl.ds(start, 16)
        wide[rows, 128:2176] = block[:, :2048]
        wide[rows, :128] = side
        wide[rows, 2176:] = side

    spread(0, above_ref[...])
    spread(656, below_ref[...])

    def spread_body(step, carry):
        start = pl.multiple_of(step * 16, 16)
        spread(pl.multiple_of(start + 16, 16), x_ref[pl.ds(start, 16), :])
        return carry

    lax.fori_loop(0, 40, spread_body, 0)
    time = lax.broadcasted_iota(jnp.int32, (8, 2304), 1) - 128
    time_in = ((time >= 0) | (part > 0)) & ((time < 2048) | (part < 7))
    sub = lax.broadcasted_iota(jnp.int32, (8, 2304), 0)

    def down(a, b, count):
        return jnp.where(
            sub < 8 - count, pltpu.roll(a, 8 - count, 0), pltpu.roll(b, 8 - count, 0)
        )

    def prod_body(step, carry):
        start = pl.multiple_of(step * 8 + 8, 8)
        here = wide[pl.ds(start, 8), :]
        prev = wide[pl.ds(pl.multiple_of(start - 8, 8), 8), :]
        nxt = wide[pl.ds(pl.multiple_of(start + 8, 8), 8), :]
        grad_chan = (down(here, nxt, 1) - down(prev, here, 7)) * 0.5
        grad_time = (pltpu.roll(here, 2303, 1) - pltpu.roll(here, 1, 1)) * 0.5
        row = sub + (start - 16)
        inside = time_in & ((row >= 0) | (chan > 0)) & ((row < 640) | (chan < 15))
        grad_time_in = jnp.where(inside, grad_time, 0.0)
        prod[0, pl.ds(start, 8), :] = grad_chan * grad_time_in
        prod[1, pl.ds(start, 8), :] = grad_time * grad_time_in
        return carry

    lax.fori_loop(0, 82, prod_body, 0)

    def sum_body(step, carry):
        start = pl.multiple_of(step * 8 + 8, 8)
        sums = []
        for n in range(2):
            a = prod[n, pl.ds(start, 8), :]
            b = prod[n, pl.ds(pl.multiple_of(start + 8, 8), 8), :]
            c = prod[n, pl.ds(pl.multiple_of(start + 16, 8), 8), :]
            p = down(a, b, 4)
            q = down(b, c, 4)
            acc = p + q
            for d in range(1, 8):
                acc = acc + down(p, q, d)
            s2 = acc + pltpu.roll(acc, 2303, 1)
            s4 = s2 + pltpu.roll(s2, 2302, 1)
            s8 = s4 + pltpu.roll(s4, 2300, 1)
            s9 = s8 + pltpu.roll(acc, 2296, 1)
            sums.append(pltpu.roll(s9, 4, 1)[:, 128:2176])
        cross = sums[0] * (1.0 / 81.0)
        along = sums[1] * (1.0 / 81.0)
        out_ref[pl.ds(pl.multiple_of(step * 8, 8), 8), :] = -cross / (along + 1e-05)
        return carry

    lax.fori_loop(0, 80, sum_body, 0)


def call(kernel, out, scratch, flops, *args, smem=0):
    nbytes = sum(a.size * a.dtype.itemsize for a in args) + out.size * out.dtype.itemsize
    return pl.pallas_call(
        kernel,
        out_shape=out,
        in_specs=[SMEM] * smem + [VMEM] * (len(args) - smem),
        out_specs=VMEM,
        scratch_shapes=scratch,
        compiler_params=pltpu.CompilerParams(vmem_limit_bytes=48 * 2**20),
        cost_estimate=pl.CostEstimate(flops=flops, bytes_accessed=nbytes, transcendentals=0),
    )(*args)


def pair(matrix):
    return jnp.asarray(np.stack(two_parts(matrix)))


def single(table):
    return jnp.asarray(table.astype(np.float32))


def forward(series, good):
    fwd, _, first, _, tc, ts = time_tables()
    scratch = [
        pltpu.VMEM((16, 8, 16, 128), F32),
        pltpu.VMEM((64 * ROWS, 256), BF),
        pltpu.VMEM((64 * ROWS, 256), BF),
    ]
    out = jax.ShapeDtypeStruct((128, ROWS, 128), BF)
    return call(
        forward_kernel, out, scratch, 4 * 10**9, series, good, single(tc), single(ts), pair(fwd), pair(first)
    )


def backward(spectra):
    _, bwd, _, last, tc, ts = time_tables()
    scratch = [pltpu.VMEM((16, 8, 16, 128), F32), pltpu.VMEM((64 * ROWS, 256), F32)]
    out = jax.ShapeDtypeStruct((8, ROWS, WIDE), BF)
    return call(
        backward_kernel, out, scratch, 4 * 10**9, spectra, single(tc), single(ts), pair(bwd), pair(last)
    )


def channels(pencil, low, high, packed):
    fwd, bwd, tc, ts = chan_tables()
    scratch = [
        pltpu.VMEM((128 * ROWS, 128), F32),
        pltpu.VMEM((ROWS, 72, 128), F32),
        pltpu.VMEM((ROWS, 72, 128), F32),
        pltpu.VMEM((ROWS, 8, 128), F32),
        pltpu.VMEM((ROWS, 8, 128), F32),
    ]
    out = jax.ShapeDtypeStruct((128, ROWS, 128), BF)
    return call(
        channel_kernel,
        out,
        scratch,
        8 * 10**9,
        pencil,
        low,
        high,
        packed,
        single(tc),
        single(ts),
        pair(fwd),
        pair(bwd),
    )


def tensor(place, cells, above, below):
    scratch = [pltpu.VMEM((672, 2304), F32), pltpu.VMEM((2, 672, 2304), F32)]
    out = jax.ShapeDtypeStruct((640, 2048), F32)
    return call(tensor_kernel, out, scratch, 10**9, place, cells, above, below, smem=1)


def window_bounds(fan_bounds, block):
    column = []
    for slot, k in enumerate(WAVES):
        column += [0, 64] if slot == 0 else [k, 128 - k]
    pick = jnp.asarray(np.array(column, np.int32))[block]
    table = fan_bounds[:, : NT // 2].reshape(2, 64, 128)
    mine = lax.dynamic_slice(table, (0, 0, pick), (2, 64, 1))
    top = jnp.broadcast_to(fan_bounds[:, NT // 2].reshape(2, 1, 1), (2, 8, 1))
    both = jnp.broadcast_to(jnp.concatenate([mine, top], axis=1), (2, 72, 128))
    return both[0], both[1]


def per_device(record, channel_ok, fan_bounds):
    chan, part = lax.axis_index("chan"), lax.axis_index("tm")
    block = chan * 8 + part
    series = lax.all_to_all(record.reshape(8, ROWS, 2048), "tm", 0, 0, tiled=True)
    good = lax.dynamic_slice(channel_ok, (part * ROWS,), (ROWS,)).astype(F32)
    good = jnp.broadcast_to(good[:, None], (ROWS, 128))
    spectra = forward(series, good)
    low, high = window_bounds(fan_bounds, block)
    corner = lax.broadcasted_iota(jnp.int32, (8, 128), 0) == 0
    packed = (corner & (block == 0)).astype(F32)
    pencil = lax.all_to_all(spectra, ("chan", "tm"), 0, 0, tiled=True)
    passed = channels(pencil, low, high, packed)
    back = lax.all_to_all(passed, ("chan", "tm"), 0, 0, tiled=True)
    rows = backward(back)
    cells = lax.all_to_all(rows, "tm", 0, 0, tiled=True).reshape(640, WIDE)
    above = lax.ppermute(cells[624:], "chan", [(i, i + 1) for i in range(15)])
    below = lax.ppermute(cells[:16], "chan", [(i + 1, i) for i in range(15)])
    place = jnp.stack([chan, part]).astype(jnp.int32)
    return tensor(place, cells, above, below)


def solution(mesh):
    in_specs = (P("chan", "tm"), P("chan"), P())
    out_specs = P("chan", "tm")
    return jax.shard_map(
        per_device, mesh=mesh, in_specs=in_specs, out_specs=out_specs, check_vma=False
    )
```

```python
import functools
import math

import jax
import jax.numpy as jnp
import ml_dtypes
import numpy as np
from jax import lax
from jax.experimental import pallas as pl
from jax.experimental.pallas import tpu as pltpu
from jax.sharding import PartitionSpec as P

NC = 10240
NT = 16384
TF = 128
R = 4
ROWS = 80
HALF = 64
WIDE = 2176
BF = jnp.bfloat16
F32 = jnp.float32
VMEM = pl.BlockSpec(memory_space=pltpu.VMEM)
SMEM = pl.BlockSpec(memory_space=pltpu.SMEM)

WAVES = [0] + [8 * n for n in range(1, 8)] + [4 + 8 * n for n in range(8)]
WAVES += [q + 8 * n for q in (1, 2, 3) for n in range(16)]


def two_parts(matrix):
    high = matrix.astype(ml_dtypes.bfloat16)
    low = (matrix - high.astype(np.float64)).astype(ml_dtypes.bfloat16)
    return high, low


def turn(numbers, length):
    angle = (numbers % length) * (2.0 * np.pi / length)
    return np.cos(angle), np.sin(angle)


def time_tables():
    n = np.arange(128)[:, None]
    j = np.concatenate([np.arange(64), 127 - np.arange(64)])[None, :]
    cos, sin = turn(n * j, 128)

    def halves(re, im):
        return np.concatenate([re[:, :64], im[:, :64], re[:, 64:], im[:, 64:]], axis=1)

    forward = np.concatenate([halves(cos, -sin), halves(sin, cos)], axis=0)
    backward = np.concatenate(
        [halves(cos, -sin).T, halves(sin, cos).T], axis=1
    ) / NT
    jj = np.arange(64)[None, :]
    c0, s0 = turn(n * 128 * jj, NT)
    c1, s1 = turn(n * (64 + 128 * jj), NT)
    zero = np.zeros((128, 128))
    even = np.concatenate([c0, -s0], axis=1)
    even[:, 64] = 1.0 - 2.0 * (np.arange(128) % 2)
    odd = np.concatenate([c1, -s1], axis=1)
    first = np.concatenate(
        [np.concatenate([even, zero], axis=1), np.concatenate([zero, odd], axis=1)], axis=0
    )
    weight = np.full(256, 2.0)
    weight[0] = 1.0
    weight[64] = 1.0
    last = (first * weight[None, :]).T / NT
    k = np.array(WAVES)[:, None]
    tw_cos, tw_sin = turn(k * np.arange(128)[None, :], NT)
    return forward, backward, first, last, tw_cos, tw_sin


def chan_tables():
    cos, sin = turn(np.arange(128)[:, None] * np.arange(128)[None, :], 128)
    forward = np.block([[cos, -sin], [sin, cos]])
    backward = np.block([[cos, sin], [-sin, cos]])
    tw_cos, tw_sin = turn(np.arange(ROWS)[:, None] * np.arange(128)[None, :], NC)
    return forward, backward, tw_cos, tw_sin


def plus(a, b):
    if a is None:
        return b
    if b is None:
        return a
    return a + b


def minus(a, b):
    if b is None:
        return a
    if a is None:
        return -b
    return a - b


def times(value, number):
    if value is None or number == 0.0:
        return None
    if number == 1.0:
        return value
    if number == -1.0:
        return -value
    return value * number


def cadd(x, y):
    return plus(x[0], y[0]), plus(x[1], y[1])


def csub(x, y):
    return minus(x[0], y[0]), minus(x[1], y[1])


def spun(x, step, length, sign):
    step = step % length
    if 4 * step % length == 0:
        quarter = 4 * step // length
        c = (1.0, 0.0, -1.0, 0.0)[quarter]
        s = (0.0, 1.0, 0.0, -1.0)[quarter]
    else:
        c = math.cos(2.0 * math.pi * step / length)
        s = math.sin(2.0 * math.pi * step / length)
    s = sign * s
    re, im = x
    if 8 * step % length == 0 and 4 * step % length != 0 and re is not None and im is not None:
        a = abs(c)
        u = re if c > 0 else -re
        v = im if c > 0 else -im
        if c * s > 0:
            return (u - v) * a, (v + u) * a
        return (u + v) * a, (v - u) * a
    return minus(times(re, c), times(im, s)), plus(times(im, c), times(re, s))


def fft_list(xs, sign):
    count = len(xs)
    if count == 1:
        return xs
    even = fft_list(xs[0::2], sign)
    odd = fft_list(xs[1::2], sign)
    head, tail = [], []
    for k in range(count // 2):
        t = spun(odd[k], k, count, sign)
        head.append(cadd(even[k], t))
        tail.append(csub(even[k], t))
    return head + tail


def rfft_list(xs):
    count = len(xs)
    if count == 2:
        return [(xs[0] + xs[1], None), (xs[0] - xs[1], None)]
    even = rfft_list(xs[0::2])
    odd = rfft_list(xs[1::2])
    out = [None] * (count // 2 + 1)
    for k in range(count // 4 + 1):
        t = spun(odd[k], k, count, -1.0)
        out[k] = cadd(even[k], t)
        if k < count // 4:
            re, im = csub(even[k], t)
            out[count // 2 - k] = (re, minus(None, im) if im is not None else None)
    return out


def irfft_list(ys):
    half = len(ys) - 1
    count = 2 * half
    if count == 2:
        return [ys[0][0] + ys[1][0], ys[0][0] - ys[1][0]]
    evens, odds = [], []
    for k in range(count // 4 + 1):
        mirror = (ys[half - k][0], minus(None, ys[half - k][1]) if ys[half - k][1] is not None else None)
        if 2 * k == half:
            evens.append((ys[k][0] * 2.0, None))
            re, _ = spun(ys[k], k, count, 1.0)
            odds.append((re * 2.0, None))
        else:
            both = cadd(ys[k], mirror)
            gap = spun(csub(ys[k], mirror), k, count, 1.0)
            if k == 0:
                both = (both[0], None)
                gap = (gap[0], None)
            evens.append(both)
            odds.append(gap)
    even = irfft_list(evens)
    odd = irfft_list(odds)
    out = []
    for e, o in zip(even, odd):
        out += [e, o]
    return out


def fft5(xs, sign):
    c1, c2 = math.cos(2 * math.pi / 5), math.cos(4 * math.pi / 5)
    s1, s2 = math.sin(2 * math.pi / 5), math.sin(4 * math.pi / 5)
    out = [[None, None] for _ in range(5)]
    pairs = []
    for part in range(2):
        x = [v[part] for v in xs]
        t1, t2, t3, t4 = x[1] + x[4], x[2] + x[3], x[1] - x[4], x[2] - x[3]
        out[0][part] = x[0] + t1 + t2
        pairs.append(
            (
                x[0] + c1 * t1 + c2 * t2,
                x[0] + c2 * t1 + c1 * t2,
                s1 * t3 + s2 * t4,
                s2 * t3 - s1 * t4,
            )
        )
    (ra, rb, rc, rd), (ia, ib, ic, idd) = pairs
    if sign > 0:
        out[1] = [ra - ic, ia + rc]
        out[4] = [ra + ic, ia - rc]
        out[2] = [rb - idd, ib + rd]
        out[3] = [rb + idd, ib - rd]
    else:
        out[1] = [ra + ic, ia - rc]
        out[4] = [ra - ic, ia + rc]
        out[2] = [rb + idd, ib - rd]
        out[3] = [rb - idd, ib + rd]
    return [tuple(v) for v in out]


def dot(a, b):
    return lax.dot_general(a, b, (((1,), (0,)), ((), ())), preferred_element_type=F32)


def parted(value):
    high = value.astype(BF)
    low = (value - high.astype(F32)).astype(BF)
    return high, low


def forward_kernel(spot_ref, *refs):
    blocks = refs[:8]
    ok_ref, tc_ref, ts_ref, w_ref, w0_ref, out_ref, x_ref, stage, hi_ref, lo_ref = refs[8:]
    for n in range(8):
        x_ref[spot_ref[n]] = blocks[n][...]

    def tile_body(tile, carry):
        rows = pl.ds(pl.multiple_of(tile * 16, 16), 16)
        good = ok_ref[rows, :]
        for a in range(16):
            xs = [x_ref[s, rows, a * 128 : (a + 1) * 128].astype(F32) * good for s in range(8)]
            ys = rfft_list(xs)
            stage[a, 0] = ys[0][0]
            for q in (1, 2, 3):
                re, im = spun(ys[q], a * q, 128, -1.0)
                stage[a, 2 * q] = re
                stage[a, 2 * q + 1] = im
            stage[a, 1] = ys[4][0]

        def put(slot, re, im):
            base = pl.ds(pl.multiple_of(slot * ROWS + tile * 16, 16), 16)
            for part, value in enumerate((re, im)):
                high, low = parted(value)
                hi_ref[base, part * 128 : (part + 1) * 128] = high
                lo_ref[base, part * 128 : (part + 1) * 128] = low

        def twist(slot, value):
            re, im = value
            c = tc_ref[slot : slot + 1, :]
            s = ts_ref[slot : slot + 1, :]
            put(slot, re * c + im * s, im * c - re * s)

        ys = rfft_list([stage[a, 0] for a in range(16)])
        put(0, ys[0][0], ys[8][0])
        for n in range(1, 8):
            twist(n, ys[n])
        ys = fft_list([spun((stage[a, 1], None), a, 32, -1.0) for a in range(16)], -1.0)
        for n in range(8):
            twist(8 + n, ys[n])
        for q in (1, 2, 3):
            ys = fft_list([(stage[a, 2 * q], stage[a, 2 * q + 1]) for a in range(16)], -1.0)
            for n in range(16):
                twist(16 * q + n, ys[n])
        return carry

    lax.fori_loop(0, 5, tile_body, 0)

    def mixed(rows, w):
        high, low = hi_ref[rows, :], lo_ref[rows, :]
        return dot(high, w[0]) + dot(low, w[0]) + dot(high, w[1])

    first = mixed(pl.ds(0, ROWS), w0_ref).astype(BF)
    out_ref[0] = first[:, :128]
    out_ref[1] = first[:, 128:]

    def wave_body(step, carry):
        res = mixed(pl.ds(pl.multiple_of(ROWS + step * 7 * ROWS, 16), 7 * ROWS), w_ref).astype(BF)
        for n in range(7):
            out_ref[2 + 14 * step + 2 * n] = res[n * ROWS : (n + 1) * ROWS, :128]
            out_ref[3 + 14 * step + 2 * n] = res[n * ROWS : (n + 1) * ROWS, 128:]
        return carry

    lax.fori_loop(0, 9, wave_body, 0)


def backward_kernel(spot_ref, in_ref, tc_ref, ts_ref, w_ref, w0_ref, *refs):
    outs = refs[:8]
    out_ref, stage, mid_ref = refs[8:]

    def joined(slot):
        return jnp.concatenate([in_ref[2 * slot], in_ref[2 * slot + 1]], axis=1)

    first = joined(0)
    mid_ref[pl.ds(0, ROWS), :] = dot(first, w0_ref[0]) + dot(first, w0_ref[1])

    def wave_body(step, carry):
        data = jnp.concatenate([joined(1 + step * 7 + n) for n in range(7)], axis=0)
        mid_ref[pl.ds(pl.multiple_of(ROWS + step * 7 * ROWS, 16), 7 * ROWS), :] = dot(
            data, w_ref[0]
        ) + dot(data, w_ref[1])
        return carry

    lax.fori_loop(0, 9, wave_body, 0)
    lane = lax.broadcasted_iota(jnp.int32, (16, 128), 1)

    def tile_body(tile, carry):
        def get(slot):
            base = pl.ds(pl.multiple_of(slot * ROWS + tile * 16, 16), 16)
            return mid_ref[base, :128], mid_ref[base, 128:]

        def twisted(slot):
            re, im = get(slot)
            c = tc_ref[slot : slot + 1, :]
            s = ts_ref[slot : slot + 1, :]
            return re * c - im * s, im * c + re * s

        mean, top = get(0)
        ys = irfft_list([(mean, None)] + [twisted(n) for n in range(1, 8)] + [(top, None)])
        for a in range(16):
            stage[a, 0] = ys[a]
        ys = fft_list([twisted(8 + n) for n in range(8)] + [(None, None)] * 8, 1.0)
        for a in range(16):
            stage[a, 1] = 2.0 * spun(ys[a], a, 32, 1.0)[0]
        for q in (1, 2, 3):
            ys = fft_list([twisted(16 * q + n) for n in range(16)], 1.0)
            for a in range(16):
                re, im = spun(ys[a], a * q, 128, 1.0)
                stage[a, 2 * q] = re
                stage[a, 2 * q + 1] = im
        rows = pl.ds(pl.multiple_of(tile * 16, 16), 16)

        def series(a):
            parts = [(stage[a, 0], None)]
            parts += [(stage[a, 2 * q], stage[a, 2 * q + 1]) for q in (1, 2, 3)]
            return [y.astype(BF) for y in irfft_list(parts + [(stage[a, 1], None)])]

        ends = {}
        for a in range(16):
            ys = series(a)
            for s in range(8):
                out_ref[s, rows, a * 128 : (a + 1) * 128] = ys[s]
            if a in (0, 15):
                ends[a] = ys
        blank = jnp.zeros((16, 128), BF)
        for s in range(8):
            after = ends[0][s + 1] if s < 7 else blank
            before = ends[15][s - 1] if s > 0 else blank
            out_ref[s, rows, 2048:] = jnp.where(
                lane < 64, after.astype(F32), before.astype(F32)
            ).astype(BF)
        return carry

    lax.fori_loop(0, 5, tile_body, 0)
    for n in range(8):
        outs[n][...] = out_ref[spot_ref[n]]


STEP = 8


def channel_kernel(
    in_ref, low_ref, high_ref, first_ref, tc_ref, ts_ref, w_ref, v_ref, out_ref, flat, u_re, u_im, a_re, a_im
):
    def load_body(p, carry):
        flat[pl.ds(pl.multiple_of(p * ROWS, 8), ROWS), :] = in_ref[p].astype(F32)
        return carry

    lax.fori_loop(0, 128, load_body, 0, unroll=4)
    packed = first_ref[...]
    blank = jnp.zeros((8, 128), F32)

    def in_body(step, carry):
        parts = []
        for n in range(STEP):
            turned = flat[pl.ds(step * STEP + n, 128, stride=ROWS), :].T
            re, im = turned[:64], turned[64:]
            im = jnp.concatenate([im[:8] * (1.0 - packed), im[8:], im[:8] * packed], axis=0)
            re = jnp.concatenate([re, blank], axis=0)
            parts.append(jnp.concatenate([re, im], axis=1).astype(BF))
        data = jnp.concatenate(parts, axis=0)
        res = dot(data, w_ref[0]) + dot(data, w_ref[1])
        for n in range(STEP):
            r = step * STEP + n
            re = res[n * 72 : (n + 1) * 72, :128]
            im = res[n * 72 : (n + 1) * 72, 128:]
            c = tc_ref[pl.ds(r, 1), :]
            s = ts_ref[pl.ds(r, 1), :]
            u_re[r] = re * c + im * s
            u_im[r] = im * c - re * s
        return carry

    lax.fori_loop(0, ROWS // STEP, in_body, 0)
    lane = lax.broadcasted_iota(jnp.int32, (8, 128), 1)

    def fan_body(tile, carry):
        rows = pl.ds(pl.multiple_of(tile * 8, 8), 8)
        low = low_ref[rows, :]
        high = high_ref[rows, :]
        for n2 in range(5):
            spots = [(5 * n1 + 16 * n2) % ROWS for n1 in range(16)]
            ys = fft_list([(u_re[r, rows, :], u_im[r, rows, :]) for r in spots], -1.0)
            for k1 in range(16):
                a_re[n2 * 16 + k1] = ys[k1][0]
                a_im[n2 * 16 + k1] = ys[k1][1]
        for k1 in range(16):
            ys = fft5([(a_re[n2 * 16 + k1], a_im[n2 * 16 + k1]) for n2 in range(5)], -1.0)
            kept = []
            for k2 in range(5):
                outer = next(k for k in range(ROWS) if k % 16 == k1 and k % 5 == k2)
                if outer < ROWS // 2:
                    fold = lane + outer * 128
                else:
                    fold = (NC - outer * 128) - lane
                keep = (fold >= low) & (fold <= high)
                kept.append(tuple(jnp.where(keep, v, 0.0) for v in ys[k2]))
            ys = fft5(kept, 1.0)
            for n2 in range(5):
                a_re[n2 * 16 + k1] = ys[n2][0]
                a_im[n2 * 16 + k1] = ys[n2][1]
        for n2 in range(5):
            spots = [(5 * n1 + 16 * n2) % ROWS for n1 in range(16)]
            ys = fft_list([(a_re[n2 * 16 + k1], a_im[n2 * 16 + k1]) for k1 in range(16)], 1.0)
            for n1 in range(16):
                u_re[spots[n1], rows, :] = ys[n1][0]
                u_im[spots[n1], rows, :] = ys[n1][1]
        return carry

    lax.fori_loop(0, 9, fan_body, 0)

    def out_body(step, carry):
        highs, lows = [], []
        for n in range(STEP):
            r = step * STEP + n
            re, im = u_re[r], u_im[r]
            re = jnp.concatenate([re[:8] + re[64:], re[8:64]], axis=0)
            im = jnp.concatenate([im[:8] + im[64:], im[8:64]], axis=0)
            c = tc_ref[pl.ds(r, 1), :]
            s = ts_ref[pl.ds(r, 1), :]
            high, low = parted(jnp.concatenate([re * c - im * s, im * c + re * s], axis=1))
            highs.append(high)
            lows.append(low)
        high = jnp.concatenate(highs, axis=0)
        low = jnp.concatenate(lows, axis=0)
        res = (dot(high, v_ref[0]) + dot(low, v_ref[0]) + dot(high, v_ref[1])) * (1.0 / NC)
        for n in range(STEP):
            block = res[n * 64 : (n + 1) * 64]
            both = jnp.concatenate([block[:, :128], block[:, 128:]], axis=0)
            flat[pl.ds(step * STEP + n, 128, stride=ROWS), :] = both.T
        return carry

    lax.fori_loop(0, ROWS // STEP, out_body, 0)

    def store_body(p, carry):
        out_ref[p] = flat[pl.ds(pl.multiple_of(p * ROWS, 8), ROWS), :].astype(BF)
        return carry

    lax.fori_loop(0, 128, store_body, 0, unroll=4)


TILES = 18


def spread(wide, start, block, count):
    block = block.astype(F32)
    rows = pl.ds(start, count)
    for t in range(16):
        wide[t + 1, rows, :] = block[:, t * 128 : (t + 1) * 128]
    wide[0, rows, :] = block[:, 2048:]
    wide[17, rows, :] = block[:, 2048:]


def ahead(parts, count, lane):
    turned = [pltpu.roll(v, (-count) % 128, 1) for v in parts]
    out = []
    for t in range(len(parts)):
        if count > 0:
            other = turned[t + 1] if t + 1 < len(parts) else turned[t]
            out.append(jnp.where(lane < 128 - count, turned[t], other))
        else:
            other = turned[t - 1] if t > 0 else turned[t]
            out.append(jnp.where(lane < -count, other, turned[t]))
    return out


def products(wide, start, first_keep, last_keep, row_keep, lane):
    low = [wide[t, pl.ds(start, 8), :] for t in range(TILES)]
    here = [wide[t, pl.ds(start + 1, 8), :] for t in range(TILES)]
    high = [wide[t, pl.ds(start + 2, 8), :] for t in range(TILES)]
    right = ahead(here, 1, lane)
    left = ahead(here, -1, lane)
    both = []
    for t in range(TILES):
        grad_time = right[t] - left[t]
        masked = grad_time
        if t == 0:
            masked = jnp.where(first_keep, grad_time, 0.0)
        if t == TILES - 1:
            masked = jnp.where(last_keep, grad_time, 0.0)
        if row_keep is not None:
            masked = jnp.where(row_keep, masked, 0.0)
        both.append(((high[t] - low[t]) * masked, grad_time * masked))
    return both


def quotient(cross, along, lane):
    sums = []
    for parts in (cross, along):
        near, far = ahead(parts, 1, lane), ahead(parts, -1, lane)
        three = [v + n + f for v, n, f in zip(parts, near, far)]
        near, far = ahead(three, 3, lane), ahead(three, -3, lane)
        sums.append([v + n + f for v, n, f in zip(three, near, far)][1:17])
    scale = 1.0 / 324.0
    out = []
    for c, a in zip(*sums):
        out.append((c * -scale) / (a * scale + 1e-05))
    return jnp.concatenate(out, axis=1)


def slide_tables():
    row = np.arange(256)[:, None]
    col = np.arange(128)[None, :]
    change = (row == col + 125) * 1.0 - (row == col + 123) * 1.0
    shift = (row == col + 124) * 1.0
    nine = ((row >= col) & (row <= col + 8)) * 1.0
    return np.concatenate([change, shift], axis=1), nine


SLABS = 17
BAND = 128


def tensor_kernel(spot_ref, *refs):
    blocks = refs[:8]
    lanes_ref, nine_ref, out_ref, slope, level, prod, trio, hi_ref, lo_ref = refs[8:]
    lane = lax.broadcasted_iota(jnp.int32, (8, 128), 1)
    step = pl.program_id(0)
    part = spot_ref[9]

    @pl.when(step == 0)
    def _():
        def lanes(t, cells):
            res = dot(cells, lanes_ref[...])
            for n in range(8):
                rows = pl.ds(pl.multiple_of(spot_ref[n] * ROWS + 16, 16), ROWS)
                slope[t, rows, :] = res[n * ROWS : (n + 1) * ROWS, :128]
                level[t, rows, :] = res[n * ROWS : (n + 1) * ROWS, 128:]

        def row_body(t, carry):
            cols = pl.ds(pl.multiple_of(t * 128 - 128, 128), 256)
            lanes(t, jnp.concatenate([b[:, cols] for b in blocks], axis=0))
            return carry

        lax.fori_loop(1, 16, row_body, 0)
        first = [jnp.concatenate([b[:, 2048:], b[:, :128]], axis=1) for b in blocks]
        lanes(0, jnp.concatenate(first, axis=0))
        last = [b[:, 1920:] for b in blocks]
        lanes(16, jnp.concatenate(last, axis=0))

    top = step * BAND

    def prod_body(k, carry):
        start = pl.multiple_of(k * 8, 8)
        base = pl.multiple_of(top + k * 8, 8)
        for t in range(SLABS):
            grad_time = slope[t, pl.ds(base + 12, 8), :]
            masked = grad_time
            if t == 0:
                masked = jnp.where((lane >= 4) | (part > 0), grad_time, 0.0)
            if t == SLABS - 1:
                masked = jnp.where((lane < 4) | (part < 7), grad_time, 0.0)
            grad_chan = level[t, pl.ds(base + 13, 8), :] - level[t, pl.ds(base + 11, 8), :]
            prod[0, t, pl.ds(start, 8), :] = grad_chan * masked
            prod[1, t, pl.ds(start, 8), :] = grad_time * masked
        return carry

    lax.fori_loop(0, BAND // 8 + 2, prod_body, 0)

    def trio_body(k, carry):
        start = pl.multiple_of(k * 8, 8)
        for n in range(2):
            for t in range(SLABS):
                trio[n, t, pl.ds(start, 8), :] = (
                    prod[n, t, pl.ds(start, 8), :]
                    + prod[n, t, pl.ds(start + 1, 8), :]
                    + prod[n, t, pl.ds(start + 2, 8), :]
                )
        return carry

    lax.fori_loop(0, BAND // 8 + 1, trio_body, 0)

    def split_body(k, carry):
        start = pl.multiple_of(k * 16, 16)
        for n in range(2):
            for t in range(SLABS):
                total = (
                    trio[n, t, pl.ds(start, 16), :]
                    + trio[n, t, pl.ds(start + 3, 16), :]
                    + trio[n, t, pl.ds(start + 6, 16), :]
                )
                for ref, value in zip((hi_ref, lo_ref), parted(total)):
                    if t < SLABS - 1:
                        ref[n, t, pl.ds(start, 16), :128] = value
                    if t > 0:
                        ref[n, t - 1, pl.ds(start, 16), 128:] = value
        return carry

    lax.fori_loop(0, BAND // 16, split_body, 0)
    nine = nine_ref[...]
    scale = 1.0 / 324.0

    def sum_body(g, carry):
        sums = []
        for n in range(2):
            high = hi_ref[n, pl.ds(g * 4, 4)].reshape(4 * BAND, 256)
            low = lo_ref[n, pl.ds(g * 4, 4)].reshape(4 * BAND, 256)
            sums.append(dot(high, nine) + dot(low, nine))
        res = (sums[0] * -scale) / (sums[1] * scale + 1e-05)
        for t in range(4):
            cols = pl.ds(pl.multiple_of(g * 512 + t * 128, 128), 128)
            out_ref[:, cols] = res[t * BAND : (t + 1) * BAND]
        return carry

    lax.fori_loop(0, 4, sum_body, 0)


def edge_kernel(spot_ref, old_ref, rows_ref, out_ref, wide, prod):
    lane = lax.broadcasted_iota(jnp.int32, (8, 128), 1)
    sub = lax.broadcasted_iota(jnp.int32, (8, 128), 0)
    step = pl.program_id(0)
    chan, part = spot_ref[8], spot_ref[9]
    for k in range(2):
        spread(wide, k * 16, rows_ref[0, pl.ds(k * 16, 16), :], 16)
    open_low = (step == 0) & (chan == 0)
    open_high = (step == 1) & (chan == 15)
    skip = 8 - step * 8
    for k in range(2):
        row = sub + (k * 8 + skip + 4)
        row_keep = ((row >= 16) | jnp.logical_not(open_low)) & (
            (row < 16) | jnp.logical_not(open_high)
        )
        both = products(wide, k * 8 + skip + 3, part > 0, part < 7, row_keep, lane)
        for t in range(TILES):
            prod[0, t, pl.ds(k * 8, 8), :] = both[t][0]
            prod[1, t, pl.ds(k * 8, 8), :] = both[t][1]
    sums = []
    for n in range(2):
        parts = []
        for t in range(TILES):
            total = prod[n, t, pl.ds(0, 8), :]
            for d in range(1, 9):
                total = total + prod[n, t, pl.ds(d, 8), :]
            parts.append(total)
        sums.append(parts)
    out_ref[...] = quotient(sums[0], sums[1], lane)


def call(kernel, out, scratch, flops, *args, smem=0):
    nbytes = sum(a.size * a.dtype.itemsize for a in args) + 3 * 2**20
    return pl.pallas_call(
        kernel,
        out_shape=out,
        in_specs=[SMEM] * smem + [VMEM] * (len(args) - smem),
        out_specs=[VMEM] * len(out) if isinstance(out, list) else VMEM,
        scratch_shapes=scratch,
        compiler_params=pltpu.CompilerParams(vmem_limit_bytes=48 * 2**20),
        cost_estimate=pl.CostEstimate(flops=flops, bytes_accessed=nbytes, transcendentals=0),
    )(*args)


def pair(matrix):
    return jnp.asarray(np.stack(two_parts(matrix)))


def single(table):
    return jnp.asarray(table.astype(np.float32))


def forward(spot, blocks, good):
    fwd, _, first, _, tc, ts = time_tables()
    scratch = [
        pltpu.VMEM((8, ROWS, 2048), BF),
        pltpu.VMEM((16, 8, 16, 128), F32),
        pltpu.VMEM((64 * ROWS, 256), BF),
        pltpu.VMEM((64 * ROWS, 256), BF),
    ]
    out = jax.ShapeDtypeStruct((128, ROWS, 128), BF)
    return call(
        forward_kernel,
        out,
        scratch,
        4 * 10**9,
        spot,
        *blocks,
        good,
        single(tc),
        single(ts),
        pair(fwd),
        pair(first),
        smem=1,
    )


def backward(spot, spectra):
    _, bwd, _, last, tc, ts = time_tables()
    scratch = [
        pltpu.VMEM((8, ROWS, WIDE), BF),
        pltpu.VMEM((16, 8, 16, 128), F32),
        pltpu.VMEM((64 * ROWS, 256), F32),
    ]
    out = [jax.ShapeDtypeStruct((ROWS, WIDE), BF)] * 8
    return call(
        backward_kernel,
        out,
        scratch,
        4 * 10**9,
        spot,
        spectra,
        single(tc),
        single(ts),
        pair(bwd),
        pair(last),
        smem=1,
    )


def channels(pencil, low, high, packed):
    fwd, bwd, tc, ts = chan_tables()
    scratch = [
        pltpu.VMEM((128 * ROWS, 128), F32),
        pltpu.VMEM((ROWS, 72, 128), F32),
        pltpu.VMEM((ROWS, 72, 128), F32),
        pltpu.VMEM((ROWS, 8, 128), F32),
        pltpu.VMEM((ROWS, 8, 128), F32),
    ]
    out = jax.ShapeDtypeStruct((128, ROWS, 128), BF)
    return call(
        channel_kernel,
        out,
        scratch,
        8 * 10**9,
        pencil,
        low,
        high,
        packed,
        single(tc),
        single(ts),
        pair(fwd),
        pair(bwd),
    )


def tensor(spot, blocks):
    lanes, nine = slide_tables()
    scratch = [
        pltpu.VMEM((SLABS, 672, 128), F32),
        pltpu.VMEM((SLABS, 672, 128), F32),
        pltpu.VMEM((2, SLABS, BAND + 16, 128), F32),
        pltpu.VMEM((2, SLABS, BAND + 16, 128), F32),
        pltpu.VMEM((2, 16, BAND, 256), BF),
        pltpu.VMEM((2, 16, BAND, 256), BF),
    ]
    return pl.pallas_call(
        tensor_kernel,
        grid=(640 // BAND,),
        out_shape=jax.ShapeDtypeStruct((640, 2048), F32),
        in_specs=[SMEM] + [VMEM] * 10,
        out_specs=pl.BlockSpec((BAND, 2048), lambda g: (g, 0)),
        scratch_shapes=scratch,
        compiler_params=pltpu.CompilerParams(vmem_limit_bytes=48 * 2**20),
        cost_estimate=pl.CostEstimate(flops=10**9, bytes_accessed=9 * 2**20, transcendentals=0),
    )(spot, *blocks, jnp.asarray(lanes.astype(ml_dtypes.bfloat16)), jnp.asarray(nine.astype(ml_dtypes.bfloat16)))


def edges(spot, whole, rows):
    scratch = [pltpu.VMEM((TILES, 32, 128), F32), pltpu.VMEM((2, TILES, 16, 128), F32)]
    return pl.pallas_call(
        edge_kernel,
        grid=(2,),
        out_shape=jax.ShapeDtypeStruct((640, 2048), F32),
        in_specs=[
            SMEM,
            pl.BlockSpec(memory_space=pl.ANY),
            pl.BlockSpec((1, 32, WIDE), lambda g: (g, 0, 0)),
        ],
        out_specs=pl.BlockSpec((8, 2048), lambda g: (79 * g, 0)),
        scratch_shapes=scratch,
        input_output_aliases={1: 0},
        compiler_params=pltpu.CompilerParams(vmem_limit_bytes=16 * 2**20),
        cost_estimate=pl.CostEstimate(flops=10**7, bytes_accessed=2**19, transcendentals=0),
    )(spot, whole, rows)


def window_bounds(fan_bounds, block):
    column = []
    for slot, k in enumerate(WAVES):
        column += [0, 64] if slot == 0 else [k, 128 - k]
    pick = jnp.asarray(np.array(column, np.int32))[block]
    table = fan_bounds[:, : NT // 2].reshape(2, 64, 128)
    mine = lax.dynamic_slice(table, (0, 0, pick), (2, 64, 1))
    top = jnp.broadcast_to(fan_bounds[:, NT // 2].reshape(2, 1, 1), (2, 8, 1))
    both = jnp.broadcast_to(jnp.concatenate([mine, top], axis=1), (2, 72, 128))
    return both[0], both[1]


MOVES = [(0, 0), (1, 2), (0, 2), (1, 1), (1, 3), (0, 1), (0, 3), (1, 0)]


def moved(part, move, sign):
    return (part // 4 + move[0]) % 2 * 4 + (part % 4 + sign * move[1]) % 4


def traded(blocks):
    out = [blocks[0]]
    for move, block in list(zip(MOVES, blocks))[1:]:
        out.append(lax.ppermute(block, "tm", [(j, moved(j, move, 1)) for j in range(8)]))
    return out


def per_device(record, channel_ok, fan_bounds):
    chan, part = lax.axis_index("chan"), lax.axis_index("tm")
    block = chan * 8 + part
    targets = [moved(part, move, 1) for move in MOVES]
    sources = [moved(part, move, -1) for move in MOVES]
    to = jnp.stack(targets).astype(jnp.int32)
    came = jnp.stack(sources + [chan, part]).astype(jnp.int32)
    pieces = [lax.dynamic_slice(record, (t * ROWS, 0), (ROWS, 2048)) for t in targets]
    series = traded(pieces)
    good = lax.dynamic_slice(channel_ok, (part * ROWS,), (ROWS,)).astype(F32)
    good = jnp.broadcast_to(good[:, None], (ROWS, 128))
    spectra = forward(came, series, good)
    low, high = window_bounds(fan_bounds, block)
    corner = lax.broadcasted_iota(jnp.int32, (8, 128), 0) == 0
    packed = (corner & (block == 0)).astype(F32)
    pencil = lax.all_to_all(spectra, ("chan", "tm"), 0, 0, tiled=True)
    passed = channels(pencil, low, high, packed)
    back = lax.all_to_all(passed, ("chan", "tm"), 0, 0, tiled=True)
    cells = traded(backward(to, back))
    top, bottom = cells[0][:16], cells[0][64:]
    for source, cell in list(zip(sources, cells))[1:]:
        top = jnp.where(source == 0, cell[:16], top)
        bottom = jnp.where(source == 7, cell[64:], bottom)
    above = lax.ppermute(bottom, "chan", [(i, i + 1) for i in range(15)])
    below = lax.ppermute(top, "chan", [(i + 1, i) for i in range(15)])
    whole = tensor(came, cells)
    rows = jnp.stack(
        [jnp.concatenate([above, top], axis=0), jnp.concatenate([bottom, below], axis=0)]
    )
    return edges(came, whole, rows)


def solution(mesh):
    in_specs = (P("chan", "tm"), P("chan"), P())
    out_specs = P("chan", "tm")
    return jax.shard_map(
        per_device, mesh=mesh, in_specs=in_specs, out_specs=out_specs, check_vma=False
    )
```

```python
import functools
import math

import jax
import jax.numpy as jnp
import ml_dtypes
import numpy as np
from jax import lax
from jax.experimental import pallas as pl
from jax.experimental.pallas import tpu as pltpu
from jax.sharding import PartitionSpec as P

NC = 10240
NT = 16384
TF = 128
R = 4
ROWS = 80
HALF = 64
NEAR = 1280
FAR = 896
BF = jnp.bfloat16
F32 = jnp.float32
VMEM = pl.BlockSpec(memory_space=pltpu.VMEM)
SMEM = pl.BlockSpec(memory_space=pltpu.SMEM)
ANY = pl.BlockSpec(memory_space=pl.ANY)

WAVES = [0] + [8 * n for n in range(1, 8)] + [4 + 8 * n for n in range(8)]
WAVES += [q + 8 * n for q in (1, 2, 3) for n in range(16)]


def two_parts(matrix):
    high = matrix.astype(ml_dtypes.bfloat16)
    low = (matrix - high.astype(np.float64)).astype(ml_dtypes.bfloat16)
    return high, low


def turn(numbers, length):
    angle = (numbers % length) * (2.0 * np.pi / length)
    return np.cos(angle), np.sin(angle)


def time_tables():
    n = np.arange(128)[:, None]
    j = np.concatenate([np.arange(64), 127 - np.arange(64)])[None, :]
    cos, sin = turn(n * j, 128)

    def halves(re, im):
        return np.concatenate([re[:, :64], im[:, :64], re[:, 64:], im[:, 64:]], axis=1)

    forward = np.concatenate([halves(cos, -sin), halves(sin, cos)], axis=0)
    backward = np.concatenate(
        [halves(cos, -sin).T, halves(sin, cos).T], axis=1
    ) / NT
    jj = np.arange(64)[None, :]
    c0, s0 = turn(n * 128 * jj, NT)
    c1, s1 = turn(n * (64 + 128 * jj), NT)
    zero = np.zeros((128, 128))
    even = np.concatenate([c0, -s0], axis=1)
    even[:, 64] = 1.0 - 2.0 * (np.arange(128) % 2)
    odd = np.concatenate([c1, -s1], axis=1)
    first = np.concatenate(
        [np.concatenate([even, zero], axis=1), np.concatenate([zero, odd], axis=1)], axis=0
    )
    weight = np.full(256, 2.0)
    weight[0] = 1.0
    weight[64] = 1.0
    last = (first * weight[None, :]).T / NT
    k = np.array(WAVES)[:, None]
    tw_cos, tw_sin = turn(k * np.arange(128)[None, :], NT)
    return forward, backward, first, last, tw_cos, tw_sin


def chan_tables():
    cos, sin = turn(np.arange(128)[:, None] * np.arange(128)[None, :], 128)
    forward = np.block([[cos, -sin], [sin, cos]])
    backward = np.block([[cos, sin], [-sin, cos]])
    tw_cos, tw_sin = turn(np.arange(ROWS)[:, None] * np.arange(128)[None, :], NC)
    return forward, backward, tw_cos, tw_sin


def plus(a, b):
    if a is None:
        return b
    if b is None:
        return a
    return a + b


def minus(a, b):
    if b is None:
        return a
    if a is None:
        return -b
    return a - b


def times(value, number):
    if value is None or number == 0.0:
        return None
    if number == 1.0:
        return value
    if number == -1.0:
        return -value
    return value * number


def cadd(x, y):
    return plus(x[0], y[0]), plus(x[1], y[1])


def csub(x, y):
    return minus(x[0], y[0]), minus(x[1], y[1])


def spun(x, step, length, sign):
    step = step % length
    if 4 * step % length == 0:
        quarter = 4 * step // length
        c = (1.0, 0.0, -1.0, 0.0)[quarter]
        s = (0.0, 1.0, 0.0, -1.0)[quarter]
    else:
        c = math.cos(2.0 * math.pi * step / length)
        s = math.sin(2.0 * math.pi * step / length)
    s = sign * s
    re, im = x
    if 8 * step % length == 0 and 4 * step % length != 0 and re is not None and im is not None:
        a = abs(c)
        u = re if c > 0 else -re
        v = im if c > 0 else -im
        if c * s > 0:
            return (u - v) * a, (v + u) * a
        return (u + v) * a, (v - u) * a
    return minus(times(re, c), times(im, s)), plus(times(im, c), times(re, s))


def fft_list(xs, sign):
    count = len(xs)
    if count == 1:
        return xs
    even = fft_list(xs[0::2], sign)
    odd = fft_list(xs[1::2], sign)
    head, tail = [], []
    for k in range(count // 2):
        t = spun(odd[k], k, count, sign)
        head.append(cadd(even[k], t))
        tail.append(csub(even[k], t))
    return head + tail


def rfft_list(xs):
    count = len(xs)
    if count == 2:
        return [(xs[0] + xs[1], None), (xs[0] - xs[1], None)]
    even = rfft_list(xs[0::2])
    odd = rfft_list(xs[1::2])
    out = [None] * (count // 2 + 1)
    for k in range(count // 4 + 1):
        t = spun(odd[k], k, count, -1.0)
        out[k] = cadd(even[k], t)
        if k < count // 4:
            re, im = csub(even[k], t)
            out[count // 2 - k] = (re, minus(None, im) if im is not None else None)
    return out


def irfft_list(ys):
    half = len(ys) - 1
    count = 2 * half
    if count == 2:
        return [ys[0][0] + ys[1][0], ys[0][0] - ys[1][0]]
    evens, odds = [], []
    for k in range(count // 4 + 1):
        mirror = (ys[half - k][0], minus(None, ys[half - k][1]) if ys[half - k][1] is not None else None)
        if 2 * k == half:
            evens.append((ys[k][0] * 2.0, None))
            re, _ = spun(ys[k], k, count, 1.0)
            odds.append((re * 2.0, None))
        else:
            both = cadd(ys[k], mirror)
            gap = spun(csub(ys[k], mirror), k, count, 1.0)
            if k == 0:
                both = (both[0], None)
                gap = (gap[0], None)
            evens.append(both)
            odds.append(gap)
    even = irfft_list(evens)
    odd = irfft_list(odds)
    out = []
    for e, o in zip(even, odd):
        out += [e, o]
    return out


def fft5(xs, sign):
    c1, c2 = math.cos(2 * math.pi / 5), math.cos(4 * math.pi / 5)
    s1, s2 = math.sin(2 * math.pi / 5), math.sin(4 * math.pi / 5)
    out = [[None, None] for _ in range(5)]
    pairs = []
    for part in range(2):
        x = [v[part] for v in xs]
        t1, t2, t3, t4 = x[1] + x[4], x[2] + x[3], x[1] - x[4], x[2] - x[3]
        out[0][part] = x[0] + t1 + t2
        pairs.append(
            (
                x[0] + c1 * t1 + c2 * t2,
                x[0] + c2 * t1 + c1 * t2,
                s1 * t3 + s2 * t4,
                s2 * t3 - s1 * t4,
            )
        )
    (ra, rb, rc, rd), (ia, ib, ic, idd) = pairs
    if sign > 0:
        out[1] = [ra - ic, ia + rc]
        out[4] = [ra + ic, ia - rc]
        out[2] = [rb - idd, ib + rd]
        out[3] = [rb + idd, ib - rd]
    else:
        out[1] = [ra + ic, ia - rc]
        out[4] = [ra - ic, ia + rc]
        out[2] = [rb + idd, ib - rd]
        out[3] = [rb - idd, ib + rd]
    return [tuple(v) for v in out]


def dot(a, b):
    return lax.dot_general(a, b, (((1,), (0,)), ((), ())), preferred_element_type=F32)


def parted(value):
    high = value.astype(BF)
    low = (value - high.astype(F32)).astype(BF)
    return high, low


def forward_kernel(
    x_ref, ok_ref, low_ref, high_ref, packed_ref, tc_ref, ts_ref, w_ref, w0_ref, out_ref,
    stage, hi_ref, lo_ref
):
    def tile_body(tile, carry):
        rows = pl.ds(pl.multiple_of(tile * 16, 16), 16)
        good = ok_ref[rows, :]
        for a in range(16):
            xs = [x_ref[s, rows, a * 128 : (a + 1) * 128].astype(F32) * good for s in range(8)]
            ys = rfft_list(xs)
            stage[a, 0] = ys[0][0]
            for q in (1, 2, 3):
                re, im = spun(ys[q], a * q, 128, -1.0)
                stage[a, 2 * q] = re
                stage[a, 2 * q + 1] = im
            stage[a, 1] = ys[4][0]

        def put(slot, re, im):
            base = pl.ds(pl.multiple_of(slot * ROWS + tile * 16, 16), 16)
            for part, value in enumerate((re, im)):
                high, low = parted(value)
                hi_ref[base, part * 128 : (part + 1) * 128] = high
                lo_ref[base, part * 128 : (part + 1) * 128] = low

        def twist(slot, value):
            re, im = value
            c = tc_ref[slot : slot + 1, :]
            s = ts_ref[slot : slot + 1, :]
            put(slot, re * c + im * s, im * c - re * s)

        ys = rfft_list([stage[a, 0] for a in range(16)])
        put(0, ys[0][0], ys[8][0])
        for n in range(1, 8):
            twist(n, ys[n])
        ys = fft_list([spun((stage[a, 1], None), a, 32, -1.0) for a in range(16)], -1.0)
        for n in range(8):
            twist(8 + n, ys[n])
        for q in (1, 2, 3):
            ys = fft_list([(stage[a, 2 * q], stage[a, 2 * q + 1]) for a in range(16)], -1.0)
            for n in range(16):
                twist(16 * q + n, ys[n])
        return carry

    lax.fori_loop(0, 5, tile_body, 0)

    def mixed(rows, w):
        high, low = hi_ref[rows, :], lo_ref[rows, :]
        return dot(high, w[0]) + dot(low, w[0]) + dot(high, w[1])

    first = mixed(pl.ds(0, ROWS), w0_ref).astype(BF)
    out_ref[0] = first[:, :128]
    out_ref[1] = first[:, 128:]

    def wave_body(step, carry):
        res = mixed(pl.ds(pl.multiple_of(ROWS + step * 7 * ROWS, 16), 7 * ROWS), w_ref).astype(BF)
        for n in range(7):
            out_ref[2 + 14 * step + 2 * n] = res[n * ROWS : (n + 1) * ROWS, :128]
            out_ref[3 + 14 * step + 2 * n] = res[n * ROWS : (n + 1) * ROWS, 128:]
        return carry

    lax.fori_loop(0, 9, wave_body, 0)


def backward_kernel(in_ref, tc_ref, ts_ref, w_ref, w0_ref, near_ref, far_ref, stage, mid_ref):
    def joined(slot):
        return jnp.concatenate([in_ref[2 * slot], in_ref[2 * slot + 1]], axis=1)

    first = joined(0)
    mid_ref[pl.ds(0, ROWS), :] = dot(first, w0_ref[0]) + dot(first, w0_ref[1])

    def wave_body(step, carry):
        data = jnp.concatenate([joined(1 + step * 7 + n) for n in range(7)], axis=0)
        mid_ref[pl.ds(pl.multiple_of(ROWS + step * 7 * ROWS, 16), 7 * ROWS), :] = dot(
            data, w_ref[0]
        ) + dot(data, w_ref[1])
        return carry

    lax.fori_loop(0, 9, wave_body, 0)
    lane = lax.broadcasted_iota(jnp.int32, (16, 128), 1)

    def tile_body(tile, carry):
        def get(slot):
            base = pl.ds(pl.multiple_of(slot * ROWS + tile * 16, 16), 16)
            return mid_ref[base, :128], mid_ref[base, 128:]

        def twisted(slot):
            re, im = get(slot)
            c = tc_ref[slot : slot + 1, :]
            s = ts_ref[slot : slot + 1, :]
            return re * c - im * s, im * c + re * s

        mean, top = get(0)
        ys = irfft_list([(mean, None)] + [twisted(n) for n in range(1, 8)] + [(top, None)])
        for a in range(16):
            stage[a, 0] = ys[a]
        ys = fft_list([twisted(8 + n) for n in range(8)] + [(None, None)] * 8, 1.0)
        for a in range(16):
            stage[a, 1] = 2.0 * spun(ys[a], a, 32, 1.0)[0]
        for q in (1, 2, 3):
            ys = fft_list([twisted(16 * q + n) for n in range(16)], 1.0)
            for a in range(16):
                re, im = spun(ys[a], a * q, 128, 1.0)
                stage[a, 2 * q] = re
                stage[a, 2 * q + 1] = im
        rows = pl.ds(pl.multiple_of(tile * 16, 16), 16)

        def series(a):
            parts = [(stage[a, 0], None)]
            parts += [(stage[a, 2 * q], stage[a, 2 * q + 1]) for q in (1, 2, 3)]
            return [y.astype(BF) for y in irfft_list(parts + [(stage[a, 1], None)])]

        ends = {}
        for a in range(16):
            ys = series(a)
            for s in range(8):
                if a < 9:
                    near_ref[s, rows, a * 128 + 128 : a * 128 + 256] = ys[s]
                else:
                    far_ref[s, rows, (a - 9) * 128 : (a - 8) * 128] = ys[s]
            if a in (0, 15):
                ends[a] = ys
        blank = jnp.zeros((16, 128), BF)
        for s in range(8):
            after = ends[0][s + 1] if s < 7 else blank
            before = ends[15][s - 1] if s > 0 else blank
            near_ref[s, rows, :128] = jnp.where(
                lane < 64, after.astype(F32), before.astype(F32)
            ).astype(BF)
        return carry

    lax.fori_loop(0, 5, tile_body, 0)


STEP = 8


def channel_kernel(
    in_ref, low_ref, high_ref, first_ref, tc_ref, ts_ref, w_ref, v_ref, out_ref,
    flat, u_re, u_im, a_re, a_im
):
    def load_body(p, carry):
        flat[pl.ds(pl.multiple_of(p * ROWS, 8), ROWS), :] = in_ref[p].astype(F32)
        return carry

    lax.fori_loop(0, 128, load_body, 0, unroll=4)
    packed = first_ref[...]
    blank = jnp.zeros((8, 128), F32)

    def in_body(step, carry):
        parts = []
        for n in range(STEP):
            turned = flat[pl.ds(step * STEP + n, 128, stride=ROWS), :].T
            re, im = turned[:64], turned[64:]
            im = jnp.concatenate([im[:8] * (1.0 - packed), im[8:], im[:8] * packed], axis=0)
            re = jnp.concatenate([re, blank], axis=0)
            parts.append(jnp.concatenate([re, im], axis=1).astype(BF))
        data = jnp.concatenate(parts, axis=0)
        res = dot(data, w_ref[0]) + dot(data, w_ref[1])
        for n in range(STEP):
            r = step * STEP + n
            re = res[n * 72 : (n + 1) * 72, :128]
            im = res[n * 72 : (n + 1) * 72, 128:]
            c = tc_ref[pl.ds(r, 1), :]
            s = ts_ref[pl.ds(r, 1), :]
            u_re[r] = re * c + im * s
            u_im[r] = im * c - re * s
        return carry

    lax.fori_loop(0, ROWS // STEP, in_body, 0)
    lane = lax.broadcasted_iota(jnp.int32, (8, 128), 1)

    def fan_body(tile, carry):
        rows = pl.ds(pl.multiple_of(tile * 8, 8), 8)
        low = low_ref[rows, :]
        high = high_ref[rows, :]
        for n2 in range(5):
            spots = [(5 * n1 + 16 * n2) % ROWS for n1 in range(16)]
            ys = fft_list([(u_re[r, rows, :], u_im[r, rows, :]) for r in spots], -1.0)
            for k1 in range(16):
                a_re[n2 * 16 + k1] = ys[k1][0]
                a_im[n2 * 16 + k1] = ys[k1][1]
        for k1 in range(16):
            ys = fft5([(a_re[n2 * 16 + k1], a_im[n2 * 16 + k1]) for n2 in range(5)], -1.0)
            kept = []
            for k2 in range(5):
                outer = next(k for k in range(ROWS) if k % 16 == k1 and k % 5 == k2)
                if outer < ROWS // 2:
                    fold = lane + outer * 128
                else:
                    fold = (NC - outer * 128) - lane
                keep = (fold >= low) & (fold <= high)
                kept.append(tuple(jnp.where(keep, v, 0.0) for v in ys[k2]))
            ys = fft5(kept, 1.0)
            for n2 in range(5):
                a_re[n2 * 16 + k1] = ys[n2][0]
                a_im[n2 * 16 + k1] = ys[n2][1]
        for n2 in range(5):
            spots = [(5 * n1 + 16 * n2) % ROWS for n1 in range(16)]
            ys = fft_list([(a_re[n2 * 16 + k1], a_im[n2 * 16 + k1]) for k1 in range(16)], 1.0)
            for n1 in range(16):
                u_re[spots[n1], rows, :] = ys[n1][0]
                u_im[spots[n1], rows, :] = ys[n1][1]
        return carry

    lax.fori_loop(0, 9, fan_body, 0)

    def out_body(step, carry):
        highs, lows = [], []
        for n in range(STEP):
            r = step * STEP + n
            re, im = u_re[r], u_im[r]
            re = jnp.concatenate([re[:8] + re[64:], re[8:64]], axis=0)
            im = jnp.concatenate([im[:8] + im[64:], im[8:64]], axis=0)
            c = tc_ref[pl.ds(r, 1), :]
            s = ts_ref[pl.ds(r, 1), :]
            high, low = parted(jnp.concatenate([re * c - im * s, im * c + re * s], axis=1))
            highs.append(high)
            lows.append(low)
        high = jnp.concatenate(highs, axis=0)
        low = jnp.concatenate(lows, axis=0)
        res = (dot(high, v_ref[0]) + dot(low, v_ref[0]) + dot(high, v_ref[1])) * (1.0 / NC)
        for n in range(STEP):
            block = res[n * 64 : (n + 1) * 64]
            both = jnp.concatenate([block[:, :128], block[:, 128:]], axis=0)
            flat[pl.ds(step * STEP + n, 128, stride=ROWS), :] = both.T
        return carry

    lax.fori_loop(0, ROWS // STEP, out_body, 0)

    def store_body(p, carry):
        out_ref[p] = flat[pl.ds(pl.multiple_of(p * ROWS, 8), ROWS), :].astype(BF)
        return carry

    lax.fori_loop(0, 128, store_body, 0, unroll=4)


TILES = 18


def spread(wide, start, block, count):
    block = block.astype(F32)
    rows = pl.ds(start, count)
    for t in range(17):
        wide[t, rows, :] = block[:, t * 128 : (t + 1) * 128]
    wide[17, rows, :] = block[:, :128]


def ahead(parts, count, lane):
    turned = [pltpu.roll(v, (-count) % 128, 1) for v in parts]
    out = []
    for t in range(len(parts)):
        if count > 0:
            other = turned[t + 1] if t + 1 < len(parts) else turned[t]
            out.append(jnp.where(lane < 128 - count, turned[t], other))
        else:
            other = turned[t - 1] if t > 0 else turned[t]
            out.append(jnp.where(lane < -count, other, turned[t]))
    return out


def products(wide, start, first_keep, last_keep, row_keep, lane):
    low = [wide[t, pl.ds(start, 8), :] for t in range(TILES)]
    here = [wide[t, pl.ds(start + 1, 8), :] for t in range(TILES)]
    high = [wide[t, pl.ds(start + 2, 8), :] for t in range(TILES)]
    right = ahead(here, 1, lane)
    left = ahead(here, -1, lane)
    both = []
    for t in range(TILES):
        grad_time = right[t] - left[t]
        masked = grad_time
        if t == 0:
            masked = jnp.where(first_keep, grad_time, 0.0)
        if t == TILES - 1:
            masked = jnp.where(last_keep, grad_time, 0.0)
        if row_keep is not None:
            masked = jnp.where(row_keep, masked, 0.0)
        both.append(((high[t] - low[t]) * masked, grad_time * masked))
    return both


def quotient(cross, along, lane):
    sums = []
    for parts in (cross, along):
        near, far = ahead(parts, 1, lane), ahead(parts, -1, lane)
        three = [v + n + f for v, n, f in zip(parts, near, far)]
        near, far = ahead(three, 3, lane), ahead(three, -3, lane)
        sums.append([v + n + f for v, n, f in zip(three, near, far)][1:17])
    scale = 1.0 / 324.0
    out = []
    for c, a in zip(*sums):
        out.append((c * -scale) / (a * scale + 1e-05))
    return jnp.concatenate(out, axis=1)


def slide_tables():
    row = np.arange(256)[:, None]
    col = np.arange(128)[None, :]
    change = (row == col + 125) * 1.0 - (row == col + 123) * 1.0
    shift = (row == col + 124) * 1.0
    nine = ((row >= col) & (row <= col + 8)) * 1.0
    nine = np.concatenate([nine[:128], nine[128:]], axis=1)
    return np.concatenate([change, shift], axis=1), np.concatenate([nine, nine], axis=0)


BAND = 128
PER = 9


def tensor_kernel(half, place_ref, *refs):
    if half == 0:
        near_ref, lanes_ref, nine_ref, out_ref, slope, level, prod, trio, both_ref = refs
    else:
        near_ref, far_ref, lanes_ref, nine_ref, _, out_ref = refs[:6]
        slope, level, prod, trio, both_ref = refs[6:]
    lane = lax.broadcasted_iota(jnp.int32, (8, 128), 1)
    step = pl.program_id(0)
    part = place_ref[1]

    def lanes(t, cells):
        res = dot(cells, lanes_ref[...])
        slope[t, 16:656, :] = res[:, :128]
        level[t, 16:656, :] = res[:, 128:]

    def cut(ref, t):
        return ref[:, pl.ds(pl.multiple_of(t * 128, 128), 256)]

    @pl.when(step == 0)
    def _():
        if half == 0:

            def lanes_body(t, carry):
                lanes(t, cut(near_ref, t))
                return carry

            lax.fori_loop(0, PER, lanes_body, 0)
        else:

            def lanes_body(t, carry):
                lanes(t + 2, cut(far_ref, t))
                return carry

            lanes(0, near_ref[:, 1024:])
            lanes(1, jnp.concatenate([near_ref[:, 1152:], far_ref[:, :128]], axis=1))
            lax.fori_loop(0, PER - 3, lanes_body, 0)
            lanes(8, jnp.concatenate([far_ref[:, 768:], near_ref[:, :128]], axis=1))

    top = step * BAND

    def prod_body(k, carry):
        start = pl.multiple_of(k * 8, 8)
        base = pl.multiple_of(top + k * 8, 8)
        for t in range(PER):
            grad_time = slope[t, pl.ds(base + 12, 8), :]
            masked = grad_time
            if half == 0 and t == 0:
                masked = jnp.where((lane >= 4) | (part > 0), grad_time, 0.0)
            if half == 1 and t == PER - 1:
                masked = jnp.where((lane < 4) | (part < 7), grad_time, 0.0)
            grad_chan = level[t, pl.ds(base + 13, 8), :] - level[t, pl.ds(base + 11, 8), :]
            prod[0, t, pl.ds(start, 8), :] = grad_chan * masked
            prod[1, t, pl.ds(start, 8), :] = grad_time * masked
        return carry

    lax.fori_loop(0, BAND // 8 + 2, prod_body, 0)

    def trio_body(k, carry):
        start = pl.multiple_of(k * 8, 8)
        for n in range(2):
            for t in range(PER):
                trio[n, t, pl.ds(start, 8), :] = (
                    prod[n, t, pl.ds(start, 8), :]
                    + prod[n, t, pl.ds(start + 1, 8), :]
                    + prod[n, t, pl.ds(start + 2, 8), :]
                )
        return carry

    lax.fori_loop(0, BAND // 8 + 1, trio_body, 0)

    def split_body(k, carry):
        start = pl.multiple_of(k * 16, 16)
        for n in range(2):
            for t in range(PER):
                total = (
                    trio[n, t, pl.ds(start, 16), :]
                    + trio[n, t, pl.ds(start + 3, 16), :]
                    + trio[n, t, pl.ds(start + 6, 16), :]
                )
                high, low = parted(total)
                both_ref[n, t, pl.ds(start, 16), :128] = high
                both_ref[n, t, pl.ds(start, 16), 128:] = low
        return carry

    lax.fori_loop(0, BAND // 16, split_body, 0)
    nine = nine_ref[...]
    scale = 1.0 / 324.0

    def sum_body(g, carry):
        sums = []
        for n in range(2):
            res = dot(both_ref[n, pl.ds(g * 4, 5)].reshape(5 * BAND, 256), nine)
            sums.append(res[: 4 * BAND, :128] + res[BAND:, 128:])
        res = (sums[0] * -scale) / (sums[1] * scale + 1e-05)
        for t in range(4):
            cols = pl.ds(pl.multiple_of(g * 512 + t * 128, 128), 128)
            out_ref[:, cols] = res[t * BAND : (t + 1) * BAND]
        return carry

    lax.fori_loop(0, 2, sum_body, 0)


def edge_kernel(place_ref, old_ref, rows_ref, out_ref, wide, prod):
    lane = lax.broadcasted_iota(jnp.int32, (8, 128), 1)
    sub = lax.broadcasted_iota(jnp.int32, (8, 128), 0)
    step = pl.program_id(0)
    chan, part = place_ref[0], place_ref[1]
    for k in range(2):
        rows = pl.ds(k * 16, 16)
        spread(wide, k * 16, rows_ref[0, rows, :], 16)
    open_low = (step == 0) & (chan == 0)
    open_high = (step == 1) & (chan == 15)
    skip = 8 - step * 8
    for k in range(2):
        row = sub + (k * 8 + skip + 4)
        row_keep = ((row >= 16) | jnp.logical_not(open_low)) & (
            (row < 16) | jnp.logical_not(open_high)
        )
        both = products(wide, k * 8 + skip + 3, part > 0, part < 7, row_keep, lane)
        for t in range(TILES):
            prod[0, t, pl.ds(k * 8, 8), :] = both[t][0]
            prod[1, t, pl.ds(k * 8, 8), :] = both[t][1]
    sums = []
    for n in range(2):
        parts = []
        for t in range(TILES):
            total = prod[n, t, pl.ds(0, 8), :]
            for d in range(1, 9):
                total = total + prod[n, t, pl.ds(d, 8), :]
            parts.append(total)
        sums.append(parts)
    out_ref[...] = quotient(sums[0], sums[1], lane)


def call(kernel, out, specs, scratch, flops, *args):
    nbytes = sum(a.size * a.dtype.itemsize for a in args) + 3 * 2**20
    return pl.pallas_call(
        kernel,
        out_shape=out,
        in_specs=[VMEM] * len(args),
        out_specs=specs,
        scratch_shapes=scratch,
        compiler_params=pltpu.CompilerParams(vmem_limit_bytes=48 * 2**20),
        cost_estimate=pl.CostEstimate(flops=flops, bytes_accessed=nbytes, transcendentals=0),
    )(*args)


def pair(matrix):
    return jnp.asarray(np.stack(two_parts(matrix)))


def single(table):
    return jnp.asarray(table.astype(np.float32))


def forward(series, good, low, high, packed):
    fwd, _, first, _, tc, ts = time_tables()
    scratch = [
        pltpu.VMEM((16, 8, 16, 128), F32),
        pltpu.VMEM((64 * ROWS, 256), BF),
        pltpu.VMEM((64 * ROWS, 256), BF),
    ]
    out = jax.ShapeDtypeStruct((128, ROWS, 128), BF)
    tables = single(tc), single(ts), pair(fwd), pair(first)
    return call(forward_kernel, out, VMEM, scratch, 4 * 10**9, series, good, low, high, packed, *tables)


def backward(spectra):
    _, bwd, _, last, tc, ts = time_tables()
    scratch = [pltpu.VMEM((16, 8, 16, 128), F32), pltpu.VMEM((64 * ROWS, 256), F32)]
    out = [jax.ShapeDtypeStruct((8, ROWS, n), BF) for n in (NEAR, FAR)]
    tables = single(tc), single(ts), pair(bwd), pair(last)
    return call(backward_kernel, out, [VMEM, VMEM], scratch, 4 * 10**9, spectra, *tables)


def channels(pencil, low, high, packed):
    fwd, bwd, tc, ts = chan_tables()
    scratch = [
        pltpu.VMEM((128 * ROWS, 128), F32),
        pltpu.VMEM((ROWS, 72, 128), F32),
        pltpu.VMEM((ROWS, 72, 128), F32),
        pltpu.VMEM((ROWS, 8, 128), F32),
        pltpu.VMEM((ROWS, 8, 128), F32),
    ]
    out = jax.ShapeDtypeStruct((128, ROWS, 128), BF)
    tables = single(tc), single(ts), pair(fwd), pair(bwd)
    return call(channel_kernel, out, VMEM, scratch, 8 * 10**9, pencil, low, high, packed, *tables)


def tensor(half, place, near, far=None, whole=None):
    lanes, nine = (jnp.asarray(t.astype(ml_dtypes.bfloat16)) for t in slide_tables())
    scratch = [
        pltpu.VMEM((PER, 672, 128), F32),
        pltpu.VMEM((PER, 672, 128), F32),
        pltpu.VMEM((2, PER, BAND + 16, 128), F32),
        pltpu.VMEM((2, PER, BAND + 16, 128), F32),
        pltpu.VMEM((2, PER, BAND, 256), BF),
    ]
    if half == 0:
        args, specs, alias = (place, near, lanes, nine), [SMEM] + [VMEM] * 3, {}
    else:
        args = (place, near, far, lanes, nine, whole)
        specs = [SMEM] + [VMEM] * 4 + [pl.BlockSpec(memory_space=pl.ANY)]
        alias = {5: 0}
    return pl.pallas_call(
        functools.partial(tensor_kernel, half),
        grid=(640 // BAND,),
        out_shape=jax.ShapeDtypeStruct((640, 2048), F32),
        in_specs=specs,
        out_specs=pl.BlockSpec((BAND, 1024), lambda g: (g, half)),
        scratch_shapes=scratch,
        input_output_aliases=alias,
        compiler_params=pltpu.CompilerParams(vmem_limit_bytes=40 * 2**20),
        cost_estimate=pl.CostEstimate(flops=10**9, bytes_accessed=9 * 2**20, transcendentals=0),
    )(*args)


def edges(place, whole, rows):
    scratch = [pltpu.VMEM((TILES, 32, 128), F32), pltpu.VMEM((2, TILES, 16, 128), F32)]
    return pl.pallas_call(
        edge_kernel,
        grid=(2,),
        out_shape=jax.ShapeDtypeStruct((640, 2048), F32),
        in_specs=[
            SMEM,
            pl.BlockSpec(memory_space=pl.ANY),
            pl.BlockSpec((1, 32, NEAR + FAR), lambda g: (g, 0, 0)),
        ],
        out_specs=pl.BlockSpec((8, 2048), lambda g: (79 * g, 0)),
        scratch_shapes=scratch,
        input_output_aliases={1: 0},
        compiler_params=pltpu.CompilerParams(vmem_limit_bytes=16 * 2**20),
        cost_estimate=pl.CostEstimate(flops=10**7, bytes_accessed=2**19, transcendentals=0),
    )(place, whole, rows)


def window_bounds(fan_bounds, block):
    column = []
    for slot, k in enumerate(WAVES):
        column += [0, 64] if slot == 0 else [k, 128 - k]
    pick = jnp.asarray(np.array(column, np.int32))[block]
    table = fan_bounds[:, : NT // 2].reshape(2, 64, 128)
    mine = lax.dynamic_slice(table, (0, 0, pick), (2, 64, 1))
    top = jnp.broadcast_to(fan_bounds[:, NT // 2].reshape(2, 1, 1), (2, 8, 1))
    both = jnp.broadcast_to(jnp.concatenate([mine, top], axis=1), (2, 72, 128))
    return both[0], both[1]


def after_kernel(value_ref, sign_ref, out_ref):
    pass


def after(value, sign):
    return pl.pallas_call(
        after_kernel,
        out_shape=jax.ShapeDtypeStruct(value.shape, value.dtype),
        in_specs=[ANY, ANY],
        out_specs=ANY,
        input_output_aliases={0: 0},
        cost_estimate=pl.CostEstimate(flops=0, bytes_accessed=0, transcendentals=0),
    )(value, sign)


def trimmed(near, far):
    top = jnp.concatenate([near[:16], far[:16]], axis=1)
    bottom = jnp.concatenate([near[624:], far[624:]], axis=1)
    above = lax.ppermute(bottom, "chan", [(i, i + 1) for i in range(15)])
    below = lax.ppermute(top, "chan", [(i + 1, i) for i in range(15)])
    return jnp.stack(
        [jnp.concatenate([above, top], axis=0), jnp.concatenate([bottom, below], axis=0)]
    )


def per_device(record, channel_ok, fan_bounds):
    chan, part = lax.axis_index("chan"), lax.axis_index("tm")
    block = chan * 8 + part
    place = jnp.stack([chan, part]).astype(jnp.int32)
    series = lax.all_to_all(record.reshape(8, ROWS, 2048), "tm", 0, 0, tiled=True)
    good = lax.dynamic_slice(channel_ok, (part * ROWS,), (ROWS,)).astype(F32)
    good = jnp.broadcast_to(good[:, None], (ROWS, 128))
    low, high = window_bounds(fan_bounds, block)
    corner = lax.broadcasted_iota(jnp.int32, (8, 128), 0) == 0
    packed = (corner & (block == 0)).astype(F32)
    spectra = forward(series, good, low, high, packed)
    pencil = lax.all_to_all(spectra, ("chan", "tm"), 0, 0, tiled=True)
    passed = channels(pencil, low, high, packed)
    back = lax.all_to_all(passed, ("chan", "tm"), 0, 0, tiled=True)
    near, far = backward(back)
    near = lax.all_to_all(near, "tm", 0, 0, tiled=True).reshape(640, NEAR)
    whole = tensor(0, place, near)
    far = lax.all_to_all(after(far, near), "tm", 0, 0, tiled=True).reshape(640, FAR)
    rows = trimmed(near, far)
    whole = tensor(1, place, near, far, whole)
    return edges(place, whole, rows)


def solution(mesh):
    in_specs = (P("chan", "tm"), P("chan"), P())
    out_specs = P("chan", "tm")
    return jax.shard_map(
        per_device, mesh=mesh, in_specs=in_specs, out_specs=out_specs, check_vma=False
    )
```

```python
import functools
import math

import jax
import jax.numpy as jnp
import ml_dtypes
import numpy as np
from jax import lax
from jax.experimental import pallas as pl
from jax.experimental.pallas import tpu as pltpu
from jax.sharding import PartitionSpec as P

NC = 10240
NT = 16384
TF = 128
R = 4
ROWS = 80
GROUP = 63
NEAR = 1280
FAR = 896
BF = jnp.bfloat16
F32 = jnp.float32
VMEM = pl.BlockSpec(memory_space=pltpu.VMEM)
SMEM = pl.BlockSpec(memory_space=pltpu.SMEM)
ANY = pl.BlockSpec(memory_space=pl.ANY)

WAVES = [0] + [8 * n for n in range(1, 8)] + [4 + 8 * n for n in range(8)]
WAVES += [q + 8 * n for q in (1, 2, 3) for n in range(16)]


def two_parts(matrix):
    high = matrix.astype(ml_dtypes.bfloat16)
    low = (matrix - high.astype(np.float64)).astype(ml_dtypes.bfloat16)
    return high, low


def turn(numbers, length):
    angle = (numbers % length) * (2.0 * np.pi / length)
    return np.cos(angle), np.sin(angle)


def time_tables():
    n = np.arange(128)[:, None]
    j = np.concatenate([np.arange(64), 127 - np.arange(64)])[None, :]
    cos, sin = turn(n * j, 128)

    def halves(re, im):
        return np.concatenate([re[:, :64], im[:, :64], re[:, 64:], im[:, 64:]], axis=1)

    forward = np.concatenate([halves(cos, -sin), halves(sin, cos)], axis=0)
    backward = np.concatenate(
        [halves(cos, -sin).T, halves(sin, cos).T], axis=1
    ) / NT
    jj = np.arange(64)[None, :]
    c0, s0 = turn(n * 128 * jj, NT)
    c1, s1 = turn(n * (64 + 128 * jj), NT)
    zero = np.zeros((128, 128))
    even = np.concatenate([c0, -s0], axis=1)
    even[:, 64] = 1.0 - 2.0 * (np.arange(128) % 2)
    odd = np.concatenate([c1, -s1], axis=1)
    first = np.concatenate(
        [np.concatenate([even, zero], axis=1), np.concatenate([zero, odd], axis=1)], axis=0
    )
    weight = np.full(256, 2.0)
    weight[0] = 1.0
    weight[64] = 1.0
    last = (first * weight[None, :]).T / NT
    k = np.array(WAVES)[:, None]
    tw_cos, tw_sin = turn(k * np.arange(128)[None, :], NT)
    return forward, backward, first, last, tw_cos, tw_sin


def chan_tables():
    cos, sin = turn(np.arange(128)[:, None] * np.arange(128)[None, :], 128)
    forward = np.block([[cos, -sin], [sin, cos]])
    backward = np.block([[cos, sin], [-sin, cos]])
    tw_cos, tw_sin = turn(np.arange(ROWS)[:, None] * np.arange(128)[None, :], NC)
    return forward, backward, tw_cos, tw_sin


def plus(a, b):
    if a is None:
        return b
    if b is None:
        return a
    return a + b


def minus(a, b):
    if b is None:
        return a
    if a is None:
        return -b
    return a - b


def times(value, number):
    if value is None or number == 0.0:
        return None
    if number == 1.0:
        return value
    if number == -1.0:
        return -value
    return value * number


def cadd(x, y):
    return plus(x[0], y[0]), plus(x[1], y[1])


def csub(x, y):
    return minus(x[0], y[0]), minus(x[1], y[1])


def spun(x, step, length, sign):
    step = step % length
    if 4 * step % length == 0:
        quarter = 4 * step // length
        c = (1.0, 0.0, -1.0, 0.0)[quarter]
        s = (0.0, 1.0, 0.0, -1.0)[quarter]
    else:
        c = math.cos(2.0 * math.pi * step / length)
        s = math.sin(2.0 * math.pi * step / length)
    s = sign * s
    re, im = x
    if 8 * step % length == 0 and 4 * step % length != 0 and re is not None and im is not None:
        a = abs(c)
        u = re if c > 0 else -re
        v = im if c > 0 else -im
        if c * s > 0:
            return (u - v) * a, (v + u) * a
        return (u + v) * a, (v - u) * a
    return minus(times(re, c), times(im, s)), plus(times(im, c), times(re, s))


def fft_list(xs, sign):
    count = len(xs)
    if count == 1:
        return xs
    even = fft_list(xs[0::2], sign)
    odd = fft_list(xs[1::2], sign)
    head, tail = [], []
    for k in range(count // 2):
        t = spun(odd[k], k, count, sign)
        head.append(cadd(even[k], t))
        tail.append(csub(even[k], t))
    return head + tail


def rfft_list(xs):
    count = len(xs)
    if count == 2:
        return [(xs[0] + xs[1], None), (xs[0] - xs[1], None)]
    even = rfft_list(xs[0::2])
    odd = rfft_list(xs[1::2])
    out = [None] * (count // 2 + 1)
    for k in range(count // 4 + 1):
        t = spun(odd[k], k, count, -1.0)
        out[k] = cadd(even[k], t)
        if k < count // 4:
            re, im = csub(even[k], t)
            out[count // 2 - k] = (re, minus(None, im) if im is not None else None)
    return out


def irfft_list(ys):
    half = len(ys) - 1
    count = 2 * half
    if count == 2:
        return [ys[0][0] + ys[1][0], ys[0][0] - ys[1][0]]
    evens, odds = [], []
    for k in range(count // 4 + 1):
        mirror = (ys[half - k][0], minus(None, ys[half - k][1]) if ys[half - k][1] is not None else None)
        if 2 * k == half:
            evens.append((ys[k][0] * 2.0, None))
            re, _ = spun(ys[k], k, count, 1.0)
            odds.append((re * 2.0, None))
        else:
            both = cadd(ys[k], mirror)
            gap = spun(csub(ys[k], mirror), k, count, 1.0)
            if k == 0:
                both = (both[0], None)
                gap = (gap[0], None)
            evens.append(both)
            odds.append(gap)
    even = irfft_list(evens)
    odd = irfft_list(odds)
    out = []
    for e, o in zip(even, odd):
        out += [e, o]
    return out


def fft5(xs, sign):
    c1, c2 = math.cos(2 * math.pi / 5), math.cos(4 * math.pi / 5)
    s1, s2 = math.sin(2 * math.pi / 5), math.sin(4 * math.pi / 5)
    out = [[None, None] for _ in range(5)]
    pairs = []
    for part in range(2):
        x = [v[part] for v in xs]
        t1, t2, t3, t4 = x[1] + x[4], x[2] + x[3], x[1] - x[4], x[2] - x[3]
        out[0][part] = x[0] + t1 + t2
        pairs.append(
            (
                x[0] + c1 * t1 + c2 * t2,
                x[0] + c2 * t1 + c1 * t2,
                s1 * t3 + s2 * t4,
                s2 * t3 - s1 * t4,
            )
        )
    (ra, rb, rc, rd), (ia, ib, ic, idd) = pairs
    if sign > 0:
        out[1] = [ra - ic, ia + rc]
        out[4] = [ra + ic, ia - rc]
        out[2] = [rb - idd, ib + rd]
        out[3] = [rb + idd, ib - rd]
    else:
        out[1] = [ra + ic, ia - rc]
        out[4] = [ra - ic, ia + rc]
        out[2] = [rb + idd, ib - rd]
        out[3] = [rb - idd, ib + rd]
    return [tuple(v) for v in out]


def dot(a, b):
    return lax.dot_general(a, b, (((1,), (0,)), ((), ())), preferred_element_type=F32)


def parted(value):
    high = value.astype(BF)
    low = (value - high.astype(F32)).astype(BF)
    return high, low


def forward_kernel(
    x_ref, ok_ref, low_ref, high_ref, packed_ref, tc_ref, ts_ref, w_ref, w0_ref, out_ref,
    stage, hi_ref, lo_ref
):
    def tile_body(tile, carry):
        rows = pl.ds(pl.multiple_of(tile * 16, 16), 16)
        good = ok_ref[rows, :]
        for a in range(16):
            xs = [x_ref[s, rows, a * 128 : (a + 1) * 128].astype(F32) * good for s in range(8)]
            ys = rfft_list(xs)
            stage[a, 0] = ys[0][0]
            for q in (1, 2, 3):
                re, im = spun(ys[q], a * q, 128, -1.0)
                stage[a, 2 * q] = re
                stage[a, 2 * q + 1] = im
            stage[a, 1] = ys[4][0]

        def put(slot, re, im):
            base = pl.ds(pl.multiple_of(slot * ROWS + tile * 16, 16), 16)
            for part, value in enumerate((re, im)):
                high, low = parted(value)
                hi_ref[base, part * 128 : (part + 1) * 128] = high
                lo_ref[base, part * 128 : (part + 1) * 128] = low

        def twist(slot, value):
            re, im = value
            c = tc_ref[slot : slot + 1, :]
            s = ts_ref[slot : slot + 1, :]
            put(slot, re * c + im * s, im * c - re * s)

        ys = rfft_list([stage[a, 0] for a in range(16)])
        put(0, ys[0][0], ys[8][0])
        for n in range(1, 8):
            twist(n, ys[n])
        ys = fft_list([spun((stage[a, 1], None), a, 32, -1.0) for a in range(16)], -1.0)
        for n in range(8):
            twist(8 + n, ys[n])
        for q in (1, 2, 3):
            ys = fft_list([(stage[a, 2 * q], stage[a, 2 * q + 1]) for a in range(16)], -1.0)
            for n in range(16):
                twist(16 * q + n, ys[n])
        return carry

    lax.fori_loop(0, 5, tile_body, 0, unroll=5)

    def mixed(rows, w):
        high, low = hi_ref[rows, :], lo_ref[rows, :]
        return dot(high, w[0]) + dot(low, w[0]) + dot(high, w[1])

    first = mixed(pl.ds(0, ROWS), w0_ref).astype(BF)
    out_ref[0] = first[:, :128]
    out_ref[1] = first[:, 128:]

    def wave_body(step, carry):
        res = mixed(pl.ds(pl.multiple_of(ROWS + step * GROUP * ROWS, 16), GROUP * ROWS), w_ref).astype(BF)
        for n in range(GROUP):
            out_ref[2 + 2 * GROUP * step + 2 * n] = res[n * ROWS : (n + 1) * ROWS, :128]
            out_ref[3 + 2 * GROUP * step + 2 * n] = res[n * ROWS : (n + 1) * ROWS, 128:]
        return carry

    lax.fori_loop(0, 63 // GROUP, wave_body, 0)


def backward_kernel(in_ref, tc_ref, ts_ref, w_ref, w0_ref, near_ref, far_ref, stage, mid_ref):
    def joined(slot):
        return jnp.concatenate([in_ref[2 * slot], in_ref[2 * slot + 1]], axis=1)

    first = joined(0)
    mid_ref[pl.ds(0, ROWS), :] = dot(first, w0_ref[0]) + dot(first, w0_ref[1])

    def wave_body(step, carry):
        data = jnp.concatenate([joined(1 + step * GROUP + n) for n in range(GROUP)], axis=0)
        mid_ref[pl.ds(pl.multiple_of(ROWS + step * GROUP * ROWS, 16), GROUP * ROWS), :] = dot(
            data, w_ref[0]
        ) + dot(data, w_ref[1])
        return carry

    lax.fori_loop(0, 63 // GROUP, wave_body, 0)
    lane = lax.broadcasted_iota(jnp.int32, (16, 128), 1)

    def tile_body(tile, carry):
        def get(slot):
            base = pl.ds(pl.multiple_of(slot * ROWS + tile * 16, 16), 16)
            return mid_ref[base, :128], mid_ref[base, 128:]

        def twisted(slot):
            re, im = get(slot)
            c = tc_ref[slot : slot + 1, :]
            s = ts_ref[slot : slot + 1, :]
            return re * c - im * s, im * c + re * s

        mean, top = get(0)
        ys = irfft_list([(mean, None)] + [twisted(n) for n in range(1, 8)] + [(top, None)])
        for a in range(16):
            stage[a, 0] = ys[a]
        ys = fft_list([twisted(8 + n) for n in range(8)] + [(None, None)] * 8, 1.0)
        for a in range(16):
            stage[a, 1] = 2.0 * spun(ys[a], a, 32, 1.0)[0]
        for q in (1, 2, 3):
            ys = fft_list([twisted(16 * q + n) for n in range(16)], 1.0)
            for a in range(16):
                re, im = spun(ys[a], a * q, 128, 1.0)
                stage[a, 2 * q] = re
                stage[a, 2 * q + 1] = im
        rows = pl.ds(pl.multiple_of(tile * 16, 16), 16)

        def series(a):
            parts = [(stage[a, 0], None)]
            parts += [(stage[a, 2 * q], stage[a, 2 * q + 1]) for q in (1, 2, 3)]
            return [y.astype(BF) for y in irfft_list(parts + [(stage[a, 1], None)])]

        ends = {}
        for a in range(16):
            ys = series(a)
            for s in range(8):
                if a < 9:
                    near_ref[s, rows, a * 128 + 128 : a * 128 + 256] = ys[s]
                else:
                    far_ref[s, rows, (a - 9) * 128 : (a - 8) * 128] = ys[s]
            if a in (0, 15):
                ends[a] = ys
        blank = jnp.zeros((16, 128), BF)
        for s in range(8):
            after = ends[0][s + 1] if s < 7 else blank
            before = ends[15][s - 1] if s > 0 else blank
            near_ref[s, rows, :128] = jnp.where(
                lane < 64, after.astype(F32), before.astype(F32)
            ).astype(BF)
        return carry

    lax.fori_loop(0, 5, tile_body, 0, unroll=5)


STEP = 40


def channel_kernel(
    in_ref, low_ref, high_ref, first_ref, tc_ref, ts_ref, w_ref, v_ref, out_ref,
    flat, u_re, u_im, a_re, a_im
):
    def load_body(p, carry):
        flat[pl.ds(pl.multiple_of(p * ROWS, 8), ROWS), :] = in_ref[p].astype(F32)
        return carry

    lax.fori_loop(0, 128, load_body, 0, unroll=16)
    packed = first_ref[...]
    blank = jnp.zeros((8, 128), F32)

    def in_body(step, carry):
        parts = []
        for n in range(STEP):
            turned = flat[pl.ds(step * STEP + n, 128, stride=ROWS), :].T
            re, im = turned[:64], turned[64:]
            im = jnp.concatenate([im[:8] * (1.0 - packed), im[8:], im[:8] * packed], axis=0)
            re = jnp.concatenate([re, blank], axis=0)
            parts.append(jnp.concatenate([re, im], axis=1).astype(BF))
        data = jnp.concatenate(parts, axis=0)
        res = dot(data, w_ref[0]) + dot(data, w_ref[1])
        for n in range(STEP):
            r = step * STEP + n
            re = res[n * 72 : (n + 1) * 72, :128]
            im = res[n * 72 : (n + 1) * 72, 128:]
            c = tc_ref[pl.ds(r, 1), :]
            s = ts_ref[pl.ds(r, 1), :]
            u_re[r] = re * c + im * s
            u_im[r] = im * c - re * s
        return carry

    lax.fori_loop(0, ROWS // STEP, in_body, 0)
    lane = lax.broadcasted_iota(jnp.int32, (8, 128), 1)

    def fan_body(tile, carry):
        rows = pl.ds(pl.multiple_of(tile * 8, 8), 8)
        low = low_ref[rows, :]
        high = high_ref[rows, :]
        for n2 in range(5):
            spots = [(5 * n1 + 16 * n2) % ROWS for n1 in range(16)]
            ys = fft_list([(u_re[r, rows, :], u_im[r, rows, :]) for r in spots], -1.0)
            for k1 in range(16):
                a_re[n2 * 16 + k1] = ys[k1][0]
                a_im[n2 * 16 + k1] = ys[k1][1]
        for k1 in range(16):
            ys = fft5([(a_re[n2 * 16 + k1], a_im[n2 * 16 + k1]) for n2 in range(5)], -1.0)
            kept = []
            for k2 in range(5):
                outer = next(k for k in range(ROWS) if k % 16 == k1 and k % 5 == k2)
                if outer < ROWS // 2:
                    fold = lane + outer * 128
                else:
                    fold = (NC - outer * 128) - lane
                keep = (fold >= low) & (fold <= high)
                kept.append(tuple(jnp.where(keep, v, 0.0) for v in ys[k2]))
            ys = fft5(kept, 1.0)
            for n2 in range(5):
                a_re[n2 * 16 + k1] = ys[n2][0]
                a_im[n2 * 16 + k1] = ys[n2][1]
        for n2 in range(5):
            spots = [(5 * n1 + 16 * n2) % ROWS for n1 in range(16)]
            ys = fft_list([(a_re[n2 * 16 + k1], a_im[n2 * 16 + k1]) for k1 in range(16)], 1.0)
            for n1 in range(16):
                u_re[spots[n1], rows, :] = ys[n1][0]
                u_im[spots[n1], rows, :] = ys[n1][1]
        return carry

    lax.fori_loop(0, 9, fan_body, 0)

    def out_body(step, carry):
        highs, lows = [], []
        for n in range(STEP):
            r = step * STEP + n
            re, im = u_re[r], u_im[r]
            re = jnp.concatenate([re[:8] + re[64:], re[8:64]], axis=0)
            im = jnp.concatenate([im[:8] + im[64:], im[8:64]], axis=0)
            c = tc_ref[pl.ds(r, 1), :]
            s = ts_ref[pl.ds(r, 1), :]
            high, low = parted(jnp.concatenate([re * c - im * s, im * c + re * s], axis=1))
            highs.append(high)
            lows.append(low)
        high = jnp.concatenate(highs, axis=0)
        low = jnp.concatenate(lows, axis=0)
        res = (dot(high, v_ref[0]) + dot(low, v_ref[0]) + dot(high, v_ref[1])) * (1.0 / NC)
        for n in range(STEP):
            block = res[n * 64 : (n + 1) * 64]
            both = jnp.concatenate([block[:, :128], block[:, 128:]], axis=0)
            flat[pl.ds(step * STEP + n, 128, stride=ROWS), :] = both.T
        return carry

    lax.fori_loop(0, ROWS // STEP, out_body, 0)

    def store_body(p, carry):
        out_ref[p] = flat[pl.ds(pl.multiple_of(p * ROWS, 8), ROWS), :].astype(BF)
        return carry

    lax.fori_loop(0, 128, store_body, 0, unroll=16)


TILES = 18


def spread(wide, start, block, count):
    block = block.astype(F32)
    rows = pl.ds(start, count)
    for t in range(17):
        wide[t, rows, :] = block[:, t * 128 : (t + 1) * 128]
    wide[17, rows, :] = block[:, :128]


def ahead(parts, count, lane):
    turned = [pltpu.roll(v, (-count) % 128, 1) for v in parts]
    out = []
    for t in range(len(parts)):
        if count > 0:
            other = turned[t + 1] if t + 1 < len(parts) else turned[t]
            out.append(jnp.where(lane < 128 - count, turned[t], other))
        else:
            other = turned[t - 1] if t > 0 else turned[t]
            out.append(jnp.where(lane < -count, other, turned[t]))
    return out


def products(wide, start, first_keep, last_keep, row_keep, lane):
    low = [wide[t, pl.ds(start, 8), :] for t in range(TILES)]
    here = [wide[t, pl.ds(start + 1, 8), :] for t in range(TILES)]
    high = [wide[t, pl.ds(start + 2, 8), :] for t in range(TILES)]
    right = ahead(here, 1, lane)
    left = ahead(here, -1, lane)
    both = []
    for t in range(TILES):
        grad_time = right[t] - left[t]
        masked = grad_time
        if t == 0:
            masked = jnp.where(first_keep, grad_time, 0.0)
        if t == TILES - 1:
            masked = jnp.where(last_keep, grad_time, 0.0)
        if row_keep is not None:
            masked = jnp.where(row_keep, masked, 0.0)
        both.append(((high[t] - low[t]) * masked, grad_time * masked))
    return both


def quotient(cross, along, lane):
    sums = []
    for parts in (cross, along):
        near, far = ahead(parts, 1, lane), ahead(parts, -1, lane)
        three = [v + n + f for v, n, f in zip(parts, near, far)]
        near, far = ahead(three, 3, lane), ahead(three, -3, lane)
        sums.append([v + n + f for v, n, f in zip(three, near, far)][1:17])
    scale = 1.0 / 324.0
    out = []
    for c, a in zip(*sums):
        out.append((c * -scale) / (a * scale + 1e-05))
    return jnp.concatenate(out, axis=1)


def slide_tables():
    row = np.arange(256)[:, None]
    col = np.arange(128)[None, :]
    change = (row == col + 125) * 1.0 - (row == col + 123) * 1.0
    shift = (row == col + 124) * 1.0
    nine = ((row >= col) & (row <= col + 8)) * 1.0
    nine = np.concatenate([nine[:128], nine[128:]], axis=1)
    return np.concatenate([change, shift], axis=1), np.concatenate([nine, nine], axis=0)


BAND = 128
PER = 9


def tensor_kernel(half, place_ref, *refs):
    if half == 0:
        near_ref, lanes_ref, nine_ref, out_ref, slope, level, prod, trio, both_ref = refs
    else:
        near_ref, far_ref, lanes_ref, nine_ref, _, out_ref = refs[:6]
        slope, level, prod, trio, both_ref = refs[6:]
    lane = lax.broadcasted_iota(jnp.int32, (8, 128), 1)
    step = pl.program_id(0)
    part = place_ref[1]

    def lanes(t, cells):
        res = dot(cells, lanes_ref[...])
        slope[t, 16:656, :] = res[:, :128]
        level[t, 16:656, :] = res[:, 128:]

    def cut(ref, t):
        return ref[:, pl.ds(pl.multiple_of(t * 128, 128), 256)]

    @pl.when(step == 0)
    def _():
        if half == 0:

            def lanes_body(t, carry):
                lanes(t, cut(near_ref, t))
                return carry

            lax.fori_loop(0, PER, lanes_body, 0, unroll=PER)
        else:

            def lanes_body(t, carry):
                lanes(t + 2, cut(far_ref, t))
                return carry

            lanes(0, near_ref[:, 1024:])
            lanes(1, jnp.concatenate([near_ref[:, 1152:], far_ref[:, :128]], axis=1))
            lax.fori_loop(0, PER - 3, lanes_body, 0, unroll=PER - 3)
            lanes(8, jnp.concatenate([far_ref[:, 768:], near_ref[:, :128]], axis=1))

    top = step * BAND

    def prod_body(k, carry):
        start = pl.multiple_of(k * 8, 8)
        base = pl.multiple_of(top + k * 8, 8)
        for t in range(PER):
            grad_time = slope[t, pl.ds(base + 12, 8), :]
            masked = grad_time
            if half == 0 and t == 0:
                masked = jnp.where((lane >= 4) | (part > 0), grad_time, 0.0)
            if half == 1 and t == PER - 1:
                masked = jnp.where((lane < 4) | (part < 7), grad_time, 0.0)
            grad_chan = level[t, pl.ds(base + 13, 8), :] - level[t, pl.ds(base + 11, 8), :]
            prod[0, t, pl.ds(start, 8), :] = grad_chan * masked
            prod[1, t, pl.ds(start, 8), :] = grad_time * masked
        return carry

    lax.fori_loop(0, BAND // 8 + 2, prod_body, 0, unroll=BAND // 8 + 2)

    def trio_body(k, carry):
        start = pl.multiple_of(k * 8, 8)
        for n in range(2):
            for t in range(PER):
                trio[n, t, pl.ds(start, 8), :] = (
                    prod[n, t, pl.ds(start, 8), :]
                    + prod[n, t, pl.ds(start + 1, 8), :]
                    + prod[n, t, pl.ds(start + 2, 8), :]
                )
        return carry

    lax.fori_loop(0, BAND // 8 + 1, trio_body, 0, unroll=BAND // 8 + 1)

    def split_body(k, carry):
        start = pl.multiple_of(k * 16, 16)
        for n in range(2):
            for t in range(PER):
                total = (
                    trio[n, t, pl.ds(start, 16), :]
                    + trio[n, t, pl.ds(start + 3, 16), :]
                    + trio[n, t, pl.ds(start + 6, 16), :]
                )
                high, low = parted(total)
                both_ref[n, t, pl.ds(start, 16), :128] = high
                both_ref[n, t, pl.ds(start, 16), 128:] = low
        return carry

    lax.fori_loop(0, BAND // 16, split_body, 0, unroll=BAND // 16)
    nine = nine_ref[...]
    scale = 1.0 / 324.0

    def sum_body(g, carry):
        sums = []
        for n in range(2):
            res = dot(both_ref[n, pl.ds(g * 4, 5)].reshape(5 * BAND, 256), nine)
            sums.append(res[: 4 * BAND, :128] + res[BAND:, 128:])
        res = (sums[0] * -scale) / (sums[1] * scale + 1e-05)
        for t in range(4):
            cols = pl.ds(pl.multiple_of(g * 512 + t * 128, 128), 128)
            out_ref[:, cols] = res[t * BAND : (t + 1) * BAND]
        return carry

    lax.fori_loop(0, 2, sum_body, 0, unroll=2)


def edge_kernel(place_ref, old_ref, rows_ref, out_ref, wide, prod):
    lane = lax.broadcasted_iota(jnp.int32, (8, 128), 1)
    sub = lax.broadcasted_iota(jnp.int32, (8, 128), 0)
    step = pl.program_id(0)
    chan, part = place_ref[0], place_ref[1]
    for k in range(2):
        rows = pl.ds(k * 16, 16)
        spread(wide, k * 16, rows_ref[0, rows, :], 16)
    open_low = (step == 0) & (chan == 0)
    open_high = (step == 1) & (chan == 15)
    skip = 8 - step * 8
    for k in range(2):
        row = sub + (k * 8 + skip + 4)
        row_keep = ((row >= 16) | jnp.logical_not(open_low)) & (
            (row < 16) | jnp.logical_not(open_high)
        )
        both = products(wide, k * 8 + skip + 3, part > 0, part < 7, row_keep, lane)
        for t in range(TILES):
            prod[0, t, pl.ds(k * 8, 8), :] = both[t][0]
            prod[1, t, pl.ds(k * 8, 8), :] = both[t][1]
    sums = []
    for n in range(2):
        parts = []
        for t in range(TILES):
            total = prod[n, t, pl.ds(0, 8), :]
            for d in range(1, 9):
                total = total + prod[n, t, pl.ds(d, 8), :]
            parts.append(total)
        sums.append(parts)
    out_ref[...] = quotient(sums[0], sums[1], lane)


def call(kernel, out, specs, scratch, flops, *args):
    nbytes = sum(a.size * a.dtype.itemsize for a in args) + 3 * 2**20
    return pl.pallas_call(
        kernel,
        out_shape=out,
        in_specs=[VMEM] * len(args),
        out_specs=specs,
        scratch_shapes=scratch,
        compiler_params=pltpu.CompilerParams(vmem_limit_bytes=48 * 2**20),
        cost_estimate=pl.CostEstimate(flops=flops, bytes_accessed=nbytes, transcendentals=0),
    )(*args)


def pair(matrix):
    return jnp.asarray(np.stack(two_parts(matrix)))


def single(table):
    return jnp.asarray(table.astype(np.float32))


def forward(series, good, low, high, packed):
    fwd, _, first, _, tc, ts = time_tables()
    scratch = [
        pltpu.VMEM((16, 8, 16, 128), F32),
        pltpu.VMEM((64 * ROWS, 256), BF),
        pltpu.VMEM((64 * ROWS, 256), BF),
    ]
    out = jax.ShapeDtypeStruct((128, ROWS, 128), BF)
    tables = single(tc), single(ts), pair(fwd), pair(first)
    return call(forward_kernel, out, VMEM, scratch, 4 * 10**9, series, good, low, high, packed, *tables)


def backward(spectra):
    _, bwd, _, last, tc, ts = time_tables()
    scratch = [pltpu.VMEM((16, 8, 16, 128), F32), pltpu.VMEM((64 * ROWS, 256), F32)]
    out = [jax.ShapeDtypeStruct((8, ROWS, n), BF) for n in (NEAR, FAR)]
    tables = single(tc), single(ts), pair(bwd), pair(last)
    return call(backward_kernel, out, [VMEM, VMEM], scratch, 4 * 10**9, spectra, *tables)


def channels(pencil, low, high, packed):
    fwd, bwd, tc, ts = chan_tables()
    scratch = [
        pltpu.VMEM((128 * ROWS, 128), F32),
        pltpu.VMEM((ROWS, 72, 128), F32),
        pltpu.VMEM((ROWS, 72, 128), F32),
        pltpu.VMEM((ROWS, 8, 128), F32),
        pltpu.VMEM((ROWS, 8, 128), F32),
    ]
    out = jax.ShapeDtypeStruct((128, ROWS, 128), BF)
    tables = single(tc), single(ts), pair(fwd), pair(bwd)
    return call(channel_kernel, out, VMEM, scratch, 8 * 10**9, pencil, low, high, packed, *tables)


def tensor(half, place, near, far=None, whole=None):
    lanes, nine = (jnp.asarray(t.astype(ml_dtypes.bfloat16)) for t in slide_tables())
    scratch = [
        pltpu.VMEM((PER, 672, 128), F32),
        pltpu.VMEM((PER, 672, 128), F32),
        pltpu.VMEM((2, PER, BAND + 16, 128), F32),
        pltpu.VMEM((2, PER, BAND + 16, 128), F32),
        pltpu.VMEM((2, PER, BAND, 256), BF),
    ]
    if half == 0:
        args, specs, alias = (place, near, lanes, nine), [SMEM] + [VMEM] * 3, {}
    else:
        args = (place, near, far, lanes, nine, whole)
        specs = [SMEM] + [VMEM] * 4 + [pl.BlockSpec(memory_space=pl.ANY)]
        alias = {5: 0}
    return pl.pallas_call(
        functools.partial(tensor_kernel, half),
        grid=(640 // BAND,),
        out_shape=jax.ShapeDtypeStruct((640, 2048), F32),
        in_specs=specs,
        out_specs=pl.BlockSpec((BAND, 1024), lambda g: (g, half)),
        scratch_shapes=scratch,
        input_output_aliases=alias,
        compiler_params=pltpu.CompilerParams(vmem_limit_bytes=40 * 2**20),
        cost_estimate=pl.CostEstimate(flops=10**9, bytes_accessed=9 * 2**20, transcendentals=0),
    )(*args)


def edges(place, whole, rows):
    scratch = [pltpu.VMEM((TILES, 32, 128), F32), pltpu.VMEM((2, TILES, 16, 128), F32)]
    return pl.pallas_call(
        edge_kernel,
        grid=(2,),
        out_shape=jax.ShapeDtypeStruct((640, 2048), F32),
        in_specs=[
            SMEM,
            pl.BlockSpec(memory_space=pl.ANY),
            pl.BlockSpec((1, 32, NEAR + FAR), lambda g: (g, 0, 0)),
        ],
        out_specs=pl.BlockSpec((8, 2048), lambda g: (79 * g, 0)),
        scratch_shapes=scratch,
        input_output_aliases={1: 0},
        compiler_params=pltpu.CompilerParams(vmem_limit_bytes=16 * 2**20),
        cost_estimate=pl.CostEstimate(flops=10**7, bytes_accessed=2**19, transcendentals=0),
    )(place, whole, rows)


def window_bounds(fan_bounds, block):
    column = []
    for slot, k in enumerate(WAVES):
        column += [0, 64] if slot == 0 else [k, 128 - k]
    pick = jnp.asarray(np.array(column, np.int32))[block]
    table = fan_bounds[:, : NT // 2].reshape(2, 64, 128)
    mine = lax.dynamic_slice(table, (0, 0, pick), (2, 64, 1))
    top = jnp.broadcast_to(fan_bounds[:, NT // 2].reshape(2, 1, 1), (2, 8, 1))
    both = jnp.broadcast_to(jnp.concatenate([mine, top], axis=1), (2, 72, 128))
    return both[0], both[1]


def after_kernel(value_ref, sign_ref, out_ref):
    pass


def after(value, sign):
    return pl.pallas_call(
        after_kernel,
        out_shape=jax.ShapeDtypeStruct(value.shape, value.dtype),
        in_specs=[ANY, ANY],
        out_specs=ANY,
        input_output_aliases={0: 0},
        cost_estimate=pl.CostEstimate(flops=0, bytes_accessed=0, transcendentals=0),
    )(value, sign)


def trimmed(near, far):
    top = jnp.concatenate([near[:16], far[:16]], axis=1)
    bottom = jnp.concatenate([near[624:], far[624:]], axis=1)
    above = lax.ppermute(bottom, "chan", [(i, i + 1) for i in range(15)])
    below = lax.ppermute(top, "chan", [(i + 1, i) for i in range(15)])
    return jnp.stack(
        [jnp.concatenate([above, top], axis=0), jnp.concatenate([bottom, below], axis=0)]
    )


def per_device(record, channel_ok, fan_bounds):
    chan, part = lax.axis_index("chan"), lax.axis_index("tm")
    block = chan * 8 + part
    place = jnp.stack([chan, part]).astype(jnp.int32)
    series = lax.all_to_all(record.reshape(8, ROWS, 2048), "tm", 0, 0, tiled=True)
    good = lax.dynamic_slice(channel_ok, (part * ROWS,), (ROWS,)).astype(F32)
    good = jnp.broadcast_to(good[:, None], (ROWS, 128))
    low, high = window_bounds(fan_bounds, block)
    corner = lax.broadcasted_iota(jnp.int32, (8, 128), 0) == 0
    packed = (corner & (block == 0)).astype(F32)
    spectra = forward(series, good, low, high, packed)
    pencil = lax.all_to_all(spectra, ("chan", "tm"), 0, 0, tiled=True)
    passed = channels(pencil, low, high, packed)
    back = lax.all_to_all(passed, ("chan", "tm"), 0, 0, tiled=True)
    near, far = backward(back)
    near = lax.all_to_all(near, "tm", 0, 0, tiled=True).reshape(640, NEAR)
    whole = tensor(0, place, near)
    far = lax.all_to_all(after(far, near), "tm", 0, 0, tiled=True).reshape(640, FAR)
    rows = trimmed(near, far)
    whole = tensor(1, place, near, far, whole)
    return edges(place, whole, rows)


def solution(mesh):
    in_specs = (P("chan", "tm"), P("chan"), P())
    out_specs = P("chan", "tm")
    return jax.shard_map(
        per_device, mesh=mesh, in_specs=in_specs, out_specs=out_specs, check_vma=False
    )
```

```python
import functools
import math

import jax
import jax.numpy as jnp
import ml_dtypes
import numpy as np
from jax import lax
from jax.experimental import pallas as pl
from jax.experimental.pallas import tpu as pltpu
from jax.sharding import PartitionSpec as P

NC = 10240
NT = 16384
ROWS = 80
TF = 128
R = 4
GROUP = 63
SIDE = 9 * ROWS
OUTER = SIDE + 16
NEAR = OUTER + 7 * 16
FAR = 896
BF = jnp.bfloat16
F32 = jnp.float32
VMEM = pl.BlockSpec(memory_space=pltpu.VMEM)
SMEM = pl.BlockSpec(memory_space=pltpu.SMEM)
ANY = pl.BlockSpec(memory_space=pl.ANY)

WAVES = [0] + [8 * n for n in range(1, 8)] + [4 + 8 * n for n in range(8)]
WAVES += [q + 8 * n for q in (1, 2, 3) for n in range(16)]


def two_parts(matrix):
    high = matrix.astype(ml_dtypes.bfloat16)
    low = (matrix - high.astype(np.float64)).astype(ml_dtypes.bfloat16)
    return high, low


def turn(numbers, length):
    angle = (numbers % length) * (2.0 * np.pi / length)
    return np.cos(angle), np.sin(angle)


def time_tables():
    n = np.arange(128)[:, None]
    j = np.concatenate([np.arange(64), 127 - np.arange(64)])[None, :]
    cos, sin = turn(n * j, 128)

    def halves(re, im):
        return np.concatenate([re[:, :64], im[:, :64], re[:, 64:], im[:, 64:]], axis=1)

    forward = np.concatenate([halves(cos, -sin), halves(sin, cos)], axis=0)
    backward = np.concatenate(
        [halves(cos, -sin).T, halves(sin, cos).T], axis=1
    ) / NT
    jj = np.arange(64)[None, :]
    c0, s0 = turn(n * 128 * jj, NT)
    c1, s1 = turn(n * (64 + 128 * jj), NT)
    zero = np.zeros((128, 128))
    even = np.concatenate([c0, -s0], axis=1)
    even[:, 64] = 1.0 - 2.0 * (np.arange(128) % 2)
    odd = np.concatenate([c1, -s1], axis=1)
    first = np.concatenate(
        [np.concatenate([even, zero], axis=1), np.concatenate([zero, odd], axis=1)], axis=0
    )
    weight = np.full(256, 2.0)
    weight[0] = 1.0
    weight[64] = 1.0
    last = (first * weight[None, :]).T / NT
    k = np.array(WAVES)[:, None]
    tw_cos, tw_sin = turn(k * np.arange(128)[None, :], NT)
    return forward, backward, first, last, tw_cos, tw_sin


def chan_tables():
    cos, sin = turn(np.arange(128)[:, None] * np.arange(128)[None, :], 128)
    forward = np.block([[cos, -sin], [sin, cos]])
    backward = np.block([[cos, sin], [-sin, cos]])
    tw_cos, tw_sin = turn(np.arange(ROWS)[:, None] * np.arange(128)[None, :], NC)
    return forward, backward, tw_cos, tw_sin


def plus(a, b):
    if a is None:
        return b
    if b is None:
        return a
    return a + b


def minus(a, b):
    if b is None:
        return a
    if a is None:
        return -b
    return a - b


def times(value, number):
    if value is None or number == 0.0:
        return None
    if number == 1.0:
        return value
    if number == -1.0:
        return -value
    return value * number


def cadd(x, y):
    return plus(x[0], y[0]), plus(x[1], y[1])


def csub(x, y):
    return minus(x[0], y[0]), minus(x[1], y[1])


def spun(x, step, length, sign):
    step = step % length
    if 4 * step % length == 0:
        quarter = 4 * step // length
        c = (1.0, 0.0, -1.0, 0.0)[quarter]
        s = (0.0, 1.0, 0.0, -1.0)[quarter]
    else:
        c = math.cos(2.0 * math.pi * step / length)
        s = math.sin(2.0 * math.pi * step / length)
    s = sign * s
    re, im = x
    if 8 * step % length == 0 and 4 * step % length != 0 and re is not None and im is not None:
        a = abs(c)
        u = re if c > 0 else -re
        v = im if c > 0 else -im
        if c * s > 0:
            return (u - v) * a, (v + u) * a
        return (u + v) * a, (v - u) * a
    return minus(times(re, c), times(im, s)), plus(times(im, c), times(re, s))


def fft_list(xs, sign):
    count = len(xs)
    if count == 1:
        return xs
    even = fft_list(xs[0::2], sign)
    odd = fft_list(xs[1::2], sign)
    head, tail = [], []
    for k in range(count // 2):
        t = spun(odd[k], k, count, sign)
        head.append(cadd(even[k], t))
        tail.append(csub(even[k], t))
    return head + tail


def rfft_list(xs):
    count = len(xs)
    if count == 2:
        return [(xs[0] + xs[1], None), (xs[0] - xs[1], None)]
    even = rfft_list(xs[0::2])
    odd = rfft_list(xs[1::2])
    out = [None] * (count // 2 + 1)
    for k in range(count // 4 + 1):
        t = spun(odd[k], k, count, -1.0)
        out[k] = cadd(even[k], t)
        if k < count // 4:
            re, im = csub(even[k], t)
            out[count // 2 - k] = (re, minus(None, im) if im is not None else None)
    return out


def irfft_list(ys):
    half = len(ys) - 1
    count = 2 * half
    if count == 2:
        return [ys[0][0] + ys[1][0], ys[0][0] - ys[1][0]]
    evens, odds = [], []
    for k in range(count // 4 + 1):
        mirror = (ys[half - k][0], minus(None, ys[half - k][1]) if ys[half - k][1] is not None else None)
        if 2 * k == half:
            evens.append((ys[k][0] * 2.0, None))
            re, _ = spun(ys[k], k, count, 1.0)
            odds.append((re * 2.0, None))
        else:
            both = cadd(ys[k], mirror)
            gap = spun(csub(ys[k], mirror), k, count, 1.0)
            if k == 0:
                both = (both[0], None)
                gap = (gap[0], None)
            evens.append(both)
            odds.append(gap)
    even = irfft_list(evens)
    odd = irfft_list(odds)
    out = []
    for e, o in zip(even, odd):
        out += [e, o]
    return out


def fft5(xs, sign):
    c1, c2 = math.cos(2 * math.pi / 5), math.cos(4 * math.pi / 5)
    s1, s2 = math.sin(2 * math.pi / 5), math.sin(4 * math.pi / 5)
    out = [[None, None] for _ in range(5)]
    pairs = []
    for part in range(2):
        x = [v[part] for v in xs]
        t1, t2, t3, t4 = x[1] + x[4], x[2] + x[3], x[1] - x[4], x[2] - x[3]
        out[0][part] = x[0] + t1 + t2
        pairs.append(
            (
                x[0] + c1 * t1 + c2 * t2,
                x[0] + c2 * t1 + c1 * t2,
                s1 * t3 + s2 * t4,
                s2 * t3 - s1 * t4,
            )
        )
    (ra, rb, rc, rd), (ia, ib, ic, idd) = pairs
    if sign > 0:
        out[1] = [ra - ic, ia + rc]
        out[4] = [ra + ic, ia - rc]
        out[2] = [rb - idd, ib + rd]
        out[3] = [rb + idd, ib - rd]
    else:
        out[1] = [ra + ic, ia - rc]
        out[4] = [ra - ic, ia + rc]
        out[2] = [rb + idd, ib - rd]
        out[3] = [rb - idd, ib + rd]
    return [tuple(v) for v in out]


def dot(a, b):
    return lax.dot_general(a, b, (((1,), (0,)), ((), ())), preferred_element_type=F32)


def parted(value):
    high = value.astype(BF)
    low = (value - high.astype(F32)).astype(BF)
    return high, low


def forward_kernel(
    place_ref, x_ref, ok_ref, low_ref, high_ref, packed_ref, tc_ref, ts_ref, w_ref, w0_ref, out_ref,
    stage, hi_ref, lo_ref
):
    def tile_body(tile, carry):
        rows = pl.ds(pl.multiple_of(tile * 16, 16), 16)
        good = ok_ref[rows, :]
        for a in range(16):
            xs = [x_ref[s, rows, a * 128 : (a + 1) * 128].astype(F32) * good for s in range(8)]
            ys = rfft_list(xs)
            stage[a, 0] = ys[0][0]
            for q in (1, 2, 3):
                re, im = spun(ys[q], a * q, 128, -1.0)
                stage[a, 2 * q] = re
                stage[a, 2 * q + 1] = im
            stage[a, 1] = ys[4][0]

        def put(slot, re, im):
            base = pl.ds(pl.multiple_of(slot * ROWS + tile * 16, 16), 16)
            for part, value in enumerate((re, im)):
                high, low = parted(value)
                hi_ref[base, part * 128 : (part + 1) * 128] = high
                lo_ref[base, part * 128 : (part + 1) * 128] = low

        def twist(slot, value):
            re, im = value
            c = tc_ref[slot : slot + 1, :]
            s = ts_ref[slot : slot + 1, :]
            put(slot, re * c + im * s, im * c - re * s)

        ys = rfft_list([stage[a, 0] for a in range(16)])
        put(0, ys[0][0], ys[8][0])
        for n in range(1, 8):
            twist(n, ys[n])
        ys = fft_list([spun((stage[a, 1], None), a, 32, -1.0) for a in range(16)], -1.0)
        for n in range(8):
            twist(8 + n, ys[n])
        for q in (1, 2, 3):
            ys = fft_list([(stage[a, 2 * q], stage[a, 2 * q + 1]) for a in range(16)], -1.0)
            for n in range(16):
                twist(16 * q + n, ys[n])
        return carry

    lax.fori_loop(0, 5, tile_body, 0, unroll=5)

    def mixed(rows, w):
        high, low = hi_ref[rows, :], lo_ref[rows, :]
        return dot(high, w[0]) + dot(low, w[0]) + dot(high, w[1])

    first = mixed(pl.ds(0, ROWS), w0_ref).astype(BF)
    out_ref[0] = first[:, :128]
    out_ref[1] = first[:, 128:]

    def wave_body(step, carry):
        res = mixed(pl.ds(pl.multiple_of(ROWS + step * GROUP * ROWS, 16), GROUP * ROWS), w_ref).astype(BF)
        for n in range(GROUP):
            out_ref[2 + 2 * GROUP * step + 2 * n] = res[n * ROWS : (n + 1) * ROWS, :128]
            out_ref[3 + 2 * GROUP * step + 2 * n] = res[n * ROWS : (n + 1) * ROWS, 128:]
        return carry

    lax.fori_loop(0, 63 // GROUP, wave_body, 0)


def backward_kernel(
    place_ref, in_ref, tc_ref, ts_ref, w_ref, w0_ref, near_ref, far_ref, stage, mid_ref
):
    def joined(slot):
        return jnp.concatenate([in_ref[2 * slot], in_ref[2 * slot + 1]], axis=1)

    first = joined(0)
    mid_ref[pl.ds(0, ROWS), :] = dot(first, w0_ref[0]) + dot(first, w0_ref[1])

    def wave_body(step, carry):
        data = jnp.concatenate([joined(1 + step * GROUP + n) for n in range(GROUP)], axis=0)
        mid_ref[pl.ds(pl.multiple_of(ROWS + step * GROUP * ROWS, 16), GROUP * ROWS), :] = dot(
            data, w_ref[0]
        ) + dot(data, w_ref[1])
        return carry

    lax.fori_loop(0, 63 // GROUP, wave_body, 0)
    lane = lax.broadcasted_iota(jnp.int32, (16, 128), 1)

    sides = [jnp.zeros((16, 128), F32) for _ in range(8)]
    for tile in range(5):

        def get(slot):
            base = pl.ds(slot * ROWS + tile * 16, 16)
            return mid_ref[base, :128], mid_ref[base, 128:]

        def twisted(slot):
            re, im = get(slot)
            c = tc_ref[slot : slot + 1, :]
            s = ts_ref[slot : slot + 1, :]
            return re * c - im * s, im * c + re * s

        mean, top = get(0)
        ys = irfft_list([(mean, None)] + [twisted(n) for n in range(1, 8)] + [(top, None)])
        for a in range(16):
            stage[a, 0] = ys[a]
        ys = fft_list([twisted(8 + n) for n in range(8)] + [(None, None)] * 8, 1.0)
        for a in range(16):
            stage[a, 1] = 2.0 * spun(ys[a], a, 32, 1.0)[0]
        for q in (1, 2, 3):
            ys = fft_list([twisted(16 * q + n) for n in range(16)], 1.0)
            for a in range(16):
                re, im = spun(ys[a], a * q, 128, 1.0)
                stage[a, 2 * q] = re
                stage[a, 2 * q + 1] = im
        rows = pl.ds(tile * 16, 16)

        def series(a):
            parts = [(stage[a, 0], None)]
            parts += [(stage[a, 2 * q], stage[a, 2 * q + 1]) for q in (1, 2, 3)]
            return [y.astype(BF) for y in irfft_list(parts + [(stage[a, 1], None)])]

        ends = {}
        for a in range(16):
            ys = series(a)
            for s in range(8):
                if a < 9:
                    near_ref[s, pl.ds(a * ROWS + tile * 16, 16), :] = ys[s]
                else:
                    far_ref[s, rows, (a - 9) * 128 : (a - 8) * 128] = ys[s]
            if a in (0, 15):
                ends[a] = ys
        blank = jnp.zeros((16, 128), BF)
        for s in range(8):
            after = ends[0][s + 1] if s < 7 else blank
            before = ends[15][s - 1] if s > 0 else blank
            both = jnp.where(lane < 64, after.astype(F32), before.astype(F32))
            here = ((lane - 16 * tile + 5) & 127) < 10
            sides[s] = jnp.where(here, pltpu.roll(both, 16 * tile, 1), sides[s])
    base = pl.multiple_of(jnp.where(place_ref[1] == 7, 64, 0), 16)
    for s in range(8):
        near_ref[s, pl.ds(SIDE, 16), :] = sides[s].astype(BF)
        for n in range(7):
            near_ref[s, pl.ds(OUTER + 16 * n, 16), :] = far_ref[
                s, pl.ds(base, 16), n * 128 : (n + 1) * 128
            ]


STEP = 40


def channel_kernel(
    in_ref, low_ref, high_ref, first_ref, tc_ref, ts_ref, w_ref, v_ref, out_ref,
    flat, u_re, u_im, a_re, a_im
):
    def load_body(p, carry):
        flat[pl.ds(pl.multiple_of(p * ROWS, 8), ROWS), :] = in_ref[p].astype(F32)
        return carry

    lax.fori_loop(0, 128, load_body, 0, unroll=16)
    packed = first_ref[...]
    blank = jnp.zeros((8, 128), F32)

    def in_body(step, carry):
        parts = []
        for n in range(STEP):
            turned = flat[pl.ds(step * STEP + n, 128, stride=ROWS), :].T
            re, im = turned[:64], turned[64:]
            im = jnp.concatenate([im[:8] * (1.0 - packed), im[8:], im[:8] * packed], axis=0)
            re = jnp.concatenate([re, blank], axis=0)
            parts.append(jnp.concatenate([re, im], axis=1).astype(BF))
        data = jnp.concatenate(parts, axis=0)
        res = dot(data, w_ref[0]) + dot(data, w_ref[1])
        for n in range(STEP):
            r = step * STEP + n
            re = res[n * 72 : (n + 1) * 72, :128]
            im = res[n * 72 : (n + 1) * 72, 128:]
            c = tc_ref[pl.ds(r, 1), :]
            s = ts_ref[pl.ds(r, 1), :]
            u_re[r] = re * c + im * s
            u_im[r] = im * c - re * s
        return carry

    lax.fori_loop(0, ROWS // STEP, in_body, 0)
    lane = lax.broadcasted_iota(jnp.int32, (8, 128), 1)

    def fan_body(tile, carry):
        rows = pl.ds(pl.multiple_of(tile * 8, 8), 8)
        low = low_ref[rows, :]
        high = high_ref[rows, :]
        for n2 in range(5):
            spots = [(5 * n1 + 16 * n2) % ROWS for n1 in range(16)]
            ys = fft_list([(u_re[r, rows, :], u_im[r, rows, :]) for r in spots], -1.0)
            for k1 in range(16):
                a_re[n2 * 16 + k1] = ys[k1][0]
                a_im[n2 * 16 + k1] = ys[k1][1]
        for k1 in range(16):
            ys = fft5([(a_re[n2 * 16 + k1], a_im[n2 * 16 + k1]) for n2 in range(5)], -1.0)
            kept = []
            for k2 in range(5):
                outer = next(k for k in range(ROWS) if k % 16 == k1 and k % 5 == k2)
                if outer < ROWS // 2:
                    fold = lane + outer * 128
                else:
                    fold = (NC - outer * 128) - lane
                keep = (fold >= low) & (fold <= high)
                kept.append(tuple(jnp.where(keep, v, 0.0) for v in ys[k2]))
            ys = fft5(kept, 1.0)
            for n2 in range(5):
                a_re[n2 * 16 + k1] = ys[n2][0]
                a_im[n2 * 16 + k1] = ys[n2][1]
        for n2 in range(5):
            spots = [(5 * n1 + 16 * n2) % ROWS for n1 in range(16)]
            ys = fft_list([(a_re[n2 * 16 + k1], a_im[n2 * 16 + k1]) for k1 in range(16)], 1.0)
            for n1 in range(16):
                u_re[spots[n1], rows, :] = ys[n1][0]
                u_im[spots[n1], rows, :] = ys[n1][1]
        return carry

    lax.fori_loop(0, 9, fan_body, 0)

    def out_body(step, carry):
        highs, lows = [], []
        for n in range(STEP):
            r = step * STEP + n
            re, im = u_re[r], u_im[r]
            re = jnp.concatenate([re[:8] + re[64:], re[8:64]], axis=0)
            im = jnp.concatenate([im[:8] + im[64:], im[8:64]], axis=0)
            c = tc_ref[pl.ds(r, 1), :]
            s = ts_ref[pl.ds(r, 1), :]
            high, low = parted(jnp.concatenate([re * c - im * s, im * c + re * s], axis=1))
            highs.append(high)
            lows.append(low)
        high = jnp.concatenate(highs, axis=0)
        low = jnp.concatenate(lows, axis=0)
        res = (dot(high, v_ref[0]) + dot(low, v_ref[0]) + dot(high, v_ref[1])) * (1.0 / NC)
        for n in range(STEP):
            block = res[n * 64 : (n + 1) * 64]
            both = jnp.concatenate([block[:, :128], block[:, 128:]], axis=0)
            flat[pl.ds(step * STEP + n, 128, stride=ROWS), :] = both.T
        return carry

    lax.fori_loop(0, ROWS // STEP, out_body, 0)

    def store_body(p, carry):
        out_ref[p] = flat[pl.ds(pl.multiple_of(p * ROWS, 8), ROWS), :].astype(BF)
        return carry

    lax.fori_loop(0, 128, store_body, 0, unroll=16)


def slide_tables():
    row = np.arange(256)[:, None]
    col = np.arange(128)[None, :]
    change = (row == col + 125) * 1.0 - (row == col + 123) * 1.0
    shift = (row == col + 124) * 1.0
    nine = ((row >= col) & (row <= col + 8)) * 1.0
    nine = np.concatenate([nine[:128], nine[128:]], axis=1)
    return np.concatenate([change, shift], axis=1), np.concatenate([nine, nine], axis=0)


BAND = 128
PER = 9


def tensor_kernel(half, place_ref, *refs):
    if half == 0:
        near_ref, above_ref, below_ref, lanes_ref, nine_ref, out_ref = refs[:6]
        slope, level, prod, trio, both_ref = refs[6:]
    else:
        near_ref, above_ref, below_ref, far_ref, lanes_ref, nine_ref, _, out_ref = refs[:8]
        slope, level, prod, trio, both_ref = refs[8:]
    lane = lax.broadcasted_iota(jnp.int32, (8, 128), 1)
    sub = lax.broadcasted_iota(jnp.int32, (8, 128), 0)
    step = pl.program_id(0)
    chan, part = place_ref[0], place_ref[1]

    def column(t):
        if t in (-1, 16):
            parts = [pltpu.roll(above_ref[pl.ds(144, 16), :].astype(F32), 64, 1).astype(BF)]
            for j in range(8):
                side = near_ref[j, pl.ds(SIDE, 16), :].astype(F32)
                parts.append(side.astype(BF))
                for n in range(1, 5):
                    parts.append(pltpu.roll(side, 128 - 16 * n, 1).astype(BF))
            return jnp.concatenate(parts + [below_ref[pl.ds(144, 16), :]], axis=0)
        rows = pl.ds(16 * t if t < 9 else 160 + 16 * (t - 9), 16)
        if t < 9:
            inner = [near_ref[j, pl.ds(t * ROWS, ROWS), :] for j in range(8)]
        else:
            inner = [far_ref[:, (t - 9) * 128 : (t - 8) * 128]]
        return jnp.concatenate([above_ref[rows, :]] + inner + [below_ref[rows, :]], axis=0)

    @pl.when(step == 0)
    def _():
        left = column(8 * half - 1)
        for t in range(PER):
            right = column(8 * half + t)
            res = dot(jnp.concatenate([left, right], axis=1), lanes_ref[...])
            slope[t] = res[:, :128]
            level[t] = res[:, 128:]
            left = right

    top = pl.multiple_of(step * BAND, BAND)
    for k in range(BAND // 8 + 2):
        base = pl.multiple_of(top + k * 8, 8)
        for t in range(PER):
            grad_time = slope[t, pl.ds(base + 12, 8), :]
            masked = grad_time
            if half == 0 and t == 0:
                masked = jnp.where((lane >= 4) | (part > 0), masked, 0.0)
            if half == 1 and t == PER - 1:
                masked = jnp.where((lane < 4) | (part < 7), masked, 0.0)
            if k == 0:
                masked = jnp.where((sub >= 4) | (chan > 0) | (step > 0), masked, 0.0)
            if k == BAND // 8:
                masked = jnp.where((sub < 4) | (chan < 15) | (step < 640 // BAND - 1), masked, 0.0)
            grad_chan = level[t, pl.ds(base + 13, 8), :] - level[t, pl.ds(base + 11, 8), :]
            prod[0, t, pl.ds(k * 8, 8), :] = grad_chan * masked
            prod[1, t, pl.ds(k * 8, 8), :] = grad_time * masked
    for k in range(BAND // 8 + 1):
        for n in range(2):
            for t in range(PER):
                trio[n, t, pl.ds(k * 8, 8), :] = (
                    prod[n, t, pl.ds(k * 8, 8), :]
                    + prod[n, t, pl.ds(k * 8 + 1, 8), :]
                    + prod[n, t, pl.ds(k * 8 + 2, 8), :]
                )
    for k in range(BAND // 16):
        for n in range(2):
            for t in range(PER):
                total = (
                    trio[n, t, pl.ds(k * 16, 16), :]
                    + trio[n, t, pl.ds(k * 16 + 3, 16), :]
                    + trio[n, t, pl.ds(k * 16 + 6, 16), :]
                )
                high, low = parted(total)
                both_ref[n, t, pl.ds(k * 16, 16), :128] = high
                both_ref[n, t, pl.ds(k * 16, 16), 128:] = low
    nine = nine_ref[...]
    scale = 1.0 / 324.0
    for g in range(2):
        sums = []
        for n in range(2):
            res = dot(both_ref[n, pl.ds(g * 4, 5)].reshape(5 * BAND, 256), nine)
            sums.append(res[: 4 * BAND, :128] + res[BAND:, 128:])
        res = (sums[0] * -scale) / (sums[1] * scale + 1e-05)
        for t in range(4):
            cols = slice(g * 512 + t * 128, g * 512 + t * 128 + 128)
            out_ref[:, cols] = res[t * BAND : (t + 1) * BAND]


def call(kernel, out, specs, scratch, flops, *args, smem=0):
    nbytes = sum(a.size * a.dtype.itemsize for a in args) + 3 * 2**20
    return pl.pallas_call(
        kernel,
        out_shape=out,
        in_specs=[SMEM] * smem + [VMEM] * (len(args) - smem),
        out_specs=specs,
        scratch_shapes=scratch,
        compiler_params=pltpu.CompilerParams(vmem_limit_bytes=48 * 2**20),
        cost_estimate=pl.CostEstimate(flops=flops, bytes_accessed=nbytes, transcendentals=0),
    )(*args)


def pair(matrix):
    return jnp.asarray(np.stack(two_parts(matrix)))


def single(table):
    return jnp.asarray(table.astype(np.float32))


def forward(place, series, good, low, high, packed):
    fwd, _, first, _, tc, ts = time_tables()
    scratch = [
        pltpu.VMEM((16, 8, 16, 128), F32),
        pltpu.VMEM((64 * ROWS, 256), BF),
        pltpu.VMEM((64 * ROWS, 256), BF),
    ]
    out = jax.ShapeDtypeStruct((128, ROWS, 128), BF)
    tables = single(tc), single(ts), pair(fwd), pair(first)
    return call(
        forward_kernel,
        out,
        VMEM,
        scratch,
        4 * 10**9,
        place,
        series,
        good,
        low,
        high,
        packed,
        *tables,
        smem=1,
    )


def backward(place, spectra):
    _, bwd, _, last, tc, ts = time_tables()
    scratch = [pltpu.VMEM((16, 8, 16, 128), F32), pltpu.VMEM((64 * ROWS, 256), F32)]
    out = [jax.ShapeDtypeStruct(s, BF) for s in ((8, NEAR, 128), (8, ROWS, FAR))]
    tables = single(tc), single(ts), pair(bwd), pair(last)
    return call(
        backward_kernel, out, [VMEM, VMEM], scratch, 4 * 10**9, place, spectra, *tables, smem=1
    )


def channels(pencil, low, high, packed):
    fwd, bwd, tc, ts = chan_tables()
    scratch = [
        pltpu.VMEM((128 * ROWS, 128), F32),
        pltpu.VMEM((ROWS, 72, 128), F32),
        pltpu.VMEM((ROWS, 72, 128), F32),
        pltpu.VMEM((ROWS, 8, 128), F32),
        pltpu.VMEM((ROWS, 8, 128), F32),
    ]
    out = jax.ShapeDtypeStruct((128, ROWS, 128), BF)
    tables = single(tc), single(ts), pair(fwd), pair(bwd)
    return call(channel_kernel, out, VMEM, scratch, 8 * 10**9, pencil, low, high, packed, *tables)


def tensor(half, place, near, above, below, far=None, whole=None):
    lanes, nine = (jnp.asarray(t.astype(ml_dtypes.bfloat16)) for t in slide_tables())
    scratch = [
        pltpu.VMEM((PER, 672, 128), F32),
        pltpu.VMEM((PER, 672, 128), F32),
        pltpu.VMEM((2, PER, BAND + 16, 128), F32),
        pltpu.VMEM((2, PER, BAND + 16, 128), F32),
        pltpu.VMEM((2, PER, BAND, 256), BF),
    ]
    if half == 0:
        args = (place, near, above, below, lanes, nine)
        specs, alias = [SMEM] + [VMEM] * 5, {}
    else:
        args = (place, near, above, below, far, lanes, nine, whole)
        specs, alias = [SMEM] + [VMEM] * 6 + [ANY], {7: 0}
    return pl.pallas_call(
        functools.partial(tensor_kernel, half),
        grid=(640 // BAND,),
        out_shape=jax.ShapeDtypeStruct((640, 2048), F32),
        in_specs=specs,
        out_specs=pl.BlockSpec((BAND, 1024), lambda g: (g, half)),
        scratch_shapes=scratch,
        input_output_aliases=alias,
        compiler_params=pltpu.CompilerParams(vmem_limit_bytes=40 * 2**20),
        cost_estimate=pl.CostEstimate(flops=10**9, bytes_accessed=9 * 2**20, transcendentals=0),
    )(*args)


def window_bounds(fan_bounds, block):
    column = []
    for slot, k in enumerate(WAVES):
        column += [0, 64] if slot == 0 else [k, 128 - k]
    pick = jnp.asarray(np.array(column, np.int32))[block]
    table = fan_bounds[:, : NT // 2].reshape(2, 64, 128)
    mine = lax.dynamic_slice(table, (0, 0, pick), (2, 64, 1))
    top = jnp.broadcast_to(fan_bounds[:, NT // 2].reshape(2, 1, 1), (2, 8, 1))
    both = jnp.broadcast_to(jnp.concatenate([mine, top], axis=1), (2, 72, 128))
    return both[0], both[1]


def after_kernel(value_ref, sign_ref, out_ref):
    pass


def after(value, sign):
    return pl.pallas_call(
        after_kernel,
        out_shape=jax.ShapeDtypeStruct(value.shape, value.dtype),
        in_specs=[ANY, ANY],
        out_specs=ANY,
        input_output_aliases={0: 0},
        cost_estimate=pl.CostEstimate(flops=0, bytes_accessed=0, transcendentals=0),
    )(value, sign)


def outer_kernel(near_ref, top_ref, bottom_ref):
    for ref, source, first in ((top_ref, 0, 0), (bottom_ref, 7, 64)):
        for t in range(9):
            ref[pl.ds(16 * t, 16), :] = near_ref[source, pl.ds(t * ROWS + first, 16), :]
        ref[pl.ds(144, 128), :] = near_ref[source, pl.ds(SIDE, 128), :]


def per_device(record, channel_ok, fan_bounds):
    chan, part = lax.axis_index("chan"), lax.axis_index("tm")
    block = chan * 8 + part
    place = jnp.stack([chan, part]).astype(jnp.int32)
    series = lax.all_to_all(record.reshape(8, ROWS, 2048), "tm", 0, 0, tiled=True)
    good = lax.dynamic_slice(channel_ok, (part * ROWS,), (ROWS,)).astype(F32)
    good = jnp.broadcast_to(good[:, None], (ROWS, 128))
    low, high = window_bounds(fan_bounds, block)
    corner = lax.broadcasted_iota(jnp.int32, (8, 128), 0) == 0
    packed = (corner & (block == 0)).astype(F32)
    spectra = forward(place, series, good, low, high, packed)
    pencil = lax.all_to_all(spectra, ("chan", "tm"), 0, 0, tiled=True)
    passed = channels(pencil, low, high, packed)
    back = lax.all_to_all(passed, ("chan", "tm"), 0, 0, tiled=True)
    near, far = backward(place, back)
    near = lax.all_to_all(near, "tm", 0, 0, tiled=True)
    down = [(i, i + 1) for i in range(15)]
    outer = jax.ShapeDtypeStruct((272, 128), BF)
    top, bottom = call(outer_kernel, [outer, outer], [VMEM, VMEM], [], 10**6, near)
    above = lax.ppermute(bottom, "chan", down)
    below = lax.ppermute(top, "chan", [(b, a) for a, b in down])
    whole = tensor(0, place, near, above, below)
    far = lax.all_to_all(after(far, near), "tm", 0, 0, tiled=True).reshape(640, FAR)
    return tensor(1, place, near, above, below, far, whole)


def solution(mesh):
    in_specs = (P("chan", "tm"), P("chan"), P())
    out_specs = P("chan", "tm")
    return jax.shard_map(
        per_device, mesh=mesh, in_specs=in_specs, out_specs=out_specs, check_vma=False
    )
```

```python
import functools
import math

import jax
import jax.numpy as jnp
import ml_dtypes
import numpy as np
from jax import lax
from jax.experimental import pallas as pl
from jax.experimental.pallas import tpu as pltpu
from jax.sharding import PartitionSpec as P

NC = 10240
NT = 16384
ROWS = 80
TF = 128
R = 4
GROUP = 63
SIDE = 9 * ROWS
OUTER = SIDE + 16
NEAR = OUTER + 7 * 16
FAR = 896
BF = jnp.bfloat16
F32 = jnp.float32
VMEM = pl.BlockSpec(memory_space=pltpu.VMEM)
SMEM = pl.BlockSpec(memory_space=pltpu.SMEM)
ANY = pl.BlockSpec(memory_space=pl.ANY)

WAVES = [0] + [8 * n for n in range(1, 8)] + [4 + 8 * n for n in range(8)]
WAVES += [q + 8 * n for q in (1, 2, 3) for n in range(16)]


def two_parts(matrix):
    high = matrix.astype(ml_dtypes.bfloat16)
    low = (matrix - high.astype(np.float64)).astype(ml_dtypes.bfloat16)
    return high, low


def turn(numbers, length):
    angle = (numbers % length) * (2.0 * np.pi / length)
    return np.cos(angle), np.sin(angle)


def time_tables():
    n = np.arange(128)[:, None]
    j = np.concatenate([np.arange(64), 127 - np.arange(64)])[None, :]
    cos, sin = turn(n * j, 128)

    def halves(re, im):
        return np.concatenate([re[:, :64], im[:, :64], re[:, 64:], im[:, 64:]], axis=1)

    forward = np.concatenate([halves(cos, -sin), halves(sin, cos)], axis=0)
    backward = np.concatenate(
        [halves(cos, -sin).T, halves(sin, cos).T], axis=1
    ) / NT
    jj = np.arange(64)[None, :]
    c0, s0 = turn(n * 128 * jj, NT)
    c1, s1 = turn(n * (64 + 128 * jj), NT)
    zero = np.zeros((128, 128))
    even = np.concatenate([c0, -s0], axis=1)
    even[:, 64] = 1.0 - 2.0 * (np.arange(128) % 2)
    odd = np.concatenate([c1, -s1], axis=1)
    first = np.concatenate(
        [np.concatenate([even, zero], axis=1), np.concatenate([zero, odd], axis=1)], axis=0
    )
    weight = np.full(256, 2.0)
    weight[0] = 1.0
    weight[64] = 1.0
    last = (first * weight[None, :]).T / NT
    k = np.array(WAVES)[:, None]
    tw_cos, tw_sin = turn(k * np.arange(128)[None, :], NT)
    return forward, backward, first, last, tw_cos, tw_sin


def chan_tables():
    cos, sin = turn(np.arange(128)[:, None] * np.arange(128)[None, :], 128)
    forward = np.block([[cos, -sin], [sin, cos]])
    backward = np.block([[cos, sin], [-sin, cos]])
    tw_cos, tw_sin = turn(np.arange(ROWS)[:, None] * np.arange(128)[None, :], NC)
    return forward, backward, tw_cos, tw_sin


def plus(a, b):
    if a is None:
        return b
    if b is None:
        return a
    return a + b


def minus(a, b):
    if b is None:
        return a
    if a is None:
        return -b
    return a - b


def times(value, number):
    if value is None or number == 0.0:
        return None
    if number == 1.0:
        return value
    if number == -1.0:
        return -value
    return value * number


def cadd(x, y):
    return plus(x[0], y[0]), plus(x[1], y[1])


def csub(x, y):
    return minus(x[0], y[0]), minus(x[1], y[1])


def spun(x, step, length, sign):
    step = step % length
    if 4 * step % length == 0:
        quarter = 4 * step // length
        c = (1.0, 0.0, -1.0, 0.0)[quarter]
        s = (0.0, 1.0, 0.0, -1.0)[quarter]
    else:
        c = math.cos(2.0 * math.pi * step / length)
        s = math.sin(2.0 * math.pi * step / length)
    s = sign * s
    re, im = x
    if 8 * step % length == 0 and 4 * step % length != 0 and re is not None and im is not None:
        a = abs(c)
        u = re if c > 0 else -re
        v = im if c > 0 else -im
        if c * s > 0:
            return (u - v) * a, (v + u) * a
        return (u + v) * a, (v - u) * a
    return minus(times(re, c), times(im, s)), plus(times(im, c), times(re, s))


def fft_list(xs, sign):
    count = len(xs)
    if count == 1:
        return xs
    even = fft_list(xs[0::2], sign)
    odd = fft_list(xs[1::2], sign)
    head, tail = [], []
    for k in range(count // 2):
        t = spun(odd[k], k, count, sign)
        head.append(cadd(even[k], t))
        tail.append(csub(even[k], t))
    return head + tail


def rfft_list(xs):
    count = len(xs)
    if count == 2:
        return [(xs[0] + xs[1], None), (xs[0] - xs[1], None)]
    even = rfft_list(xs[0::2])
    odd = rfft_list(xs[1::2])
    out = [None] * (count // 2 + 1)
    for k in range(count // 4 + 1):
        t = spun(odd[k], k, count, -1.0)
        out[k] = cadd(even[k], t)
        if k < count // 4:
            re, im = csub(even[k], t)
            out[count // 2 - k] = (re, minus(None, im) if im is not None else None)
    return out


def irfft_list(ys):
    half = len(ys) - 1
    count = 2 * half
    if count == 2:
        return [ys[0][0] + ys[1][0], ys[0][0] - ys[1][0]]
    evens, odds = [], []
    for k in range(count // 4 + 1):
        mirror = (ys[half - k][0], minus(None, ys[half - k][1]) if ys[half - k][1] is not None else None)
        if 2 * k == half:
            evens.append((ys[k][0] * 2.0, None))
            re, _ = spun(ys[k], k, count, 1.0)
            odds.append((re * 2.0, None))
        else:
            both = cadd(ys[k], mirror)
            gap = spun(csub(ys[k], mirror), k, count, 1.0)
            if half == 1 and k == 0:
                both = (both[0], None)
                gap = (gap[0], None)
            evens.append(both)
            odds.append(gap)
    even = irfft_list(evens)
    odd = irfft_list(odds)
    out = []
    for e, o in zip(even, odd):
        out += [e, o]
    return out


def fft5(xs, sign):
    c1, c2 = math.cos(2 * math.pi / 5), math.cos(4 * math.pi / 5)
    s1, s2 = math.sin(2 * math.pi / 5), math.sin(4 * math.pi / 5)
    out = [[None, None] for _ in range(5)]
    pairs = []
    for part in range(2):
        x = [v[part] for v in xs]
        t1, t2, t3, t4 = x[1] + x[4], x[2] + x[3], x[1] - x[4], x[2] - x[3]
        out[0][part] = x[0] + t1 + t2
        pairs.append(
            (
                x[0] + c1 * t1 + c2 * t2,
                x[0] + c2 * t1 + c1 * t2,
                s1 * t3 + s2 * t4,
                s2 * t3 - s1 * t4,
            )
        )
    (ra, rb, rc, rd), (ia, ib, ic, idd) = pairs
    if sign > 0:
        out[1] = [ra - ic, ia + rc]
        out[4] = [ra + ic, ia - rc]
        out[2] = [rb - idd, ib + rd]
        out[3] = [rb + idd, ib - rd]
    else:
        out[1] = [ra + ic, ia - rc]
        out[4] = [ra - ic, ia + rc]
        out[2] = [rb + idd, ib - rd]
        out[3] = [rb - idd, ib + rd]
    return [tuple(v) for v in out]


def dot(a, b):
    return lax.dot_general(a, b, (((1,), (0,)), ((), ())), preferred_element_type=F32)


def parted(value):
    high = value.astype(BF)
    low = (value - high.astype(F32)).astype(BF)
    return high, low


def forward_kernel(
    place_ref, x_ref, ok_ref, low_ref, high_ref, packed_ref, tc_ref, ts_ref, w_ref, w0_ref, out_ref,
    stage, hi_ref, lo_ref
):
    def tile_body(tile, carry):
        rows = pl.ds(pl.multiple_of(tile * 16, 16), 16)
        good = ok_ref[rows, :]
        for a in range(16):
            xs = [x_ref[s, rows, a * 128 : (a + 1) * 128].astype(F32) * good for s in range(8)]
            ys = rfft_list(xs)
            stage[a, 0] = ys[0][0]
            for q in (1, 2, 3):
                re, im = spun(ys[q], a * q, 128, -1.0)
                stage[a, 2 * q] = re
                stage[a, 2 * q + 1] = im
            stage[a, 1] = ys[4][0]

        def put(slot, re, im):
            base = pl.ds(pl.multiple_of(slot * ROWS + tile * 16, 16), 16)
            for part, value in enumerate((re, im)):
                high, low = parted(value)
                hi_ref[base, part * 128 : (part + 1) * 128] = high
                lo_ref[base, part * 128 : (part + 1) * 128] = low

        def twist(slot, value):
            re, im = value
            c = tc_ref[slot : slot + 1, :]
            s = ts_ref[slot : slot + 1, :]
            put(slot, re * c + im * s, im * c - re * s)

        ys = rfft_list([stage[a, 0] for a in range(16)])
        put(0, ys[0][0], ys[8][0])
        for n in range(1, 8):
            twist(n, ys[n])
        ys = fft_list([spun((stage[a, 1], None), a, 32, -1.0) for a in range(16)], -1.0)
        for n in range(8):
            twist(8 + n, ys[n])
        for q in (1, 2, 3):
            ys = fft_list([(stage[a, 2 * q], stage[a, 2 * q + 1]) for a in range(16)], -1.0)
            for n in range(16):
                twist(16 * q + n, ys[n])
        return carry

    lax.fori_loop(0, 5, tile_body, 0, unroll=5)

    def mixed(rows, w):
        high, low = hi_ref[rows, :], lo_ref[rows, :]
        return dot(high, w[0]) + dot(low, w[0]) + dot(high, w[1])

    first = mixed(pl.ds(0, ROWS), w0_ref).astype(BF)
    out_ref[0] = first[:, :128]
    out_ref[1] = first[:, 128:]

    def wave_body(step, carry):
        res = mixed(pl.ds(pl.multiple_of(ROWS + step * GROUP * ROWS, 16), GROUP * ROWS), w_ref).astype(BF)
        for n in range(GROUP):
            out_ref[2 + 2 * GROUP * step + 2 * n] = res[n * ROWS : (n + 1) * ROWS, :128]
            out_ref[3 + 2 * GROUP * step + 2 * n] = res[n * ROWS : (n + 1) * ROWS, 128:]
        return carry

    lax.fori_loop(0, 63 // GROUP, wave_body, 0)


def backward_kernel(
    place_ref, in_ref, tc_ref, ts_ref, w_ref, w0_ref, near_ref, far_ref, stage, mid_ref
):
    def joined(slot):
        return jnp.concatenate([in_ref[2 * slot], in_ref[2 * slot + 1]], axis=1)

    first = joined(0)
    mid_ref[pl.ds(0, ROWS), :] = dot(first, w0_ref[0]) + dot(first, w0_ref[1])

    def wave_body(step, carry):
        data = jnp.concatenate([joined(1 + step * GROUP + n) for n in range(GROUP)], axis=0)
        mid_ref[pl.ds(pl.multiple_of(ROWS + step * GROUP * ROWS, 16), GROUP * ROWS), :] = dot(
            data, w_ref[0]
        ) + dot(data, w_ref[1])
        return carry

    lax.fori_loop(0, 63 // GROUP, wave_body, 0)
    lane = lax.broadcasted_iota(jnp.int32, (16, 128), 1)

    sides = [jnp.zeros((16, 128), F32) for _ in range(8)]
    for tile in range(5):

        def get(slot):
            base = pl.ds(slot * ROWS + tile * 16, 16)
            return mid_ref[base, :128], mid_ref[base, 128:]

        def twisted(slot):
            re, im = get(slot)
            c = tc_ref[slot : slot + 1, :]
            s = ts_ref[slot : slot + 1, :]
            return re * c - im * s, im * c + re * s

        mean, top = get(0)
        ys = irfft_list([(mean, None)] + [twisted(n) for n in range(1, 8)] + [(top, None)])
        for a in range(16):
            stage[a, 0] = ys[a]
        ys = fft_list([twisted(8 + n) for n in range(8)] + [(None, None)] * 8, 1.0)
        for a in range(16):
            stage[a, 1] = 2.0 * spun(ys[a], a, 32, 1.0)[0]
        for q in (1, 2, 3):
            ys = fft_list([twisted(16 * q + n) for n in range(16)], 1.0)
            for a in range(16):
                re, im = spun(ys[a], a * q, 128, 1.0)
                stage[a, 2 * q] = re
                stage[a, 2 * q + 1] = im
        rows = pl.ds(tile * 16, 16)

        def series(a):
            parts = [(stage[a, 0], None)]
            parts += [(stage[a, 2 * q], stage[a, 2 * q + 1]) for q in (1, 2, 3)]
            return [y.astype(BF) for y in irfft_list(parts + [(stage[a, 1], None)])]

        ends = {}
        for a in range(16):
            ys = series(a)
            for s in range(8):
                if a < 9:
                    near_ref[s, pl.ds(a * ROWS + tile * 16, 16), :] = ys[s]
                else:
                    far_ref[s, rows, (a - 9) * 128 : (a - 8) * 128] = ys[s]
            if a in (0, 15):
                ends[a] = ys
        blank = jnp.zeros((16, 128), BF)
        for s in range(8):
            after = ends[0][s + 1] if s < 7 else blank
            before = ends[15][s - 1] if s > 0 else blank
            both = jnp.where(lane < 64, after.astype(F32), before.astype(F32))
            here = ((lane - 16 * tile + 5) & 127) < 10
            sides[s] = jnp.where(here, pltpu.roll(both, 16 * tile, 1), sides[s])
    base = pl.multiple_of(jnp.where(place_ref[1] == 7, 64, 0), 16)
    for s in range(8):
        near_ref[s, pl.ds(SIDE, 16), :] = sides[s].astype(BF)
        for n in range(7):
            near_ref[s, pl.ds(OUTER + 16 * n, 16), :] = far_ref[
                s, pl.ds(base, 16), n * 128 : (n + 1) * 128
            ]


STEP = 40


def channel_kernel(
    in_ref, low_ref, high_ref, first_ref, tc_ref, ts_ref, w_ref, v_ref, out_ref,
    flat, u_re, u_im, a_re, a_im
):
    def load_body(p, carry):
        flat[pl.ds(pl.multiple_of(p * ROWS, 8), ROWS), :] = in_ref[p].astype(F32)
        return carry

    lax.fori_loop(0, 128, load_body, 0, unroll=16)
    packed = first_ref[...]
    blank = jnp.zeros((8, 128), F32)

    def in_body(step, carry):
        parts = []
        for n in range(STEP):
            turned = flat[pl.ds(step * STEP + n, 128, stride=ROWS), :].T
            re, im = turned[:64], turned[64:]
            im = jnp.concatenate([im[:8] * (1.0 - packed), im[8:], im[:8] * packed], axis=0)
            re = jnp.concatenate([re, blank], axis=0)
            parts.append(jnp.concatenate([re, im], axis=1).astype(BF))
        data = jnp.concatenate(parts, axis=0)
        res = dot(data, w_ref[0]) + dot(data, w_ref[1])
        for n in range(STEP):
            r = step * STEP + n
            re = res[n * 72 : (n + 1) * 72, :128]
            im = res[n * 72 : (n + 1) * 72, 128:]
            c = tc_ref[pl.ds(r, 1), :]
            s = ts_ref[pl.ds(r, 1), :]
            u_re[r] = re * c + im * s
            u_im[r] = im * c - re * s
        return carry

    lax.fori_loop(0, ROWS // STEP, in_body, 0)
    lane = lax.broadcasted_iota(jnp.int32, (8, 128), 1)

    def fan_body(tile, carry):
        rows = pl.ds(pl.multiple_of(tile * 8, 8), 8)
        low = low_ref[rows, :]
        high = high_ref[rows, :]
        for n2 in range(5):
            spots = [(5 * n1 + 16 * n2) % ROWS for n1 in range(16)]
            ys = fft_list([(u_re[r, rows, :], u_im[r, rows, :]) for r in spots], -1.0)
            for k1 in range(16):
                a_re[n2 * 16 + k1] = ys[k1][0]
                a_im[n2 * 16 + k1] = ys[k1][1]
        for k1 in range(16):
            ys = fft5([(a_re[n2 * 16 + k1], a_im[n2 * 16 + k1]) for n2 in range(5)], -1.0)
            kept = []
            for k2 in range(5):
                outer = next(k for k in range(ROWS) if k % 16 == k1 and k % 5 == k2)
                if outer < ROWS // 2:
                    fold = lane + outer * 128
                else:
                    fold = (NC - outer * 128) - lane
                keep = (fold >= low) & (fold <= high)
                kept.append(tuple(jnp.where(keep, v, 0.0) for v in ys[k2]))
            ys = fft5(kept, 1.0)
            for n2 in range(5):
                a_re[n2 * 16 + k1] = ys[n2][0]
                a_im[n2 * 16 + k1] = ys[n2][1]
        for n2 in range(5):
            spots = [(5 * n1 + 16 * n2) % ROWS for n1 in range(16)]
            ys = fft_list([(a_re[n2 * 16 + k1], a_im[n2 * 16 + k1]) for k1 in range(16)], 1.0)
            for n1 in range(16):
                u_re[spots[n1], rows, :] = ys[n1][0]
                u_im[spots[n1], rows, :] = ys[n1][1]
        return carry

    lax.fori_loop(0, 9, fan_body, 0)

    def out_body(step, carry):
        highs, lows = [], []
        for n in range(STEP):
            r = step * STEP + n
            re, im = u_re[r], u_im[r]
            re = jnp.concatenate([re[:8] + re[64:], re[8:64]], axis=0)
            im = jnp.concatenate([im[:8] + im[64:], im[8:64]], axis=0)
            c = tc_ref[pl.ds(r, 1), :]
            s = ts_ref[pl.ds(r, 1), :]
            high, low = parted(jnp.concatenate([re * c - im * s, im * c + re * s], axis=1))
            highs.append(high)
            lows.append(low)
        high = jnp.concatenate(highs, axis=0)
        low = jnp.concatenate(lows, axis=0)
        res = (dot(high, v_ref[0]) + dot(low, v_ref[0]) + dot(high, v_ref[1])) * (1.0 / NC)
        for n in range(STEP):
            block = res[n * 64 : (n + 1) * 64]
            both = jnp.concatenate([block[:, :128], block[:, 128:]], axis=0)
            flat[pl.ds(step * STEP + n, 128, stride=ROWS), :] = both.T
        return carry

    lax.fori_loop(0, ROWS // STEP, out_body, 0)

    def store_body(p, carry):
        out_ref[p] = flat[pl.ds(pl.multiple_of(p * ROWS, 8), ROWS), :].astype(BF)
        return carry

    lax.fori_loop(0, 128, store_body, 0, unroll=16)


def slide_tables():
    row = np.arange(256)[:, None]
    col = np.arange(128)[None, :]
    change = (row == col + 125) * 1.0 - (row == col + 123) * 1.0
    shift = (row == col + 124) * 1.0
    nine = ((row >= col) & (row <= col + 8)) * 1.0
    nine = np.concatenate([nine[:128], nine[128:]], axis=1)
    return np.concatenate([change, shift], axis=1), np.concatenate([nine, nine], axis=0)


BAND = 128
PER = 9


def tensor_kernel(half, place_ref, *refs):
    if half == 0:
        near_ref, lanes_ref, nine_ref, out_ref = refs[:4]
        slope, level, prod, trio, both_ref = refs[4:]
    else:
        near_ref, above_ref, below_ref, far_ref, lanes_ref, nine_ref, _, out_ref = refs[:8]
        slope, level, prod, trio, both_ref = refs[8:]
    lane = lax.broadcasted_iota(jnp.int32, (8, 128), 1)
    sub = lax.broadcasted_iota(jnp.int32, (8, 128), 0)
    step = pl.program_id(0)
    chan, part = place_ref[0], place_ref[1]

    def column(t):
        if t in (-1, 16):
            parts = []
            for j in range(8):
                side = near_ref[j, pl.ds(SIDE, 16), :].astype(F32)
                parts.append(side.astype(BF))
                for n in range(1, 5):
                    parts.append(pltpu.roll(side, 128 - 16 * n, 1).astype(BF))
            if half == 1:
                first = pltpu.roll(above_ref[pl.ds(144, 16), :].astype(F32), 64, 1).astype(BF)
                parts = [first] + parts + [below_ref[pl.ds(144, 16), :]]
            return jnp.concatenate(parts, axis=0)
        rows = pl.ds(16 * t if t < 9 else 160 + 16 * (t - 9), 16)
        if t < 9:
            inner = [near_ref[j, pl.ds(t * ROWS, ROWS), :] for j in range(8)]
        else:
            inner = [far_ref[:, (t - 9) * 128 : (t - 8) * 128]]
        if half == 1:
            inner = [above_ref[rows, :]] + inner + [below_ref[rows, :]]
        return jnp.concatenate(inner, axis=0)

    @pl.when(step == 0)
    def _():
        left = column(8 * half - 1)
        for t in range(PER):
            right = column(8 * half + t)
            res = dot(jnp.concatenate([left, right], axis=1), lanes_ref[...])
            rows = pl.ds(16 - 16 * half, 640 + 32 * half)
            slope[t, rows, :] = res[:, :128]
            level[t, rows, :] = res[:, 128:]
            left = right

    top = pl.multiple_of(step * BAND, BAND)
    for k in range(BAND // 8 + 2):
        base = pl.multiple_of(top + k * 8, 8)
        for t in range(PER):
            grad_time = slope[t, pl.ds(base + 12, 8), :]
            masked = grad_time
            if half == 0 and t == 0:
                masked = jnp.where((lane >= 4) | (part > 0), masked, 0.0)
            if half == 1 and t == PER - 1:
                masked = jnp.where((lane < 4) | (part < 7), masked, 0.0)
            if half == 1 and k == 0:
                masked = jnp.where((sub >= 4) | (chan > 0) | (step > 0), masked, 0.0)
            if half == 1 and k == BAND // 8:
                masked = jnp.where((sub < 4) | (chan < 15) | (step < 640 // BAND - 1), masked, 0.0)
            grad_chan = level[t, pl.ds(base + 13, 8), :] - level[t, pl.ds(base + 11, 8), :]
            prod[0, t, pl.ds(k * 8, 8), :] = grad_chan * masked
            prod[1, t, pl.ds(k * 8, 8), :] = grad_time * masked
    for k in range(BAND // 8 + 1):
        for n in range(2):
            for t in range(PER):
                trio[n, t, pl.ds(k * 8, 8), :] = (
                    prod[n, t, pl.ds(k * 8, 8), :]
                    + prod[n, t, pl.ds(k * 8 + 1, 8), :]
                    + prod[n, t, pl.ds(k * 8 + 2, 8), :]
                )
    for k in range(BAND // 16):
        for n in range(2):
            for t in range(PER):
                total = (
                    trio[n, t, pl.ds(k * 16, 16), :]
                    + trio[n, t, pl.ds(k * 16 + 3, 16), :]
                    + trio[n, t, pl.ds(k * 16 + 6, 16), :]
                )
                high, low = parted(total)
                both_ref[n, t, pl.ds(k * 16, 16), :128] = high
                both_ref[n, t, pl.ds(k * 16, 16), 128:] = low
    nine = nine_ref[...]
    scale = 1.0 / 324.0
    for g in range(2):
        sums = []
        for n in range(2):
            res = dot(both_ref[n, pl.ds(g * 4, 5)].reshape(5 * BAND, 256), nine)
            sums.append(res[: 4 * BAND, :128] + res[BAND:, 128:])
        res = (sums[0] * -scale) / (sums[1] * scale + 1e-05)
        for t in range(4):
            cols = slice(g * 512 + t * 128, g * 512 + t * 128 + 128)
            out_ref[:, cols] = res[t * BAND : (t + 1) * BAND]


def ahead(parts, count, lane):
    turned = [pltpu.roll(v, (-count) % 128, 1) for v in parts]
    out = []
    for t in range(len(parts)):
        if count > 0:
            other = turned[min(t + 1, len(parts) - 1)]
            out.append(jnp.where(lane < 128 - count, turned[t], other))
        else:
            other = turned[max(t - 1, 0)]
            out.append(jnp.where(lane < -count, other, turned[t]))
    return out


def edge_kernel(place_ref, above_ref, top_ref, bottom_ref, below_ref, _, out_ref, wide, prod):
    lane = lax.broadcasted_iota(jnp.int32, (8, 128), 1)
    sub = lax.broadcasted_iota(jnp.int32, (8, 128), 0)
    step = pl.program_id(0)
    chan, part = place_ref[0], place_ref[1]

    def spread(start, ref, turned):
        rows = pl.ds(start, 16)
        wide[0, rows, :] = pltpu.roll(ref[pl.ds(144, 16), :].astype(F32), turned, 1)
        for t in range(9):
            wide[t + 1, rows, :] = ref[pl.ds(16 * t, 16), :].astype(F32)

    @pl.when(step == 0)
    def _():
        spread(0, above_ref, 64)
        spread(16, top_ref, 0)

    @pl.when(step == 1)
    def _():
        spread(0, bottom_ref, 64)
        spread(16, below_ref, 0)

    skip = pl.multiple_of(8 - step * 8, 8)
    for k in range(2):
        first = skip + k * 8 + 4
        row = sub + first
        keep = ((row >= 16) | (step == 1) | (chan > 0)) & ((row < 16) | (step == 0) | (chan < 15))
        here = [wide[t, pl.ds(first, 8), :] for t in range(10)]
        right, left = ahead(here, 1, lane), ahead(here, -1, lane)
        for t in range(10):
            grad_time = right[t] - left[t]
            masked = jnp.where(keep, grad_time, 0.0)
            if t == 0:
                masked = jnp.where(part > 0, masked, 0.0)
            grad_chan = wide[t, pl.ds(first + 1, 8), :] - wide[t, pl.ds(first - 1, 8), :]
            prod[0, t, pl.ds(k * 8, 8), :] = grad_chan * masked
            prod[1, t, pl.ds(k * 8, 8), :] = grad_time * masked
    sums = []
    for n in range(2):
        parts = []
        for t in range(10):
            total = prod[n, t, pl.ds(0, 8), :]
            for d in range(1, 9):
                total = total + prod[n, t, pl.ds(d, 8), :]
            parts.append(total)
        near, far = ahead(parts, 1, lane), ahead(parts, -1, lane)
        three = [v + a + b for v, a, b in zip(parts, near, far)]
        near, far = ahead(three, 3, lane), ahead(three, -3, lane)
        sums.append([v + a + b for v, a, b in zip(three, near, far)][1:9])
    scale = 1.0 / 324.0
    out = [(c * -scale) / (a * scale + 1e-05) for c, a in zip(*sums)]
    out_ref[...] = jnp.concatenate(out, axis=1)


def call(kernel, out, specs, scratch, flops, *args, smem=0):
    nbytes = sum(a.size * a.dtype.itemsize for a in args) + 3 * 2**20
    return pl.pallas_call(
        kernel,
        out_shape=out,
        in_specs=[SMEM] * smem + [VMEM] * (len(args) - smem),
        out_specs=specs,
        scratch_shapes=scratch,
        compiler_params=pltpu.CompilerParams(vmem_limit_bytes=48 * 2**20),
        cost_estimate=pl.CostEstimate(flops=flops, bytes_accessed=nbytes, transcendentals=0),
    )(*args)


def pair(matrix):
    return jnp.asarray(np.stack(two_parts(matrix)))


def single(table):
    return jnp.asarray(table.astype(np.float32))


def forward(place, series, good, low, high, packed):
    fwd, _, first, _, tc, ts = time_tables()
    scratch = [
        pltpu.VMEM((16, 8, 16, 128), F32),
        pltpu.VMEM((64 * ROWS, 256), BF),
        pltpu.VMEM((64 * ROWS, 256), BF),
    ]
    out = jax.ShapeDtypeStruct((128, ROWS, 128), BF)
    tables = single(tc), single(ts), pair(fwd), pair(first)
    return call(
        forward_kernel,
        out,
        VMEM,
        scratch,
        4 * 10**9,
        place,
        series,
        good,
        low,
        high,
        packed,
        *tables,
        smem=1,
    )


def backward(place, spectra):
    _, bwd, _, last, tc, ts = time_tables()
    scratch = [pltpu.VMEM((16, 8, 16, 128), F32), pltpu.VMEM((64 * ROWS, 256), F32)]
    out = [jax.ShapeDtypeStruct(s, BF) for s in ((8, NEAR, 128), (8, ROWS, FAR))]
    tables = single(tc), single(ts), pair(bwd), pair(last)
    return call(
        backward_kernel, out, [VMEM, VMEM], scratch, 4 * 10**9, place, spectra, *tables, smem=1
    )


def channels(pencil, low, high, packed):
    fwd, bwd, tc, ts = chan_tables()
    scratch = [
        pltpu.VMEM((128 * ROWS, 128), F32),
        pltpu.VMEM((ROWS, 72, 128), F32),
        pltpu.VMEM((ROWS, 72, 128), F32),
        pltpu.VMEM((ROWS, 8, 128), F32),
        pltpu.VMEM((ROWS, 8, 128), F32),
    ]
    out = jax.ShapeDtypeStruct((128, ROWS, 128), BF)
    tables = single(tc), single(ts), pair(fwd), pair(bwd)
    return call(channel_kernel, out, VMEM, scratch, 8 * 10**9, pencil, low, high, packed, *tables)


def tensor(half, place, near, above=None, below=None, far=None, whole=None):
    lanes, nine = (jnp.asarray(t.astype(ml_dtypes.bfloat16)) for t in slide_tables())
    scratch = [
        pltpu.VMEM((PER, 672, 128), F32),
        pltpu.VMEM((PER, 672, 128), F32),
        pltpu.VMEM((2, PER, BAND + 16, 128), F32),
        pltpu.VMEM((2, PER, BAND + 16, 128), F32),
        pltpu.VMEM((2, PER, BAND, 256), BF),
    ]
    if half == 0:
        args = (place, near, lanes, nine)
        specs, alias = [SMEM] + [VMEM] * 3, {}
    else:
        args = (place, near, above, below, far, lanes, nine, whole)
        specs, alias = [SMEM] + [VMEM] * 6 + [ANY], {7: 0}
    return pl.pallas_call(
        functools.partial(tensor_kernel, half),
        grid=(640 // BAND,),
        out_shape=jax.ShapeDtypeStruct((640, 2048), F32),
        in_specs=specs,
        out_specs=pl.BlockSpec((BAND, 1024), lambda g: (g, half)),
        scratch_shapes=scratch,
        input_output_aliases=alias,
        compiler_params=pltpu.CompilerParams(vmem_limit_bytes=40 * 2**20),
        cost_estimate=pl.CostEstimate(flops=10**9, bytes_accessed=9 * 2**20, transcendentals=0),
    )(*args)


def edges(place, above, top, bottom, below, whole):
    return pl.pallas_call(
        edge_kernel,
        grid=(2,),
        out_shape=jax.ShapeDtypeStruct((640, 2048), F32),
        in_specs=[SMEM] + [VMEM] * 4 + [ANY],
        out_specs=pl.BlockSpec((8, 1024), lambda g: (79 * g, 0)),
        scratch_shapes=[pltpu.VMEM((10, 32, 128), F32), pltpu.VMEM((2, 10, 16, 128), F32)],
        input_output_aliases={5: 0},
        compiler_params=pltpu.CompilerParams(vmem_limit_bytes=16 * 2**20),
        cost_estimate=pl.CostEstimate(flops=10**7, bytes_accessed=2**19, transcendentals=0),
    )(place, above, top, bottom, below, whole)


def window_bounds(fan_bounds, block):
    column = []
    for slot, k in enumerate(WAVES):
        column += [0, 64] if slot == 0 else [k, 128 - k]
    pick = jnp.asarray(np.array(column, np.int32))[block]
    table = fan_bounds[:, : NT // 2].reshape(2, 64, 128)
    mine = lax.dynamic_slice(table, (0, 0, pick), (2, 64, 1))
    top = jnp.broadcast_to(fan_bounds[:, NT // 2].reshape(2, 1, 1), (2, 8, 1))
    both = jnp.broadcast_to(jnp.concatenate([mine, top], axis=1), (2, 72, 128))
    return both[0], both[1]


def after_kernel(value_ref, sign_ref, out_ref):
    pass


def after(value, sign):
    return pl.pallas_call(
        after_kernel,
        out_shape=jax.ShapeDtypeStruct(value.shape, value.dtype),
        in_specs=[ANY, ANY],
        out_specs=ANY,
        input_output_aliases={0: 0},
        cost_estimate=pl.CostEstimate(flops=0, bytes_accessed=0, transcendentals=0),
    )(value, sign)


def outer_kernel(near_ref, top_ref, bottom_ref):
    for ref, source, first in ((top_ref, 0, 0), (bottom_ref, 7, 64)):
        for t in range(9):
            ref[pl.ds(16 * t, 16), :] = near_ref[source, pl.ds(t * ROWS + first, 16), :]
        ref[pl.ds(144, 128), :] = near_ref[source, pl.ds(SIDE, 128), :]


def per_device(record, channel_ok, fan_bounds):
    chan, part = lax.axis_index("chan"), lax.axis_index("tm")
    block = chan * 8 + part
    place = jnp.stack([chan, part]).astype(jnp.int32)
    series = lax.all_to_all(record.reshape(8, ROWS, 2048), "tm", 0, 0, tiled=True)
    good = lax.dynamic_slice(channel_ok, (part * ROWS,), (ROWS,)).astype(F32)
    good = jnp.broadcast_to(good[:, None], (ROWS, 128))
    low, high = window_bounds(fan_bounds, block)
    corner = lax.broadcasted_iota(jnp.int32, (8, 128), 0) == 0
    packed = (corner & (block == 0)).astype(F32)
    spectra = forward(place, series, good, low, high, packed)
    pencil = lax.all_to_all(spectra, ("chan", "tm"), 0, 0, tiled=True)
    passed = channels(pencil, low, high, packed)
    back = lax.all_to_all(passed, ("chan", "tm"), 0, 0, tiled=True)
    near, far = backward(place, back)
    near = lax.all_to_all(near, "tm", 0, 0, tiled=True)
    down = [(i, i + 1) for i in range(15)]
    outer = jax.ShapeDtypeStruct((272, 128), BF)
    top, bottom = call(outer_kernel, [outer, outer], [VMEM, VMEM], [], 10**6, near)
    above = lax.ppermute(bottom, "chan", down)
    below = lax.ppermute(top, "chan", [(b, a) for a, b in down])
    whole = edges(place, above, top, bottom, below, tensor(0, place, near))
    far = lax.all_to_all(after(far, near), "tm", 0, 0, tiled=True).reshape(640, FAR)
    return tensor(1, place, near, above, below, far, whole)


def solution(mesh):
    in_specs = (P("chan", "tm"), P("chan"), P())
    out_specs = P("chan", "tm")
    return jax.shard_map(
        per_device, mesh=mesh, in_specs=in_specs, out_specs=out_specs, check_vma=False
    )
```

```python
import functools
import math

import jax
import jax.numpy as jnp
import ml_dtypes
import numpy as np
from jax import lax
from jax.experimental import pallas as pl
from jax.experimental.pallas import tpu as pltpu
from jax.sharding import PartitionSpec as P

NC = 10240
NT = 16384
ROWS = 80
TF = 128
R = 4
GROUP = 63
SIDE = 9 * ROWS
OUTER = SIDE + 16
NEAR = OUTER + 7 * 16
FAR = 896
BF = jnp.bfloat16
F32 = jnp.float32
VMEM = pl.BlockSpec(memory_space=pltpu.VMEM)
ANY = pl.BlockSpec(memory_space=pl.ANY)

WAVES = [0] + [8 * n for n in range(1, 8)] + [4 + 8 * n for n in range(8)]
WAVES += [q + 8 * n for q in (1, 2, 3) for n in range(16)]


def two_parts(matrix):
    high = matrix.astype(ml_dtypes.bfloat16)
    low = (matrix - high.astype(np.float64)).astype(ml_dtypes.bfloat16)
    return high, low


def turn(numbers, length):
    angle = (numbers % length) * (2.0 * np.pi / length)
    return np.cos(angle), np.sin(angle)


def time_tables():
    n = np.arange(128)[:, None]
    j = np.concatenate([np.arange(64), 127 - np.arange(64)])[None, :]
    cos, sin = turn(n * j, 128)

    def halves(re, im):
        return np.concatenate([re[:, :64], im[:, :64], re[:, 64:], im[:, 64:]], axis=1)

    forward = np.concatenate([halves(cos, -sin), halves(sin, cos)], axis=0)
    backward = np.concatenate(
        [halves(cos, -sin).T, halves(sin, cos).T], axis=1
    ) / NT
    jj = np.arange(64)[None, :]
    c0, s0 = turn(n * 128 * jj, NT)
    c1, s1 = turn(n * (64 + 128 * jj), NT)
    zero = np.zeros((128, 128))
    even = np.concatenate([c0, -s0], axis=1)
    even[:, 64] = 1.0 - 2.0 * (np.arange(128) % 2)
    odd = np.concatenate([c1, -s1], axis=1)
    first = np.concatenate(
        [np.concatenate([even, zero], axis=1), np.concatenate([zero, odd], axis=1)], axis=0
    )
    weight = np.full(256, 2.0)
    weight[0] = 1.0
    weight[64] = 1.0
    last = (first * weight[None, :]).T / NT
    k = np.array(WAVES)[:, None]
    tw_cos, tw_sin = turn(k * np.arange(128)[None, :], NT)
    return forward, backward, first, last, tw_cos, tw_sin


def chan_tables():
    cos, sin = turn(np.arange(128)[:, None] * np.arange(128)[None, :], 128)
    forward = np.block([[cos, -sin], [sin, cos]])
    backward = np.block([[cos, sin], [-sin, cos]])
    tw_cos, tw_sin = turn(np.arange(ROWS)[:, None] * np.arange(128)[None, :], NC)
    return forward, backward, tw_cos, tw_sin


def plus(a, b):
    if a is None:
        return b
    if b is None:
        return a
    return a + b


def minus(a, b):
    if b is None:
        return a
    if a is None:
        return -b
    return a - b


def times(value, number):
    if value is None or number == 0.0:
        return None
    if number == 1.0:
        return value
    if number == -1.0:
        return -value
    return value * number


def cadd(x, y):
    return plus(x[0], y[0]), plus(x[1], y[1])


def csub(x, y):
    return minus(x[0], y[0]), minus(x[1], y[1])


def spun(x, step, length, sign):
    step = step % length
    if 4 * step % length == 0:
        quarter = 4 * step // length
        c = (1.0, 0.0, -1.0, 0.0)[quarter]
        s = (0.0, 1.0, 0.0, -1.0)[quarter]
    else:
        c = math.cos(2.0 * math.pi * step / length)
        s = math.sin(2.0 * math.pi * step / length)
    s = sign * s
    re, im = x
    if 8 * step % length == 0 and 4 * step % length != 0 and re is not None and im is not None:
        a = abs(c)
        u = re if c > 0 else -re
        v = im if c > 0 else -im
        if c * s > 0:
            return (u - v) * a, (v + u) * a
        return (u + v) * a, (v - u) * a
    return minus(times(re, c), times(im, s)), plus(times(im, c), times(re, s))


def fft_list(xs, sign):
    count = len(xs)
    if count == 1:
        return xs
    even = fft_list(xs[0::2], sign)
    odd = fft_list(xs[1::2], sign)
    head, tail = [], []
    for k in range(count // 2):
        t = spun(odd[k], k, count, sign)
        head.append(cadd(even[k], t))
        tail.append(csub(even[k], t))
    return head + tail


def rfft_list(xs):
    count = len(xs)
    if count == 2:
        return [(xs[0] + xs[1], None), (xs[0] - xs[1], None)]
    even = rfft_list(xs[0::2])
    odd = rfft_list(xs[1::2])
    out = [None] * (count // 2 + 1)
    for k in range(count // 4 + 1):
        t = spun(odd[k], k, count, -1.0)
        out[k] = cadd(even[k], t)
        if k < count // 4:
            re, im = csub(even[k], t)
            out[count // 2 - k] = (re, minus(None, im) if im is not None else None)
    return out


def irfft_list(ys):
    half = len(ys) - 1
    count = 2 * half
    if count == 2:
        return [ys[0][0] + ys[1][0], ys[0][0] - ys[1][0]]
    evens, odds = [], []
    for k in range(count // 4 + 1):
        mirror = (ys[half - k][0], minus(None, ys[half - k][1]) if ys[half - k][1] is not None else None)
        if 2 * k == half:
            evens.append((ys[k][0] * 2.0, None))
            re, _ = spun(ys[k], k, count, 1.0)
            odds.append((re * 2.0, None))
        else:
            both = cadd(ys[k], mirror)
            gap = spun(csub(ys[k], mirror), k, count, 1.0)
            if half == 1 and k == 0:
                both = (both[0], None)
                gap = (gap[0], None)
            evens.append(both)
            odds.append(gap)
    even = irfft_list(evens)
    odd = irfft_list(odds)
    out = []
    for e, o in zip(even, odd):
        out += [e, o]
    return out


def fft5(xs, sign):
    c1, c2 = math.cos(2 * math.pi / 5), math.cos(4 * math.pi / 5)
    s1, s2 = math.sin(2 * math.pi / 5), math.sin(4 * math.pi / 5)
    out = [[None, None] for _ in range(5)]
    pairs = []
    for part in range(2):
        x = [v[part] for v in xs]
        t1, t2, t3, t4 = x[1] + x[4], x[2] + x[3], x[1] - x[4], x[2] - x[3]
        out[0][part] = x[0] + t1 + t2
        pairs.append(
            (
                x[0] + c1 * t1 + c2 * t2,
                x[0] + c2 * t1 + c1 * t2,
                s1 * t3 + s2 * t4,
                s2 * t3 - s1 * t4,
            )
        )
    (ra, rb, rc, rd), (ia, ib, ic, idd) = pairs
    if sign > 0:
        out[1] = [ra - ic, ia + rc]
        out[4] = [ra + ic, ia - rc]
        out[2] = [rb - idd, ib + rd]
        out[3] = [rb + idd, ib - rd]
    else:
        out[1] = [ra + ic, ia - rc]
        out[4] = [ra - ic, ia + rc]
        out[2] = [rb + idd, ib - rd]
        out[3] = [rb - idd, ib + rd]
    return [tuple(v) for v in out]


def dot(a, b):
    return lax.dot_general(a, b, (((1,), (0,)), ((), ())), preferred_element_type=F32)


def parted(value):
    high = value.astype(BF)
    low = (value - high.astype(F32)).astype(BF)
    return high, low


def forward_kernel(
    x_ref, ok_ref, low_ref, high_ref, packed_ref, tc_ref, ts_ref, w_ref, w0_ref, out_ref,
    stage, hi_ref, lo_ref
):
    def tile_body(tile, carry):
        rows = pl.ds(pl.multiple_of(tile * 16, 16), 16)
        good = ok_ref[rows, :]
        for a in range(16):
            xs = [x_ref[s, rows, a * 128 : (a + 1) * 128].astype(F32) * good for s in range(8)]
            ys = rfft_list(xs)
            stage[a, 0] = ys[0][0]
            for q in (1, 2, 3):
                re, im = spun(ys[q], a * q, 128, -1.0)
                stage[a, 2 * q] = re
                stage[a, 2 * q + 1] = im
            stage[a, 1] = ys[4][0]

        def put(slot, re, im):
            base = pl.ds(pl.multiple_of(slot * ROWS + tile * 16, 16), 16)
            for part, value in enumerate((re, im)):
                high, low = parted(value)
                hi_ref[base, part * 128 : (part + 1) * 128] = high
                lo_ref[base, part * 128 : (part + 1) * 128] = low

        def twist(slot, value):
            re, im = value
            c = tc_ref[slot : slot + 1, :]
            s = ts_ref[slot : slot + 1, :]
            put(slot, re * c + im * s, im * c - re * s)

        ys = rfft_list([stage[a, 0] for a in range(16)])
        put(0, ys[0][0], ys[8][0])
        for n in range(1, 8):
            twist(n, ys[n])
        ys = fft_list([spun((stage[a, 1], None), a, 32, -1.0) for a in range(16)], -1.0)
        for n in range(8):
            twist(8 + n, ys[n])
        for q in (1, 2, 3):
            ys = fft_list([(stage[a, 2 * q], stage[a, 2 * q + 1]) for a in range(16)], -1.0)
            for n in range(16):
                twist(16 * q + n, ys[n])
        return carry

    lax.fori_loop(0, 5, tile_body, 0, unroll=5)

    def mixed(rows, w):
        high, low = hi_ref[rows, :], lo_ref[rows, :]
        return dot(high, w[0]) + dot(low, w[0]) + dot(high, w[1])

    first = mixed(pl.ds(0, ROWS), w0_ref).astype(BF)
    out_ref[0] = first[:, :128]
    out_ref[1] = first[:, 128:]

    def wave_body(step, carry):
        res = mixed(pl.ds(pl.multiple_of(ROWS + step * GROUP * ROWS, 16), GROUP * ROWS), w_ref).astype(BF)
        for n in range(GROUP):
            out_ref[2 + 2 * GROUP * step + 2 * n] = res[n * ROWS : (n + 1) * ROWS, :128]
            out_ref[3 + 2 * GROUP * step + 2 * n] = res[n * ROWS : (n + 1) * ROWS, 128:]
        return carry

    lax.fori_loop(0, 63 // GROUP, wave_body, 0)


def backward_kernel(
    in_ref, tc_ref, ts_ref, w_ref, w0_ref, near_ref, far_ref, stage, mid_ref
):
    def joined(slot):
        return jnp.concatenate([in_ref[2 * slot], in_ref[2 * slot + 1]], axis=1)

    first = joined(0)
    mid_ref[pl.ds(0, ROWS), :] = dot(first, w0_ref[0]) + dot(first, w0_ref[1])

    def wave_body(step, carry):
        data = jnp.concatenate([joined(1 + step * GROUP + n) for n in range(GROUP)], axis=0)
        mid_ref[pl.ds(pl.multiple_of(ROWS + step * GROUP * ROWS, 16), GROUP * ROWS), :] = dot(
            data, w_ref[0]
        ) + dot(data, w_ref[1])
        return carry

    lax.fori_loop(0, 63 // GROUP, wave_body, 0)
    lane = lax.broadcasted_iota(jnp.int32, (16, 128), 1)

    sides = [jnp.zeros((16, 128), F32) for _ in range(8)]
    for tile in range(5):

        def get(slot):
            base = pl.ds(slot * ROWS + tile * 16, 16)
            return mid_ref[base, :128], mid_ref[base, 128:]

        def twisted(slot):
            re, im = get(slot)
            c = tc_ref[slot : slot + 1, :]
            s = ts_ref[slot : slot + 1, :]
            return re * c - im * s, im * c + re * s

        mean, top = get(0)
        ys = irfft_list([(mean, None)] + [twisted(n) for n in range(1, 8)] + [(top, None)])
        for a in range(16):
            stage[a, 0] = ys[a]
        ys = fft_list([twisted(8 + n) for n in range(8)] + [(None, None)] * 8, 1.0)
        for a in range(16):
            stage[a, 1] = 2.0 * spun(ys[a], a, 32, 1.0)[0]
        for q in (1, 2, 3):
            ys = fft_list([twisted(16 * q + n) for n in range(16)], 1.0)
            for a in range(16):
                re, im = spun(ys[a], a * q, 128, 1.0)
                stage[a, 2 * q] = re
                stage[a, 2 * q + 1] = im
        rows = pl.ds(tile * 16, 16)

        def series(a):
            parts = [(stage[a, 0], None)]
            parts += [(stage[a, 2 * q], stage[a, 2 * q + 1]) for q in (1, 2, 3)]
            return [y.astype(BF) for y in irfft_list(parts + [(stage[a, 1], None)])]

        ends = {}
        for a in range(16):
            ys = series(a)
            for s in range(8):
                if a < 9:
                    near_ref[s, pl.ds(a * ROWS + tile * 16, 16), :] = ys[s]
                else:
                    far_ref[s, rows, (a - 9) * 128 : (a - 8) * 128] = ys[s]
            if a in (0, 15):
                ends[a] = ys
        blank = jnp.zeros((16, 128), BF)
        for s in range(8):
            after = ends[0][s + 1] if s < 7 else blank
            before = ends[15][s - 1] if s > 0 else blank
            both = jnp.where(lane < 64, after.astype(F32), before.astype(F32))
            here = ((lane - 16 * tile + 5) & 127) < 10
            sides[s] = jnp.where(here, pltpu.roll(both, 16 * tile, 1), sides[s])
    base = pl.multiple_of(jnp.where(lax.axis_index("tm") == 7, 64, 0), 16)
    for s in range(8):
        near_ref[s, pl.ds(SIDE, 16), :] = sides[s].astype(BF)
        for n in range(7):
            near_ref[s, pl.ds(OUTER + 16 * n, 16), :] = far_ref[
                s, pl.ds(base, 16), n * 128 : (n + 1) * 128
            ]


STEP = 40


def channel_kernel(
    in_ref, low_ref, high_ref, first_ref, tc_ref, ts_ref, w_ref, v_ref, out_ref,
    flat, u_re, u_im, a_re, a_im
):
    def load_body(p, carry):
        flat[pl.ds(pl.multiple_of(p * ROWS, 8), ROWS), :] = in_ref[p].astype(F32)
        return carry

    lax.fori_loop(0, 128, load_body, 0, unroll=16)
    packed = first_ref[...]
    blank = jnp.zeros((8, 128), F32)

    def in_body(step, carry):
        parts = []
        for n in range(STEP):
            turned = flat[pl.ds(step * STEP + n, 128, stride=ROWS), :].T
            re, im = turned[:64], turned[64:]
            im = jnp.concatenate([im[:8] * (1.0 - packed), im[8:], im[:8] * packed], axis=0)
            re = jnp.concatenate([re, blank], axis=0)
            parts.append(jnp.concatenate([re, im], axis=1).astype(BF))
        data = jnp.concatenate(parts, axis=0)
        res = dot(data, w_ref[0]) + dot(data, w_ref[1])
        for n in range(STEP):
            r = step * STEP + n
            re = res[n * 72 : (n + 1) * 72, :128]
            im = res[n * 72 : (n + 1) * 72, 128:]
            c = tc_ref[pl.ds(r, 1), :]
            s = ts_ref[pl.ds(r, 1), :]
            u_re[r] = re * c + im * s
            u_im[r] = im * c - re * s
        return carry

    lax.fori_loop(0, ROWS // STEP, in_body, 0)
    lane = lax.broadcasted_iota(jnp.int32, (8, 128), 1)

    def fan_body(tile, carry):
        rows = pl.ds(pl.multiple_of(tile * 8, 8), 8)
        low = low_ref[rows, :]
        high = high_ref[rows, :]
        for n2 in range(5):
            spots = [(5 * n1 + 16 * n2) % ROWS for n1 in range(16)]
            ys = fft_list([(u_re[r, rows, :], u_im[r, rows, :]) for r in spots], -1.0)
            for k1 in range(16):
                a_re[n2 * 16 + k1] = ys[k1][0]
                a_im[n2 * 16 + k1] = ys[k1][1]
        for k1 in range(16):
            ys = fft5([(a_re[n2 * 16 + k1], a_im[n2 * 16 + k1]) for n2 in range(5)], -1.0)
            kept = []
            for k2 in range(5):
                outer = next(k for k in range(ROWS) if k % 16 == k1 and k % 5 == k2)
                if outer < ROWS // 2:
                    fold = lane + outer * 128
                else:
                    fold = (NC - outer * 128) - lane
                keep = (fold >= low) & (fold <= high)
                kept.append(tuple(jnp.where(keep, v, 0.0) for v in ys[k2]))
            ys = fft5(kept, 1.0)
            for n2 in range(5):
                a_re[n2 * 16 + k1] = ys[n2][0]
                a_im[n2 * 16 + k1] = ys[n2][1]
        for n2 in range(5):
            spots = [(5 * n1 + 16 * n2) % ROWS for n1 in range(16)]
            ys = fft_list([(a_re[n2 * 16 + k1], a_im[n2 * 16 + k1]) for k1 in range(16)], 1.0)
            for n1 in range(16):
                u_re[spots[n1], rows, :] = ys[n1][0]
                u_im[spots[n1], rows, :] = ys[n1][1]
        return carry

    lax.fori_loop(0, 9, fan_body, 0)

    def out_body(step, carry):
        highs, lows = [], []
        for n in range(STEP):
            r = step * STEP + n
            re, im = u_re[r], u_im[r]
            re = jnp.concatenate([re[:8] + re[64:], re[8:64]], axis=0)
            im = jnp.concatenate([im[:8] + im[64:], im[8:64]], axis=0)
            c = tc_ref[pl.ds(r, 1), :]
            s = ts_ref[pl.ds(r, 1), :]
            high, low = parted(jnp.concatenate([re * c - im * s, im * c + re * s], axis=1))
            highs.append(high)
            lows.append(low)
        high = jnp.concatenate(highs, axis=0)
        low = jnp.concatenate(lows, axis=0)
        res = (dot(high, v_ref[0]) + dot(low, v_ref[0]) + dot(high, v_ref[1])) * (1.0 / NC)
        for n in range(STEP):
            block = res[n * 64 : (n + 1) * 64]
            both = jnp.concatenate([block[:, :128], block[:, 128:]], axis=0)
            flat[pl.ds(step * STEP + n, 128, stride=ROWS), :] = both.T
        return carry

    lax.fori_loop(0, ROWS // STEP, out_body, 0)

    def store_body(p, carry):
        out_ref[p] = flat[pl.ds(pl.multiple_of(p * ROWS, 8), ROWS), :].astype(BF)
        return carry

    lax.fori_loop(0, 128, store_body, 0, unroll=16)


def slide_tables():
    row = np.arange(256)[:, None]
    col = np.arange(128)[None, :]
    change = (row == col + 125) * 1.0 - (row == col + 123) * 1.0
    shift = (row == col + 124) * 1.0
    nine = ((row >= col) & (row <= col + 8)) * 1.0
    nine = np.concatenate([nine[:128], nine[128:]], axis=1)
    return np.concatenate([change, shift], axis=1), np.concatenate([nine, nine], axis=0)


BAND = 128
PER = 9


def tensor_kernel(half, *refs):
    if half == 0:
        near_ref, lanes_ref, nine_ref, out_ref = refs[:4]
        slope, level, prod, trio, both_ref = refs[4:]
    else:
        near_ref, above_ref, below_ref, far_ref, lanes_ref, nine_ref, _, out_ref = refs[:8]
        slope, level, prod, trio, both_ref = refs[8:]
    lane = lax.broadcasted_iota(jnp.int32, (8, 128), 1)
    sub = lax.broadcasted_iota(jnp.int32, (8, 128), 0)
    step = pl.program_id(0)
    chan, part = lax.axis_index("chan"), lax.axis_index("tm")

    def column(t):
        if t in (-1, 16):
            parts = []
            for j in range(8):
                side = near_ref[j, pl.ds(SIDE, 16), :].astype(F32)
                parts.append(side.astype(BF))
                for n in range(1, 5):
                    parts.append(pltpu.roll(side, 128 - 16 * n, 1).astype(BF))
            if half == 1:
                first = pltpu.roll(above_ref[pl.ds(144, 16), :].astype(F32), 64, 1).astype(BF)
                parts = [first] + parts + [below_ref[pl.ds(144, 16), :]]
            return jnp.concatenate(parts, axis=0)
        rows = pl.ds(16 * t if t < 9 else 160 + 16 * (t - 9), 16)
        if t < 9:
            inner = [near_ref[j, pl.ds(t * ROWS, ROWS), :] for j in range(8)]
        else:
            inner = [far_ref[:, (t - 9) * 128 : (t - 8) * 128]]
        if half == 1:
            inner = [above_ref[rows, :]] + inner + [below_ref[rows, :]]
        return jnp.concatenate(inner, axis=0)

    @pl.when(step == 0)
    def _():
        left = column(8 * half - 1)
        for t in range(PER):
            right = column(8 * half + t)
            res = dot(jnp.concatenate([left, right], axis=1), lanes_ref[...])
            rows = pl.ds(16 - 16 * half, 640 + 32 * half)
            slope[t, rows, :] = res[:, :128]
            level[t, rows, :] = res[:, 128:]
            left = right

    top = pl.multiple_of(step * BAND, BAND)
    for k in range(BAND // 8 + 2):
        base = pl.multiple_of(top + k * 8, 8)
        for t in range(PER):
            grad_time = slope[t, pl.ds(base + 12, 8), :]
            masked = grad_time
            if half == 0 and t == 0:
                masked = jnp.where((lane >= 4) | (part > 0), masked, 0.0)
            if half == 1 and t == PER - 1:
                masked = jnp.where((lane < 4) | (part < 7), masked, 0.0)
            if half == 1 and k == 0:
                masked = jnp.where((sub >= 4) | (chan > 0) | (step > 0), masked, 0.0)
            if half == 1 and k == BAND // 8:
                masked = jnp.where((sub < 4) | (chan < 15) | (step < 640 // BAND - 1), masked, 0.0)
            grad_chan = level[t, pl.ds(base + 13, 8), :] - level[t, pl.ds(base + 11, 8), :]
            prod[0, t, pl.ds(k * 8, 8), :] = grad_chan * masked
            prod[1, t, pl.ds(k * 8, 8), :] = grad_time * masked
    for k in range(BAND // 8 + 1):
        for n in range(2):
            for t in range(PER):
                trio[n, t, pl.ds(k * 8, 8), :] = (
                    prod[n, t, pl.ds(k * 8, 8), :]
                    + prod[n, t, pl.ds(k * 8 + 1, 8), :]
                    + prod[n, t, pl.ds(k * 8 + 2, 8), :]
                )
    for k in range(BAND // 16):
        for n in range(2):
            for t in range(PER):
                total = (
                    trio[n, t, pl.ds(k * 16, 16), :]
                    + trio[n, t, pl.ds(k * 16 + 3, 16), :]
                    + trio[n, t, pl.ds(k * 16 + 6, 16), :]
                )
                high, low = parted(total)
                both_ref[n, t, pl.ds(k * 16, 16), :128] = high
                both_ref[n, t, pl.ds(k * 16, 16), 128:] = low
    nine = nine_ref[...]
    scale = 1.0 / 324.0
    for g in range(2):
        sums = []
        for n in range(2):
            res = dot(both_ref[n, pl.ds(g * 4, 5)].reshape(5 * BAND, 256), nine)
            sums.append(res[: 4 * BAND, :128] + res[BAND:, 128:])
        res = (sums[0] * -scale) / (sums[1] * scale + 1e-05)
        for t in range(4):
            cols = slice(g * 512 + t * 128, g * 512 + t * 128 + 128)
            out_ref[:, cols] = res[t * BAND : (t + 1) * BAND]


def ahead(parts, count, lane):
    turned = [pltpu.roll(v, (-count) % 128, 1) for v in parts]
    out = []
    for t in range(len(parts)):
        if count > 0:
            other = turned[min(t + 1, len(parts) - 1)]
            out.append(jnp.where(lane < 128 - count, turned[t], other))
        else:
            other = turned[max(t - 1, 0)]
            out.append(jnp.where(lane < -count, other, turned[t]))
    return out


def edge_kernel(above_ref, top_ref, bottom_ref, below_ref, _, out_ref, wide, prod):
    lane = lax.broadcasted_iota(jnp.int32, (8, 128), 1)
    sub = lax.broadcasted_iota(jnp.int32, (8, 128), 0)
    step = pl.program_id(0)
    chan, part = lax.axis_index("chan"), lax.axis_index("tm")

    def spread(start, ref, turned):
        rows = pl.ds(start, 16)
        wide[0, rows, :] = pltpu.roll(ref[pl.ds(144, 16), :].astype(F32), turned, 1)
        for t in range(9):
            wide[t + 1, rows, :] = ref[pl.ds(16 * t, 16), :].astype(F32)

    @pl.when(step == 0)
    def _():
        spread(0, above_ref, 64)
        spread(16, top_ref, 0)

    @pl.when(step == 1)
    def _():
        spread(0, bottom_ref, 64)
        spread(16, below_ref, 0)

    skip = pl.multiple_of(8 - step * 8, 8)
    for k in range(2):
        first = skip + k * 8 + 4
        row = sub + first
        keep = ((row >= 16) | (step == 1) | (chan > 0)) & ((row < 16) | (step == 0) | (chan < 15))
        here = [wide[t, pl.ds(first, 8), :] for t in range(10)]
        right, left = ahead(here, 1, lane), ahead(here, -1, lane)
        for t in range(10):
            grad_time = right[t] - left[t]
            masked = jnp.where(keep, grad_time, 0.0)
            if t == 0:
                masked = jnp.where(part > 0, masked, 0.0)
            grad_chan = wide[t, pl.ds(first + 1, 8), :] - wide[t, pl.ds(first - 1, 8), :]
            prod[0, t, pl.ds(k * 8, 8), :] = grad_chan * masked
            prod[1, t, pl.ds(k * 8, 8), :] = grad_time * masked
    sums = []
    for n in range(2):
        parts = []
        for t in range(10):
            total = prod[n, t, pl.ds(0, 8), :]
            for d in range(1, 9):
                total = total + prod[n, t, pl.ds(d, 8), :]
            parts.append(total)
        near, far = ahead(parts, 1, lane), ahead(parts, -1, lane)
        three = [v + a + b for v, a, b in zip(parts, near, far)]
        near, far = ahead(three, 3, lane), ahead(three, -3, lane)
        sums.append([v + a + b for v, a, b in zip(three, near, far)][1:9])
    scale = 1.0 / 324.0
    out = [(c * -scale) / (a * scale + 1e-05) for c, a in zip(*sums)]
    out_ref[...] = jnp.concatenate(out, axis=1)


def call(kernel, out, specs, scratch, flops, *args):
    nbytes = sum(a.size * a.dtype.itemsize for a in args) + 3 * 2**20
    return pl.pallas_call(
        kernel,
        out_shape=out,
        in_specs=[VMEM] * len(args),
        out_specs=specs,
        scratch_shapes=scratch,
        compiler_params=pltpu.CompilerParams(vmem_limit_bytes=48 * 2**20),
        cost_estimate=pl.CostEstimate(flops=flops, bytes_accessed=nbytes, transcendentals=0),
    )(*args)


def pair(matrix):
    return jnp.asarray(np.stack(two_parts(matrix)))


def single(table):
    return jnp.asarray(table.astype(np.float32))


def forward(series, good, low, high, packed):
    fwd, _, first, _, tc, ts = time_tables()
    scratch = [
        pltpu.VMEM((16, 8, 16, 128), F32),
        pltpu.VMEM((64 * ROWS, 256), BF),
        pltpu.VMEM((64 * ROWS, 256), BF),
    ]
    out = jax.ShapeDtypeStruct((128, ROWS, 128), BF)
    tables = single(tc), single(ts), pair(fwd), pair(first)
    return call(
        forward_kernel,
        out,
        VMEM,
        scratch,
        4 * 10**9,
        series,
        good,
        low,
        high,
        packed,
        *tables,
    )


def backward(spectra):
    _, bwd, _, last, tc, ts = time_tables()
    scratch = [pltpu.VMEM((16, 8, 16, 128), F32), pltpu.VMEM((64 * ROWS, 256), F32)]
    out = [jax.ShapeDtypeStruct(s, BF) for s in ((8, NEAR, 128), (8, ROWS, FAR))]
    tables = single(tc), single(ts), pair(bwd), pair(last)
    return call(
        backward_kernel, out, [VMEM, VMEM], scratch, 4 * 10**9, spectra, *tables
    )


def channels(pencil, low, high, packed):
    fwd, bwd, tc, ts = chan_tables()
    scratch = [
        pltpu.VMEM((128 * ROWS, 128), F32),
        pltpu.VMEM((ROWS, 72, 128), F32),
        pltpu.VMEM((ROWS, 72, 128), F32),
        pltpu.VMEM((ROWS, 8, 128), F32),
        pltpu.VMEM((ROWS, 8, 128), F32),
    ]
    out = jax.ShapeDtypeStruct((128, ROWS, 128), BF)
    tables = single(tc), single(ts), pair(fwd), pair(bwd)
    return call(channel_kernel, out, VMEM, scratch, 8 * 10**9, pencil, low, high, packed, *tables)


def tensor(half, near, above=None, below=None, far=None, whole=None):
    lanes, nine = (jnp.asarray(t.astype(ml_dtypes.bfloat16)) for t in slide_tables())
    scratch = [
        pltpu.VMEM((PER, 672, 128), F32),
        pltpu.VMEM((PER, 672, 128), F32),
        pltpu.VMEM((2, PER, BAND + 16, 128), F32),
        pltpu.VMEM((2, PER, BAND + 16, 128), F32),
        pltpu.VMEM((2, PER, BAND, 256), BF),
    ]
    if half == 0:
        args = (near, lanes, nine)
        specs, alias = [VMEM] * 3, {}
    else:
        args = (near, above, below, far, lanes, nine, whole)
        specs, alias = [VMEM] * 6 + [ANY], {6: 0}
    return pl.pallas_call(
        functools.partial(tensor_kernel, half),
        grid=(640 // BAND,),
        out_shape=jax.ShapeDtypeStruct((640, 2048), F32),
        in_specs=specs,
        out_specs=pl.BlockSpec((BAND, 1024), lambda g: (g, half)),
        scratch_shapes=scratch,
        input_output_aliases=alias,
        compiler_params=pltpu.CompilerParams(vmem_limit_bytes=40 * 2**20),
        cost_estimate=pl.CostEstimate(flops=10**9, bytes_accessed=9 * 2**20, transcendentals=0),
    )(*args)


def edges(above, top, bottom, below, whole):
    return pl.pallas_call(
        edge_kernel,
        grid=(2,),
        out_shape=jax.ShapeDtypeStruct((640, 2048), F32),
        in_specs=[VMEM] * 4 + [ANY],
        out_specs=pl.BlockSpec((8, 1024), lambda g: (79 * g, 0)),
        scratch_shapes=[pltpu.VMEM((10, 32, 128), F32), pltpu.VMEM((2, 10, 16, 128), F32)],
        input_output_aliases={4: 0},
        compiler_params=pltpu.CompilerParams(vmem_limit_bytes=16 * 2**20),
        cost_estimate=pl.CostEstimate(flops=10**7, bytes_accessed=2**19, transcendentals=0),
    )(above, top, bottom, below, whole)


def window_bounds(fan_bounds, block):
    column = []
    for slot, k in enumerate(WAVES):
        column += [0, 64] if slot == 0 else [k, 128 - k]
    pick = jnp.asarray(np.array(column, np.int32))[block]
    table = fan_bounds[:, : NT // 2].reshape(2, 64, 128)
    mine = lax.dynamic_slice(table, (0, 0, pick), (2, 64, 1))
    top = jnp.broadcast_to(fan_bounds[:, NT // 2].reshape(2, 1, 1), (2, 8, 1))
    both = jnp.broadcast_to(jnp.concatenate([mine, top], axis=1), (2, 72, 128))
    return both[0], both[1]


def after_kernel(value_ref, sign_ref, out_ref):
    pass


def after(value, sign):
    return pl.pallas_call(
        after_kernel,
        out_shape=jax.ShapeDtypeStruct(value.shape, value.dtype),
        in_specs=[ANY, ANY],
        out_specs=ANY,
        input_output_aliases={0: 0},
        cost_estimate=pl.CostEstimate(flops=0, bytes_accessed=0, transcendentals=0),
    )(value, sign)


def outer_kernel(near_ref, top_ref, bottom_ref):
    for ref, source, first in ((top_ref, 0, 0), (bottom_ref, 7, 64)):
        for t in range(9):
            ref[pl.ds(16 * t, 16), :] = near_ref[source, pl.ds(t * ROWS + first, 16), :]
        ref[pl.ds(144, 128), :] = near_ref[source, pl.ds(SIDE, 128), :]


def per_device(record, channel_ok, fan_bounds):
    chan, part = lax.axis_index("chan"), lax.axis_index("tm")
    block = chan * 8 + part
    series = lax.all_to_all(record.reshape(8, ROWS, 2048), "tm", 0, 0, tiled=True)
    good = lax.dynamic_slice(channel_ok, (part * ROWS,), (ROWS,)).astype(F32)
    good = jnp.broadcast_to(good[:, None], (ROWS, 128))
    low, high = window_bounds(fan_bounds, block)
    corner = lax.broadcasted_iota(jnp.int32, (8, 128), 0) == 0
    packed = (corner & (block == 0)).astype(F32)
    spectra = forward(series, good, low, high, packed)
    pencil = lax.all_to_all(spectra, ("chan", "tm"), 0, 0, tiled=True)
    passed = channels(pencil, low, high, packed)
    back = lax.all_to_all(passed, ("chan", "tm"), 0, 0, tiled=True)
    near, far = backward(back)
    near = lax.all_to_all(near, "tm", 0, 0, tiled=True)
    down = [(i, i + 1) for i in range(15)]
    outer = jax.ShapeDtypeStruct((272, 128), BF)
    top, bottom = call(outer_kernel, [outer, outer], [VMEM, VMEM], [], 10**6, near)
    above = lax.ppermute(bottom, "chan", down)
    below = lax.ppermute(top, "chan", [(b, a) for a, b in down])
    whole = edges(above, top, bottom, below, tensor(0, near))
    far = lax.all_to_all(after(far, near), "tm", 0, 0, tiled=True).reshape(640, FAR)
    return tensor(1, near, above, below, far, whole)


def solution(mesh):
    in_specs = (P("chan", "tm"), P("chan"), P())
    out_specs = P("chan", "tm")
    return jax.shard_map(
        per_device, mesh=mesh, in_specs=in_specs, out_specs=out_specs, check_vma=False
    )
```

```python
import functools
import math

import jax
import jax.numpy as jnp
import ml_dtypes
import numpy as np
from jax import lax
from jax.experimental import pallas as pl
from jax.experimental.pallas import tpu as pltpu
from jax.sharding import PartitionSpec as P

NC = 10240
NT = 16384
ROWS = 80
TF = 128
R = 4
GROUP = 63
SIDE = 8 * ROWS
OUTER = SIDE + 16
NEAR = OUTER + 8 * 16
FAR = 1024
BF = jnp.bfloat16
F32 = jnp.float32
VMEM = pl.BlockSpec(memory_space=pltpu.VMEM)
ANY = pl.BlockSpec(memory_space=pl.ANY)

WAVES = [0] + [8 * n for n in range(1, 8)] + [4 + 8 * n for n in range(8)]
WAVES += [q + 8 * n for q in (1, 2, 3) for n in range(16)]


def two_parts(matrix):
    high = matrix.astype(ml_dtypes.bfloat16)
    low = (matrix - high.astype(np.float64)).astype(ml_dtypes.bfloat16)
    return high, low


def turn(numbers, length):
    angle = (numbers % length) * (2.0 * np.pi / length)
    return np.cos(angle), np.sin(angle)


def time_tables():
    n = np.arange(128)[:, None]
    j = np.concatenate([np.arange(64), 127 - np.arange(64)])[None, :]
    cos, sin = turn(n * j, 128)

    def halves(re, im):
        return np.concatenate([re[:, :64], im[:, :64], re[:, 64:], im[:, 64:]], axis=1)

    forward = np.concatenate([halves(cos, -sin), halves(sin, cos)], axis=0)
    backward = np.concatenate(
        [halves(cos, -sin).T, halves(sin, cos).T], axis=1
    ) / NT
    jj = np.arange(64)[None, :]
    c0, s0 = turn(n * 128 * jj, NT)
    c1, s1 = turn(n * (64 + 128 * jj), NT)
    zero = np.zeros((128, 128))
    even = np.concatenate([c0, -s0], axis=1)
    even[:, 64] = 1.0 - 2.0 * (np.arange(128) % 2)
    odd = np.concatenate([c1, -s1], axis=1)
    first = np.concatenate(
        [np.concatenate([even, zero], axis=1), np.concatenate([zero, odd], axis=1)], axis=0
    )
    weight = np.full(256, 2.0)
    weight[0] = 1.0
    weight[64] = 1.0
    last = (first * weight[None, :]).T / NT
    k = np.array(WAVES)[:, None]
    tw_cos, tw_sin = turn(k * np.arange(128)[None, :], NT)
    return forward, backward, first, last, tw_cos, tw_sin


def chan_tables():
    cos, sin = turn(np.arange(128)[:, None] * np.arange(128)[None, :], 128)
    forward = np.block([[cos, -sin], [sin, cos]])
    backward = np.block([[cos, sin], [-sin, cos]])
    tw_cos, tw_sin = turn(np.arange(ROWS)[:, None] * np.arange(128)[None, :], NC)
    return forward, backward, tw_cos, tw_sin


def plus(a, b):
    if a is None:
        return b
    if b is None:
        return a
    return a + b


def minus(a, b):
    if b is None:
        return a
    if a is None:
        return -b
    return a - b


def times(value, number):
    if value is None or number == 0.0:
        return None
    if number == 1.0:
        return value
    if number == -1.0:
        return -value
    return value * number


def cadd(x, y):
    return plus(x[0], y[0]), plus(x[1], y[1])


def csub(x, y):
    return minus(x[0], y[0]), minus(x[1], y[1])


def spun(x, step, length, sign):
    step = step % length
    if 4 * step % length == 0:
        quarter = 4 * step // length
        c = (1.0, 0.0, -1.0, 0.0)[quarter]
        s = (0.0, 1.0, 0.0, -1.0)[quarter]
    else:
        c = math.cos(2.0 * math.pi * step / length)
        s = math.sin(2.0 * math.pi * step / length)
    s = sign * s
    re, im = x
    if 8 * step % length == 0 and 4 * step % length != 0 and re is not None and im is not None:
        a = abs(c)
        u = re if c > 0 else -re
        v = im if c > 0 else -im
        if c * s > 0:
            return (u - v) * a, (v + u) * a
        return (u + v) * a, (v - u) * a
    return minus(times(re, c), times(im, s)), plus(times(im, c), times(re, s))


def fft_list(xs, sign):
    count = len(xs)
    if count == 1:
        return xs
    even = fft_list(xs[0::2], sign)
    odd = fft_list(xs[1::2], sign)
    head, tail = [], []
    for k in range(count // 2):
        t = spun(odd[k], k, count, sign)
        head.append(cadd(even[k], t))
        tail.append(csub(even[k], t))
    return head + tail


def rfft_list(xs):
    count = len(xs)
    if count == 2:
        return [(xs[0] + xs[1], None), (xs[0] - xs[1], None)]
    even = rfft_list(xs[0::2])
    odd = rfft_list(xs[1::2])
    out = [None] * (count // 2 + 1)
    for k in range(count // 4 + 1):
        t = spun(odd[k], k, count, -1.0)
        out[k] = cadd(even[k], t)
        if k < count // 4:
            re, im = csub(even[k], t)
            out[count // 2 - k] = (re, minus(None, im) if im is not None else None)
    return out


def irfft_list(ys):
    half = len(ys) - 1
    count = 2 * half
    if count == 2:
        return [ys[0][0] + ys[1][0], ys[0][0] - ys[1][0]]
    evens, odds = [], []
    for k in range(count // 4 + 1):
        mirror = (ys[half - k][0], minus(None, ys[half - k][1]) if ys[half - k][1] is not None else None)
        if 2 * k == half:
            evens.append((ys[k][0] * 2.0, None))
            re, _ = spun(ys[k], k, count, 1.0)
            odds.append((re * 2.0, None))
        else:
            both = cadd(ys[k], mirror)
            gap = spun(csub(ys[k], mirror), k, count, 1.0)
            if half == 1 and k == 0:
                both = (both[0], None)
                gap = (gap[0], None)
            evens.append(both)
            odds.append(gap)
    even = irfft_list(evens)
    odd = irfft_list(odds)
    out = []
    for e, o in zip(even, odd):
        out += [e, o]
    return out


def fft5(xs, sign):
    c1, c2 = math.cos(2 * math.pi / 5), math.cos(4 * math.pi / 5)
    s1, s2 = math.sin(2 * math.pi / 5), math.sin(4 * math.pi / 5)
    out = [[None, None] for _ in range(5)]
    pairs = []
    for part in range(2):
        x = [v[part] for v in xs]
        t1, t2, t3, t4 = x[1] + x[4], x[2] + x[3], x[1] - x[4], x[2] - x[3]
        out[0][part] = x[0] + t1 + t2
        pairs.append(
            (
                x[0] + c1 * t1 + c2 * t2,
                x[0] + c2 * t1 + c1 * t2,
                s1 * t3 + s2 * t4,
                s2 * t3 - s1 * t4,
            )
        )
    (ra, rb, rc, rd), (ia, ib, ic, idd) = pairs
    if sign > 0:
        out[1] = [ra - ic, ia + rc]
        out[4] = [ra + ic, ia - rc]
        out[2] = [rb - idd, ib + rd]
        out[3] = [rb + idd, ib - rd]
    else:
        out[1] = [ra + ic, ia - rc]
        out[4] = [ra - ic, ia + rc]
        out[2] = [rb + idd, ib - rd]
        out[3] = [rb - idd, ib + rd]
    return [tuple(v) for v in out]


def dot(a, b):
    return lax.dot_general(a, b, (((1,), (0,)), ((), ())), preferred_element_type=F32)


def parted(value):
    high = value.astype(BF)
    low = (value - high.astype(F32)).astype(BF)
    return high, low


def forward_kernel(
    x_ref, ok_ref, low_ref, high_ref, packed_ref, tc_ref, ts_ref, w_ref, w0_ref, out_ref,
    stage, hi_ref, lo_ref
):
    def tile_body(tile, carry):
        rows = pl.ds(pl.multiple_of(tile * 16, 16), 16)
        good = ok_ref[rows, :]
        for a in range(16):
            xs = [x_ref[s, rows, a * 128 : (a + 1) * 128].astype(F32) * good for s in range(8)]
            ys = rfft_list(xs)
            stage[a, 0] = ys[0][0]
            for q in (1, 2, 3):
                re, im = spun(ys[q], a * q, 128, -1.0)
                stage[a, 2 * q] = re
                stage[a, 2 * q + 1] = im
            stage[a, 1] = ys[4][0]

        def put(slot, re, im):
            base = pl.ds(pl.multiple_of(slot * ROWS + tile * 16, 16), 16)
            for part, value in enumerate((re, im)):
                high, low = parted(value)
                hi_ref[base, part * 128 : (part + 1) * 128] = high
                lo_ref[base, part * 128 : (part + 1) * 128] = low

        def twist(slot, value):
            re, im = value
            c = tc_ref[slot : slot + 1, :]
            s = ts_ref[slot : slot + 1, :]
            put(slot, re * c + im * s, im * c - re * s)

        ys = rfft_list([stage[a, 0] for a in range(16)])
        put(0, ys[0][0], ys[8][0])
        for n in range(1, 8):
            twist(n, ys[n])
        ys = fft_list([spun((stage[a, 1], None), a, 32, -1.0) for a in range(16)], -1.0)
        for n in range(8):
            twist(8 + n, ys[n])
        for q in (1, 2, 3):
            ys = fft_list([(stage[a, 2 * q], stage[a, 2 * q + 1]) for a in range(16)], -1.0)
            for n in range(16):
                twist(16 * q + n, ys[n])
        return carry

    lax.fori_loop(0, 5, tile_body, 0, unroll=5)

    def mixed(rows, w):
        high, low = hi_ref[rows, :], lo_ref[rows, :]
        return dot(high, w[0]) + dot(low, w[0]) + dot(high, w[1])

    first = mixed(pl.ds(0, ROWS), w0_ref).astype(BF)
    out_ref[0] = first[:, :128]
    out_ref[1] = first[:, 128:]

    def wave_body(step, carry):
        res = mixed(pl.ds(pl.multiple_of(ROWS + step * GROUP * ROWS, 16), GROUP * ROWS), w_ref).astype(BF)
        for n in range(GROUP):
            out_ref[2 + 2 * GROUP * step + 2 * n] = res[n * ROWS : (n + 1) * ROWS, :128]
            out_ref[3 + 2 * GROUP * step + 2 * n] = res[n * ROWS : (n + 1) * ROWS, 128:]
        return carry

    lax.fori_loop(0, 63 // GROUP, wave_body, 0)


def backward_kernel(
    in_ref, tc_ref, ts_ref, w_ref, w0_ref, near_ref, far_ref, stage, mid_ref
):
    def joined(slot):
        return jnp.concatenate([in_ref[2 * slot], in_ref[2 * slot + 1]], axis=1)

    first = joined(0)
    mid_ref[pl.ds(0, ROWS), :] = dot(first, w0_ref[0]) + dot(first, w0_ref[1])

    def wave_body(step, carry):
        data = jnp.concatenate([joined(1 + step * GROUP + n) for n in range(GROUP)], axis=0)
        mid_ref[pl.ds(pl.multiple_of(ROWS + step * GROUP * ROWS, 16), GROUP * ROWS), :] = dot(
            data, w_ref[0]
        ) + dot(data, w_ref[1])
        return carry

    lax.fori_loop(0, 63 // GROUP, wave_body, 0)
    lane = lax.broadcasted_iota(jnp.int32, (16, 128), 1)

    sides = [jnp.zeros((16, 128), F32) for _ in range(8)]
    for tile in range(5):

        def get(slot):
            base = pl.ds(slot * ROWS + tile * 16, 16)
            return mid_ref[base, :128], mid_ref[base, 128:]

        def twisted(slot):
            re, im = get(slot)
            c = tc_ref[slot : slot + 1, :]
            s = ts_ref[slot : slot + 1, :]
            return re * c - im * s, im * c + re * s

        mean, top = get(0)
        ys = irfft_list([(mean, None)] + [twisted(n) for n in range(1, 8)] + [(top, None)])
        for a in range(16):
            stage[a, 0] = ys[a]
        ys = fft_list([twisted(8 + n) for n in range(8)] + [(None, None)] * 8, 1.0)
        for a in range(16):
            stage[a, 1] = 2.0 * spun(ys[a], a, 32, 1.0)[0]
        for q in (1, 2, 3):
            ys = fft_list([twisted(16 * q + n) for n in range(16)], 1.0)
            for a in range(16):
                re, im = spun(ys[a], a * q, 128, 1.0)
                stage[a, 2 * q] = re
                stage[a, 2 * q + 1] = im
        rows = pl.ds(tile * 16, 16)

        def series(a):
            parts = [(stage[a, 0], None)]
            parts += [(stage[a, 2 * q], stage[a, 2 * q + 1]) for q in (1, 2, 3)]
            return [y.astype(BF) for y in irfft_list(parts + [(stage[a, 1], None)])]

        ends = {}
        for a in range(16):
            ys = series(a)
            for s in range(8):
                if a < 8:
                    near_ref[s, pl.ds(a * ROWS + tile * 16, 16), :] = ys[s]
                else:
                    far_ref[s, rows, (a - 8) * 128 : (a - 7) * 128] = ys[s]
            if a in (0, 8, 15):
                ends[a] = ys
        blank = jnp.zeros((16, 128), BF)
        for s in range(8):
            after = ends[0][s + 1] if s < 7 else blank
            before = ends[15][s - 1] if s > 0 else blank
            both = jnp.where(lane < 64, after.astype(F32), before.astype(F32))
            here = ((lane - 16 * tile + 5) & 127) < 10
            sides[s] = jnp.where(here, pltpu.roll(both, 16 * tile, 1), sides[s])
            here = ((lane - 16 * tile - 5) & 127) < 5
            middle = pltpu.roll(ends[8][s].astype(F32), 16 * tile + 5, 1)
            sides[s] = jnp.where(here, middle, sides[s])
    base = pl.multiple_of(jnp.where(lax.axis_index("tm") == 7, 64, 0), 16)
    for s in range(8):
        near_ref[s, pl.ds(SIDE, 16), :] = sides[s].astype(BF)
        for n in range(8):
            near_ref[s, pl.ds(OUTER + 16 * n, 16), :] = far_ref[
                s, pl.ds(base, 16), n * 128 : (n + 1) * 128
            ]


STEP = 40


def channel_kernel(
    in_ref, low_ref, high_ref, first_ref, tc_ref, ts_ref, w_ref, v_ref, out_ref,
    flat, u_re, u_im, a_re, a_im
):
    def load_body(p, carry):
        flat[pl.ds(pl.multiple_of(p * ROWS, 8), ROWS), :] = in_ref[p].astype(F32)
        return carry

    lax.fori_loop(0, 128, load_body, 0, unroll=16)
    packed = first_ref[...]
    blank = jnp.zeros((8, 128), F32)

    def in_body(step, carry):
        parts = []
        for n in range(STEP):
            turned = flat[pl.ds(step * STEP + n, 128, stride=ROWS), :].T
            re, im = turned[:64], turned[64:]
            im = jnp.concatenate([im[:8] * (1.0 - packed), im[8:], im[:8] * packed], axis=0)
            re = jnp.concatenate([re, blank], axis=0)
            parts.append(jnp.concatenate([re, im], axis=1).astype(BF))
        data = jnp.concatenate(parts, axis=0)
        res = dot(data, w_ref[0]) + dot(data, w_ref[1])
        for n in range(STEP):
            r = step * STEP + n
            re = res[n * 72 : (n + 1) * 72, :128]
            im = res[n * 72 : (n + 1) * 72, 128:]
            c = tc_ref[pl.ds(r, 1), :]
            s = ts_ref[pl.ds(r, 1), :]
            u_re[r] = re * c + im * s
            u_im[r] = im * c - re * s
        return carry

    lax.fori_loop(0, ROWS // STEP, in_body, 0)
    lane = lax.broadcasted_iota(jnp.int32, (8, 128), 1)

    def fan_body(tile, carry):
        rows = pl.ds(pl.multiple_of(tile * 8, 8), 8)
        low = low_ref[rows, :]
        high = high_ref[rows, :]
        for n2 in range(5):
            spots = [(5 * n1 + 16 * n2) % ROWS for n1 in range(16)]
            ys = fft_list([(u_re[r, rows, :], u_im[r, rows, :]) for r in spots], -1.0)
            for k1 in range(16):
                a_re[n2 * 16 + k1] = ys[k1][0]
                a_im[n2 * 16 + k1] = ys[k1][1]
        for k1 in range(16):
            ys = fft5([(a_re[n2 * 16 + k1], a_im[n2 * 16 + k1]) for n2 in range(5)], -1.0)
            kept = []
            for k2 in range(5):
                outer = next(k for k in range(ROWS) if k % 16 == k1 and k % 5 == k2)
                if outer < ROWS // 2:
                    fold = lane + outer * 128
                else:
                    fold = (NC - outer * 128) - lane
                keep = (fold >= low) & (fold <= high)
                kept.append(tuple(jnp.where(keep, v, 0.0) for v in ys[k2]))
            ys = fft5(kept, 1.0)
            for n2 in range(5):
                a_re[n2 * 16 + k1] = ys[n2][0]
                a_im[n2 * 16 + k1] = ys[n2][1]
        for n2 in range(5):
            spots = [(5 * n1 + 16 * n2) % ROWS for n1 in range(16)]
            ys = fft_list([(a_re[n2 * 16 + k1], a_im[n2 * 16 + k1]) for k1 in range(16)], 1.0)
            for n1 in range(16):
                u_re[spots[n1], rows, :] = ys[n1][0]
                u_im[spots[n1], rows, :] = ys[n1][1]
        return carry

    lax.fori_loop(0, 9, fan_body, 0)

    def out_body(step, carry):
        highs, lows = [], []
        for n in range(STEP):
            r = step * STEP + n
            re, im = u_re[r], u_im[r]
            re = jnp.concatenate([re[:8] + re[64:], re[8:64]], axis=0)
            im = jnp.concatenate([im[:8] + im[64:], im[8:64]], axis=0)
            c = tc_ref[pl.ds(r, 1), :]
            s = ts_ref[pl.ds(r, 1), :]
            high, low = parted(jnp.concatenate([re * c - im * s, im * c + re * s], axis=1))
            highs.append(high)
            lows.append(low)
        high = jnp.concatenate(highs, axis=0)
        low = jnp.concatenate(lows, axis=0)
        res = (dot(high, v_ref[0]) + dot(low, v_ref[0]) + dot(high, v_ref[1])) * (1.0 / NC)
        for n in range(STEP):
            block = res[n * 64 : (n + 1) * 64]
            both = jnp.concatenate([block[:, :128], block[:, 128:]], axis=0)
            flat[pl.ds(step * STEP + n, 128, stride=ROWS), :] = both.T
        return carry

    lax.fori_loop(0, ROWS // STEP, out_body, 0)

    def store_body(p, carry):
        out_ref[p] = flat[pl.ds(pl.multiple_of(p * ROWS, 8), ROWS), :].astype(BF)
        return carry

    lax.fori_loop(0, 128, store_body, 0, unroll=16)


def slide_tables():
    row = np.arange(256)[:, None]
    col = np.arange(128)[None, :]
    change = (row == col + 125) * 1.0 - (row == col + 123) * 1.0
    shift = (row == col + 124) * 1.0
    nine = ((row >= col) & (row <= col + 8)) * 1.0
    nine = np.concatenate([nine[:128], nine[128:]], axis=1)
    return np.concatenate([change, shift], axis=1), np.concatenate([nine, nine], axis=0)


BAND = 128
PER = 9


def tensor_kernel(half, *refs):
    if half == 0:
        near_ref, lanes_ref, nine_ref, out_ref = refs[:4]
        slope, level, prod, trio, both_ref = refs[4:]
    else:
        near_ref, above_ref, below_ref, far_ref, lanes_ref, nine_ref, _, out_ref = refs[:8]
        slope, level, prod, trio, both_ref = refs[8:]
    lane = lax.broadcasted_iota(jnp.int32, (8, 128), 1)
    sub = lax.broadcasted_iota(jnp.int32, (8, 128), 0)
    step = pl.program_id(0)
    chan, part = lax.axis_index("chan"), lax.axis_index("tm")

    def column(t):
        if t in (-1, 16) or (half == 0 and t == 8):
            parts = []
            skip = 5 if t == 8 else 0
            for j in range(8):
                side = near_ref[j, pl.ds(SIDE, 16), :].astype(F32)
                for n in range(5):
                    parts.append(pltpu.roll(side, (-16 * n - skip) % 128, 1).astype(BF))
            if half == 1:
                first = pltpu.roll(above_ref[pl.ds(128, 16), :].astype(F32), 64, 1).astype(BF)
                parts = [first] + parts + [below_ref[pl.ds(128, 16), :]]
            return jnp.concatenate(parts, axis=0)
        rows = pl.ds(16 * t if t < 8 else 144 + 16 * (t - 8), 16)
        if t < 8:
            inner = [near_ref[j, pl.ds(t * ROWS, ROWS), :] for j in range(8)]
        else:
            inner = [far_ref[:, (t - 8) * 128 : (t - 7) * 128]]
        if half == 1:
            inner = [above_ref[rows, :]] + inner + [below_ref[rows, :]]
        return jnp.concatenate(inner, axis=0)

    @pl.when(step == 0)
    def _():
        left = column(8 * half - 1)
        for t in range(PER):
            right = column(8 * half + t)
            res = dot(jnp.concatenate([left, right], axis=1), lanes_ref[...])
            rows = pl.ds(16 - 16 * half, 640 + 32 * half)
            slope[t, rows, :] = res[:, :128]
            level[t, rows, :] = res[:, 128:]
            left = right

    top = pl.multiple_of(step * BAND, BAND)
    for k in range(BAND // 8 + 2):
        base = pl.multiple_of(top + k * 8, 8)
        for t in range(PER):
            grad_time = slope[t, pl.ds(base + 12, 8), :]
            masked = grad_time
            if half == 0 and t == 0:
                masked = jnp.where((lane >= 4) | (part > 0), masked, 0.0)
            if half == 1 and t == PER - 1:
                masked = jnp.where((lane < 4) | (part < 7), masked, 0.0)
            if half == 1 and k == 0:
                masked = jnp.where((sub >= 4) | (chan > 0) | (step > 0), masked, 0.0)
            if half == 1 and k == BAND // 8:
                masked = jnp.where((sub < 4) | (chan < 15) | (step < 640 // BAND - 1), masked, 0.0)
            grad_chan = level[t, pl.ds(base + 13, 8), :] - level[t, pl.ds(base + 11, 8), :]
            prod[0, t, pl.ds(k * 8, 8), :] = grad_chan * masked
            prod[1, t, pl.ds(k * 8, 8), :] = grad_time * masked
    for k in range(BAND // 8 + 1):
        for n in range(2):
            for t in range(PER):
                trio[n, t, pl.ds(k * 8, 8), :] = (
                    prod[n, t, pl.ds(k * 8, 8), :]
                    + prod[n, t, pl.ds(k * 8 + 1, 8), :]
                    + prod[n, t, pl.ds(k * 8 + 2, 8), :]
                )
    for k in range(BAND // 16):
        for n in range(2):
            for t in range(PER):
                total = (
                    trio[n, t, pl.ds(k * 16, 16), :]
                    + trio[n, t, pl.ds(k * 16 + 3, 16), :]
                    + trio[n, t, pl.ds(k * 16 + 6, 16), :]
                )
                high, low = parted(total)
                both_ref[n, t, pl.ds(k * 16, 16), :128] = high
                both_ref[n, t, pl.ds(k * 16, 16), 128:] = low
    nine = nine_ref[...]
    scale = 1.0 / 324.0
    for g in range(2):
        sums = []
        for n in range(2):
            res = dot(both_ref[n, pl.ds(g * 4, 5)].reshape(5 * BAND, 256), nine)
            sums.append(res[: 4 * BAND, :128] + res[BAND:, 128:])
        res = (sums[0] * -scale) / (sums[1] * scale + 1e-05)
        for t in range(4):
            cols = slice(g * 512 + t * 128, g * 512 + t * 128 + 128)
            out_ref[:, cols] = res[t * BAND : (t + 1) * BAND]


def ahead(parts, count, lane):
    turned = [pltpu.roll(v, (-count) % 128, 1) for v in parts]
    out = []
    for t in range(len(parts)):
        if count > 0:
            other = turned[min(t + 1, len(parts) - 1)]
            out.append(jnp.where(lane < 128 - count, turned[t], other))
        else:
            other = turned[max(t - 1, 0)]
            out.append(jnp.where(lane < -count, other, turned[t]))
    return out


def edge_kernel(above_ref, top_ref, bottom_ref, below_ref, _, out_ref, wide, prod):
    lane = lax.broadcasted_iota(jnp.int32, (8, 128), 1)
    sub = lax.broadcasted_iota(jnp.int32, (8, 128), 0)
    step = pl.program_id(0)
    chan, part = lax.axis_index("chan"), lax.axis_index("tm")

    def spread(start, ref, turned):
        rows = pl.ds(start, 16)
        side = ref[pl.ds(128, 16), :].astype(F32)
        wide[0, rows, :] = pltpu.roll(side, turned, 1)
        wide[9, rows, :] = pltpu.roll(side, (turned - 5) % 128, 1)
        for t in range(8):
            wide[t + 1, rows, :] = ref[pl.ds(16 * t, 16), :].astype(F32)

    @pl.when(step == 0)
    def _():
        spread(0, above_ref, 64)
        spread(16, top_ref, 0)

    @pl.when(step == 1)
    def _():
        spread(0, bottom_ref, 64)
        spread(16, below_ref, 0)

    skip = pl.multiple_of(8 - step * 8, 8)
    for k in range(2):
        first = skip + k * 8 + 4
        row = sub + first
        keep = ((row >= 16) | (step == 1) | (chan > 0)) & ((row < 16) | (step == 0) | (chan < 15))
        here = [wide[t, pl.ds(first, 8), :] for t in range(10)]
        right, left = ahead(here, 1, lane), ahead(here, -1, lane)
        for t in range(10):
            grad_time = right[t] - left[t]
            masked = jnp.where(keep, grad_time, 0.0)
            if t == 0:
                masked = jnp.where(part > 0, masked, 0.0)
            grad_chan = wide[t, pl.ds(first + 1, 8), :] - wide[t, pl.ds(first - 1, 8), :]
            prod[0, t, pl.ds(k * 8, 8), :] = grad_chan * masked
            prod[1, t, pl.ds(k * 8, 8), :] = grad_time * masked
    sums = []
    for n in range(2):
        parts = []
        for t in range(10):
            total = prod[n, t, pl.ds(0, 8), :]
            for d in range(1, 9):
                total = total + prod[n, t, pl.ds(d, 8), :]
            parts.append(total)
        near, far = ahead(parts, 1, lane), ahead(parts, -1, lane)
        three = [v + a + b for v, a, b in zip(parts, near, far)]
        near, far = ahead(three, 3, lane), ahead(three, -3, lane)
        sums.append([v + a + b for v, a, b in zip(three, near, far)][1:9])
    scale = 1.0 / 324.0
    out = [(c * -scale) / (a * scale + 1e-05) for c, a in zip(*sums)]
    out_ref[...] = jnp.concatenate(out, axis=1)


def call(kernel, out, specs, scratch, flops, *args):
    nbytes = sum(a.size * a.dtype.itemsize for a in args) + 3 * 2**20
    return pl.pallas_call(
        kernel,
        out_shape=out,
        in_specs=[VMEM] * len(args),
        out_specs=specs,
        scratch_shapes=scratch,
        compiler_params=pltpu.CompilerParams(vmem_limit_bytes=48 * 2**20),
        cost_estimate=pl.CostEstimate(flops=flops, bytes_accessed=nbytes, transcendentals=0),
    )(*args)


def pair(matrix):
    return jnp.asarray(np.stack(two_parts(matrix)))


def single(table):
    return jnp.asarray(table.astype(np.float32))


def forward(series, good, low, high, packed):
    fwd, _, first, _, tc, ts = time_tables()
    scratch = [
        pltpu.VMEM((16, 8, 16, 128), F32),
        pltpu.VMEM((64 * ROWS, 256), BF),
        pltpu.VMEM((64 * ROWS, 256), BF),
    ]
    out = jax.ShapeDtypeStruct((128, ROWS, 128), BF)
    tables = single(tc), single(ts), pair(fwd), pair(first)
    return call(
        forward_kernel,
        out,
        VMEM,
        scratch,
        4 * 10**9,
        series,
        good,
        low,
        high,
        packed,
        *tables,
    )


def backward(spectra):
    _, bwd, _, last, tc, ts = time_tables()
    scratch = [pltpu.VMEM((16, 8, 16, 128), F32), pltpu.VMEM((64 * ROWS, 256), F32)]
    out = [jax.ShapeDtypeStruct(s, BF) for s in ((8, NEAR, 128), (8, ROWS, FAR))]
    tables = single(tc), single(ts), pair(bwd), pair(last)
    return call(
        backward_kernel, out, [VMEM, VMEM], scratch, 4 * 10**9, spectra, *tables
    )


def channels(pencil, low, high, packed):
    fwd, bwd, tc, ts = chan_tables()
    scratch = [
        pltpu.VMEM((128 * ROWS, 128), F32),
        pltpu.VMEM((ROWS, 72, 128), F32),
        pltpu.VMEM((ROWS, 72, 128), F32),
        pltpu.VMEM((ROWS, 8, 128), F32),
        pltpu.VMEM((ROWS, 8, 128), F32),
    ]
    out = jax.ShapeDtypeStruct((128, ROWS, 128), BF)
    tables = single(tc), single(ts), pair(fwd), pair(bwd)
    return call(channel_kernel, out, VMEM, scratch, 8 * 10**9, pencil, low, high, packed, *tables)


def tensor(half, near, above=None, below=None, far=None, whole=None):
    lanes, nine = (jnp.asarray(t.astype(ml_dtypes.bfloat16)) for t in slide_tables())
    scratch = [
        pltpu.VMEM((PER, 672, 128), F32),
        pltpu.VMEM((PER, 672, 128), F32),
        pltpu.VMEM((2, PER, BAND + 16, 128), F32),
        pltpu.VMEM((2, PER, BAND + 16, 128), F32),
        pltpu.VMEM((2, PER, BAND, 256), BF),
    ]
    if half == 0:
        args = (near, lanes, nine)
        specs, alias = [VMEM] * 3, {}
    else:
        args = (near, above, below, far, lanes, nine, whole)
        specs, alias = [VMEM] * 6 + [ANY], {6: 0}
    return pl.pallas_call(
        functools.partial(tensor_kernel, half),
        grid=(640 // BAND,),
        out_shape=jax.ShapeDtypeStruct((640, 2048), F32),
        in_specs=specs,
        out_specs=pl.BlockSpec((BAND, 1024), lambda g: (g, half)),
        scratch_shapes=scratch,
        input_output_aliases=alias,
        compiler_params=pltpu.CompilerParams(vmem_limit_bytes=40 * 2**20),
        cost_estimate=pl.CostEstimate(flops=10**9, bytes_accessed=9 * 2**20, transcendentals=0),
    )(*args)


def edges(above, top, bottom, below, whole):
    return pl.pallas_call(
        edge_kernel,
        grid=(2,),
        out_shape=jax.ShapeDtypeStruct((640, 2048), F32),
        in_specs=[VMEM] * 4 + [ANY],
        out_specs=pl.BlockSpec((8, 1024), lambda g: (79 * g, 0)),
        scratch_shapes=[pltpu.VMEM((10, 32, 128), F32), pltpu.VMEM((2, 10, 16, 128), F32)],
        input_output_aliases={4: 0},
        compiler_params=pltpu.CompilerParams(vmem_limit_bytes=16 * 2**20),
        cost_estimate=pl.CostEstimate(flops=10**7, bytes_accessed=2**19, transcendentals=0),
    )(above, top, bottom, below, whole)


def window_bounds(fan_bounds, block):
    column = []
    for slot, k in enumerate(WAVES):
        column += [0, 64] if slot == 0 else [k, 128 - k]
    pick = jnp.asarray(np.array(column, np.int32))[block]
    table = fan_bounds[:, : NT // 2].reshape(2, 64, 128)
    mine = lax.dynamic_slice(table, (0, 0, pick), (2, 64, 1))
    top = jnp.broadcast_to(fan_bounds[:, NT // 2].reshape(2, 1, 1), (2, 8, 1))
    both = jnp.broadcast_to(jnp.concatenate([mine, top], axis=1), (2, 72, 128))
    return both[0], both[1]


def after_kernel(value_ref, sign_ref, out_ref):
    pass


def after(value, sign):
    return pl.pallas_call(
        after_kernel,
        out_shape=jax.ShapeDtypeStruct(value.shape, value.dtype),
        in_specs=[ANY, ANY],
        out_specs=ANY,
        input_output_aliases={0: 0},
        cost_estimate=pl.CostEstimate(flops=0, bytes_accessed=0, transcendentals=0),
    )(value, sign)


def outer_kernel(near_ref, top_ref, bottom_ref):
    for ref, source, first in ((top_ref, 0, 0), (bottom_ref, 7, 64)):
        for t in range(8):
            ref[pl.ds(16 * t, 16), :] = near_ref[source, pl.ds(t * ROWS + first, 16), :]
        ref[pl.ds(128, 144), :] = near_ref[source, pl.ds(SIDE, 144), :]


def per_device(record, channel_ok, fan_bounds):
    chan, part = lax.axis_index("chan"), lax.axis_index("tm")
    block = chan * 8 + part
    series = lax.all_to_all(record.reshape(8, ROWS, 2048), "tm", 0, 0, tiled=True)
    good = lax.dynamic_slice(channel_ok, (part * ROWS,), (ROWS,)).astype(F32)
    good = jnp.broadcast_to(good[:, None], (ROWS, 128))
    low, high = window_bounds(fan_bounds, block)
    corner = lax.broadcasted_iota(jnp.int32, (8, 128), 0) == 0
    packed = (corner & (block == 0)).astype(F32)
    spectra = forward(series, good, low, high, packed)
    pencil = lax.all_to_all(spectra, ("chan", "tm"), 0, 0, tiled=True)
    passed = channels(pencil, low, high, packed)
    back = lax.all_to_all(passed, ("chan", "tm"), 0, 0, tiled=True)
    near, far = backward(back)
    near = lax.all_to_all(near, "tm", 0, 0, tiled=True)
    down = [(i, i + 1) for i in range(15)]
    outer = jax.ShapeDtypeStruct((272, 128), BF)
    top, bottom = call(outer_kernel, [outer, outer], [VMEM, VMEM], [], 10**6, near)
    above = lax.ppermute(bottom, "chan", down)
    below = lax.ppermute(top, "chan", [(b, a) for a, b in down])
    whole = edges(above, top, bottom, below, tensor(0, near))
    far = lax.all_to_all(after(far, near), "tm", 0, 0, tiled=True).reshape(640, FAR)
    return tensor(1, near, above, below, far, whole)


def solution(mesh):
    in_specs = (P("chan", "tm"), P("chan"), P())
    out_specs = P("chan", "tm")
    return jax.shard_map(
        per_device, mesh=mesh, in_specs=in_specs, out_specs=out_specs, check_vma=False
    )
```
